32 devices in a mesh: beams: 2 (over y), freq: 4 (over z), tm: 2 (over x), sub: 2 (over core).
Axes of the slice: x: 2, y: 2, z: 4, core: 2. Of those that a mesh axis runs over, the one named last changes fastest.
Arguments:
- filterbank: bfloat16 [1024, 4096], P(('beams', 'freq', 'sub'), 'tm'), parts along dimension 0, may hold values from -8 to 8
- delay_shifts: int32 [9, 512], replicated, may hold values from 0 to 256, as said below
- pulse_filters: bfloat16 [6, 256], replicated, may hold values from -0.375 to 0.375
Outputs:
- dedispersed: float32 [1024, 4096], P(('beams', 'freq', 'sub'), 'tm'), parts along dimension 0
The draws below stay inside these ranges and needn't reach their ends.
There are 2 independent parts, one for each index of `beams`. The reference program is written for one: setup_inputs(seed, part) draws one part's arguments, and reference() takes and returns one part's arrays. A program takes and returns all parts, laid end to end along the dimension named above; an argument that names none is the same for every part. Nothing has to cross between parts.
Inputs may be any that keep to these rules, and one draw needn't show every extreme that they name: `delay_shifts`: at level l every shift lies in 0 to 2^l; trial 0 of every subband has shift 0 and its last trial shift 2^l.
All inputs are finite; a program needn't handle non-finite values.
Results may differ from the reference program's by a relative error of at most 0.0035.
Values may be sent and summed in bfloat16 or wider, within the bound.
No kernel may reach another device: no remote copies, remote signals or barrier semaphores. Data moves between devices by JAX's collectives and lax.ppermute only.
A program may use at most 64 MiB of HBM per device.

```python
import math
import jax
import jax.numpy as jnp
import numpy as np
from jax import lax

CH_DEV = 64
GROUPS = 8
C = 512
LEVELS = 9
TW = 4096
TAPS = 256
NW = 6


def draw_filterbank(key, part):
    noise = jnp.clip(jax.random.normal(key, (C, TW), jnp.float32), -6.0, 6.0)
    return noise.astype(jnp.bfloat16)


def draw_delay_shifts(key, part):
    positions = jnp.arange(C, dtype=jnp.int32)
    stacked = []
    for level_num in range(LEVELS):
        width_now = 2 ** level_num
        band_width = 2 * width_now
        trial_num = positions % band_width
        base_shift = trial_num * width_now // (band_width - 1)
        jitter = jax.random.randint(jax.random.fold_in(key, 101 + level_num), (C,), -2, 3)
        shifted = jnp.clip(base_shift + jitter, 0, width_now)
        shifted = jnp.where(trial_num == 0, 0, jnp.where(trial_num == band_width - 1, width_now, shifted))
        stacked.append(shifted)
    return jnp.stack(stacked).astype(jnp.int32)


def scatter_about(rng, shape, deviation, most, kind=jnp.bfloat16):
    return jnp.clip(deviation * jax.random.normal(rng, shape, jnp.float32), -most, most).astype(kind)


def setup_inputs(seed: int = 0, part: int = 0) -> dict:
    key_of = jax.random.split(jax.random.key(seed), 4)
    own_keys = jax.random.split(jax.random.fold_in(key_of[3], part), 4)
    filterbank = draw_filterbank(jax.random.fold_in(jax.random.fold_in(key_of[3], part), 71), part)
    delay_shifts = draw_delay_shifts(jax.random.fold_in(key_of[3], 71), part)
    pulse_filters = scatter_about(key_of[2], (NW, TAPS), TAPS ** -0.5, 0.375)
    return dict(filterbank=filterbank, delay_shifts=delay_shifts, pulse_filters=pulse_filters)


def delayed_rows(source, amounts, out_len):

    def one_row(row_data, amount):
        return lax.dynamic_slice_in_dim(row_data, amount.astype(jnp.int32), out_len)
    return jax.vmap(one_row)(source, amounts)

def toeplitz_rows(filter_taps):
    tap_count = filter_taps.shape[0]
    extended = jnp.concatenate([filter_taps, jnp.zeros((tap_count + 1,), filter_taps.dtype)])
    tiled = jnp.tile(extended, tap_count)[:2 * tap_count * tap_count]
    return tiled.reshape(tap_count, 2 * tap_count)

def reference(filterbank, delay_shifts, pulse_filters):
    total_rows, window = filterbank.shape
    level_count = delay_shifts.shape[0]
    state = filterbank.astype(jnp.float32)
    for level_num in range(level_count):
        width_now = 2 ** level_num
        grouped = state.reshape(total_rows // (2 * width_now), 2, width_now, window)
        lower_rows = grouped[:, 0].reshape(-1, window)
        upper_rows = grouped[:, 1].reshape(-1, window)
        padded = jnp.concatenate([upper_rows, jnp.zeros((upper_rows.shape[0], width_now), jnp.float32)], axis=1)
        amounts = delay_shifts[level_num].reshape(-1, 2)
        even_rows = lower_rows + delayed_rows(padded, amounts[:, 0], window)
        odd_rows = lower_rows + delayed_rows(padded, amounts[:, 1], window)
        state = jnp.stack([even_rows, odd_rows], axis=1).reshape(total_rows, window)
    normalized = (state * (1.0 / math.sqrt(total_rows))).astype(jnp.bfloat16)
    extended = jnp.concatenate([normalized, jnp.zeros((total_rows, TAPS), jnp.bfloat16)], axis=1)
    block_count = window // TAPS
    windows = extended.reshape(total_rows, block_count + 1, TAPS)
    leading = windows[:, :block_count].reshape(-1, TAPS).astype(jnp.float32)
    trailing = windows[:, 1:].reshape(-1, TAPS).astype(jnp.float32)
    running_max = jnp.full(leading.shape, -1e+30, jnp.float32)
    running_sum = jnp.zeros(leading.shape, jnp.float32)
    for width_num in range(pulse_filters.shape[0]):
        kernel = toeplitz_rows(pulse_filters[width_num]).astype(jnp.float32)
        response = jnp.dot(leading, kernel[:, :TAPS].T, preferred_element_type=jnp.float32)
        response = response + jnp.dot(trailing, kernel[:, TAPS:].T, preferred_element_type=jnp.float32)
        energy = 0.5 * response * response
        new_max = jnp.maximum(running_max, energy)
        running_sum = running_sum * jnp.exp(running_max - new_max) + jnp.exp(energy - new_max)
        running_max = new_max
    natural_map = (jnp.log(running_sum) + running_max).reshape(total_rows, window)
    bit_count = GROUPS.bit_length() - 1
    flips = np.array([sum(((block_num >> bit_num & 1) << bit_count - 1 - bit_num for bit_num in range(bit_count))) for block_num in range(GROUPS)], dtype=np.int32)
    return natural_map.reshape(GROUPS, CH_DEV, window)[flips].reshape(total_rows, window)
```

```python
import functools
import math

import jax
import jax.numpy as jnp
from jax import lax
from jax.experimental import pallas as pl
from jax.experimental.pallas import tpu as pltpu
from jax.sharding import PartitionSpec as P

LANES = 128
SUBLANES = 8
CHANNEL_AXES = ("freq", "sub")
VMEM_LIMIT = 48 * 2**20


def rounded_up(value, unit):
    return -(-value // unit) * unit


def reversed_bits(value, bit_count):
    result = 0
    for bit_num in range(bit_count):
        result = result | (value >> bit_num & 1) << bit_count - 1 - bit_num
    return result


def from_behind(value, axis, steps):
    count = lax.axis_size(axis)
    first, last = (max(0, -steps), min(count, count - steps))
    return lax.ppermute(value, axis, [(source, source + steps) for source in range(first, last)])


def from_partner(block, axes, mask):
    count = lax.axis_size(axes)
    return lax.ppermute(block, axes, [(source, source ^ mask) for source in range(count)])


def delayed(source, start, tiles, amount, most):
    if isinstance(amount, int):
        whole, part = divmod(amount, LANES)
    elif most < LANES:
        whole, part = 0, amount
    else:
        whole, part = amount >> 7, amount & LANES - 1
    first = source[pl.ds(start + whole, tiles), :]
    if isinstance(part, int) and part == 0:
        return first
    second = source[pl.ds(start + whole + 1, tiles), :]
    lane = lax.broadcasted_iota(jnp.int32, first.shape, 1)
    mixed = jnp.where(lane >= part, first, second)
    return pltpu.roll(mixed, LANES - part & LANES - 1, 1)


def merge_level(source, target, shifts, level, subbands, width, base, in_step, out_step, tiles):
    most = 2**level
    for subband in range(subbands):
        place, complete = base(subband)
        for trial in range(width):
            low_row = subband * 2 * width + trial
            lower = source[pl.ds(low_row * in_step, tiles), :]
            for odd in range(2):
                row = 2 * trial + odd
                if complete and row == 0:
                    amount = 0
                elif complete and row == 2 * width - 1:
                    amount = most
                else:
                    amount = shifts[level, place + row]
                upper = delayed(source, (low_row + width) * in_step, tiles, amount, most)
                target[pl.ds((subband * 2 * width + row) * out_step, tiles), :] = lower + upper


def local_kernel(group_count, piece_count, tile_count, shifts, *refs):
    pieces, refs = refs[:piece_count], refs[piece_count:]
    blocks, (ping, pong) = refs[:group_count], refs[group_count:]
    chan_rows = pieces[0].shape[0]
    bit_count = group_count.bit_length() - 1
    local_count = chan_rows.bit_length() - 1
    step = rounded_up(tile_count, SUBLANES)
    position = lax.axis_index(CHANNEL_AXES)
    for first_row in range(0, chan_rows, SUBLANES):
        rows = slice(first_row, first_row + SUBLANES)
        tile = 0
        for piece in pieces:
            for start in range(0, piece.shape[1], LANES):
                part = piece[rows, start : start + LANES].astype(jnp.float32)
                ping[pl.ds(first_row * step + tile, SUBLANES, stride=step), :] = part
                tile += 1
        for later in range(tile, tile_count):
            ping[pl.ds(first_row * step + later, SUBLANES, stride=step), :] = jnp.zeros(
                (SUBLANES, LANES), jnp.float32
            )
    source, target = ping, pong
    for level in range(local_count):
        width = 2**level
        last = level == local_count - 1
        merge_level(
            source,
            target,
            shifts,
            level,
            chan_rows // (2 * width),
            width,
            lambda subband: (position * chan_rows + subband * 2 * width, True),
            step,
            tile_count if last else step,
            step,
        )
        source, target = target, source
    block_rows = chan_rows // group_count
    size = block_rows * tile_count
    own = reversed_bits(position, bit_count)
    for mask, block in enumerate(blocks):
        start = (own ^ reversed_bits(mask, bit_count)) * size
        if size % SUBLANES == 0:
            start = pl.multiple_of(start, SUBLANES)
        block[...] = source[pl.ds(start, size), :].astype(jnp.bfloat16)


def toeplitz(filters, target):
    width_count, tap_count = filters.shape
    lane = lax.broadcasted_iota(jnp.int32, (LANES, LANES), 1)
    row = lax.broadcasted_iota(jnp.int32, (LANES, LANES), 0)
    taps = filters[...].astype(jnp.float32)
    zeros = jnp.zeros((LANES, LANES), jnp.float32)
    for width in range(width_count):
        before = zeros
        for start in range(0, tap_count + LANES, LANES):
            if start < tap_count:
                spread = jnp.broadcast_to(taps[width : width + 1, start : start + LANES], (LANES, LANES))
                rolled = pltpu.roll(spread, 0, 1, stride=1, stride_axis=0)
            else:
                rolled = zeros
            part = jnp.where(lane >= row, rolled, before)
            target[width * LANES : (width + 1) * LANES, start : start + LANES] = part.astype(jnp.bfloat16)
            before = rolled


def trial_kernel(group_count, tile_count, shifts, filters, *refs):
    blocks, (out, ping, pong, taps, linear) = refs[:group_count], refs[group_count:]
    chan_rows, time_len = out.shape
    level_count = shifts.shape[0]
    width_count, tap_count = filters.shape
    bit_count = group_count.bit_length() - 1
    local_count = level_count - bit_count
    block_rows = chan_rows // group_count
    size = block_rows * tile_count
    position = lax.axis_index(CHANNEL_AXES)
    own = reversed_bits(position, bit_count)
    toeplitz(filters, taps)
    for mask, block in enumerate(blocks):
        start = (position ^ mask) * size
        if size % SUBLANES == 0:
            start = pl.multiple_of(start, SUBLANES)
        ping[pl.ds(start, size), :] = block[...].astype(jnp.float32)
    step = rounded_up(tile_count, SUBLANES)
    source, target = ping, pong
    in_step = tile_count
    for section in range(bit_count):
        level = local_count + section
        width = block_rows * 2**section
        needed = time_len + tap_count + 2**level_count - 2 ** (level + 1)
        merge_level(
            source,
            target,
            shifts,
            level,
            group_count >> section + 1,
            width,
            lambda subband: (subband * 2 ** (level + 1) + own * 2 * width, False),
            in_step,
            step,
            rounded_up(-(-needed // LANES), SUBLANES),
        )
        source, target = target, source
        in_step = step
    scale = 1.0 / math.sqrt(shifts.shape[1])
    out_tiles = time_len // LANES
    for first_row in range(0, chan_rows, SUBLANES):
        columns = []
        for offset in range(tap_count // LANES + 1):
            picked = [
                source[pl.ds((first_row + row) * in_step + offset, out_tiles), :] for row in range(SUBLANES)
            ]
            columns.append((jnp.concatenate(picked, axis=0) * scale).astype(jnp.bfloat16))
        windows = jnp.concatenate(columns, axis=1)
        response = lax.dot_general(
            windows, taps[...], (((1,), (1,)), ((), ())), preferred_element_type=jnp.float32
        )
        energies = []
        for width in range(width_count):
            one = response[:, width * LANES : (width + 1) * LANES]
            energies.append(0.5 * one * one)
        highest = functools.reduce(jnp.maximum, energies)
        total = functools.reduce(jnp.add, [jnp.exp(energy - highest) for energy in energies])
        linear[first_row * out_tiles : (first_row + SUBLANES) * out_tiles, :] = jnp.log(total) + highest
        for tile in range(out_tiles):
            out[first_row : first_row + SUBLANES, tile * LANES : (tile + 1) * LANES] = linear[
                pl.ds(first_row * out_tiles + tile, SUBLANES, stride=out_tiles), :
            ]


def local(filterbank, delay_shifts, pulse_filters):
    chan_rows, time_len = filterbank.shape
    group_count = lax.axis_size(CHANNEL_AXES)
    level_count = delay_shifts.shape[0]
    width_count, tap_count = pulse_filters.shape
    margin_len = rounded_up(2**level_count - 1 + tap_count, LANES)
    hop_count = min(lax.axis_size("tm") - 1, -(-margin_len // time_len))
    pieces = [filterbank]
    collected = 0
    for hop_num in range(1, hop_count + 1):
        take_len = min(time_len, margin_len - collected)
        pieces.append(from_behind(filterbank[:, :take_len], "tm", -hop_num))
        collected = collected + take_len
    tile_count = (time_len + margin_len) // LANES
    step = rounded_up(tile_count, SUBLANES)
    block_rows = chan_rows // group_count
    spare = rounded_up(2 ** (level_count - 1) // LANES + 1 + SUBLANES, SUBLANES)
    state = pltpu.VMEM((chan_rows * step + spare, LANES), jnp.float32)
    in_vmem = pl.BlockSpec(memory_space=pltpu.VMEM)
    in_smem = pl.BlockSpec(memory_space=pltpu.SMEM)
    params = pltpu.CompilerParams(vmem_limit_bytes=VMEM_LIMIT)
    blocks = pl.pallas_call(
        functools.partial(local_kernel, group_count, len(pieces), tile_count),
        out_shape=[jax.ShapeDtypeStruct((block_rows * tile_count, LANES), jnp.bfloat16)] * group_count,
        in_specs=[in_smem] + [in_vmem] * len(pieces),
        out_specs=[in_vmem] * group_count,
        scratch_shapes=[state, state],
        compiler_params=params,
    )(delay_shifts, *pieces)
    arrived = [blocks[0]] + [
        from_partner(blocks[mask], CHANNEL_AXES, mask) for mask in range(1, group_count)
    ]
    return pl.pallas_call(
        functools.partial(trial_kernel, group_count, tile_count),
        out_shape=jax.ShapeDtypeStruct((chan_rows, time_len), jnp.float32),
        in_specs=[in_smem, in_vmem] + [in_vmem] * group_count,
        out_specs=in_vmem,
        scratch_shapes=[
            state,
            state,
            pltpu.VMEM((width_count * LANES, tap_count + LANES), jnp.bfloat16),
            pltpu.VMEM((chan_rows * time_len // LANES, LANES), jnp.float32),
        ],
        compiler_params=params,
    )(delay_shifts, pulse_filters, *arrived)


def solution(mesh):
    in_specs = (P(("beams", "freq", "sub"), "tm"), P(), P())
    out_specs = P(("beams", "freq", "sub"), "tm")
    return jax.shard_map(local, mesh=mesh, in_specs=in_specs, out_specs=out_specs, check_vma=False)
```

```python
import functools
import math

import jax
import jax.numpy as jnp
from jax import lax
from jax.experimental import pallas as pl
from jax.experimental.pallas import tpu as pltpu
from jax.sharding import PartitionSpec as P

LANES = 128
SUBLANES = 8
CHANNEL_AXES = ("freq", "sub")
VMEM_LIMIT = 48 * 2**20


def rounded_up(value, unit):
    return -(-value // unit) * unit


def reversed_bits(value, bit_count):
    result = 0
    for bit_num in range(bit_count):
        result = result | (value >> bit_num & 1) << bit_count - 1 - bit_num
    return result


def from_behind(value, axis, steps):
    count = lax.axis_size(axis)
    first, last = (max(0, -steps), min(count, count - steps))
    return lax.ppermute(value, axis, [(source, source + steps) for source in range(first, last)])


def delayed(source, start, tiles, amount, most):
    if isinstance(amount, int):
        whole, part = divmod(amount, LANES)
    elif most < LANES:
        whole, part = 0, amount
    else:
        whole, part = amount >> 7, amount & LANES - 1
    first = source[pl.ds(start + whole, tiles), :]
    if isinstance(part, int) and part == 0:
        return first
    second = source[pl.ds(start + whole + 1, tiles), :]
    lane = lax.broadcasted_iota(jnp.int32, first.shape, 1)
    mixed = jnp.where(lane >= part, first, second)
    return pltpu.roll(mixed, LANES - part & LANES - 1, 1)


def merge_level(source, target, shifts, level, subbands, width, base, in_step, out_step, tiles):
    most = 2**level
    for subband in range(subbands):
        place, complete = base(subband)
        for trial in range(width):
            low_row = subband * 2 * width + trial
            lower = source[pl.ds(low_row * in_step, tiles), :]
            for odd in range(2):
                row = 2 * trial + odd
                if complete and row == 0:
                    amount = 0
                elif complete and row == 2 * width - 1:
                    amount = most
                else:
                    amount = shifts[level, place + row]
                upper = delayed(source, (low_row + width) * in_step, tiles, amount, most)
                target[pl.ds((subband * 2 * width + row) * out_step, tiles), :] = lower + upper


def local_kernel(group_count, piece_count, tile_count, shifts, *refs):
    pieces, refs = refs[:piece_count], refs[piece_count:]
    blocks, ping, pong = refs
    chan_rows = pieces[0].shape[0]
    bit_count = group_count.bit_length() - 1
    local_count = chan_rows.bit_length() - 1
    step = rounded_up(tile_count, SUBLANES)
    position = lax.axis_index(CHANNEL_AXES)
    for first_row in range(0, chan_rows, SUBLANES):
        rows = slice(first_row, first_row + SUBLANES)
        tile = 0
        for piece in pieces:
            for start in range(0, piece.shape[1], LANES):
                part = piece[rows, start : start + LANES].astype(jnp.float32)
                ping[pl.ds(first_row * step + tile, SUBLANES, stride=step), :] = part
                tile += 1
        for later in range(tile, tile_count):
            ping[pl.ds(first_row * step + later, SUBLANES, stride=step), :] = jnp.zeros(
                (SUBLANES, LANES), jnp.float32
            )
    source, target = ping, pong
    for level in range(local_count):
        width = 2**level
        last = level == local_count - 1
        merge_level(
            source,
            target,
            shifts,
            level,
            chan_rows // (2 * width),
            width,
            lambda subband: (position * chan_rows + subband * 2 * width, True),
            step,
            tile_count if last else step,
            step,
        )
        source, target = target, source
    block_rows = chan_rows // group_count
    size = block_rows * tile_count
    for group in range(group_count):
        start = reversed_bits(group, bit_count) * size
        blocks[group, :, :] = source[start : start + size, :].astype(jnp.bfloat16)


def toeplitz(filters, target):
    width_count, tap_count = filters.shape
    lane = lax.broadcasted_iota(jnp.int32, (LANES, LANES), 1)
    row = lax.broadcasted_iota(jnp.int32, (LANES, LANES), 0)
    taps = filters[...].astype(jnp.float32)
    zeros = jnp.zeros((LANES, LANES), jnp.float32)
    for width in range(width_count):
        before = zeros
        for start in range(0, tap_count + LANES, LANES):
            if start < tap_count:
                spread = jnp.broadcast_to(taps[width : width + 1, start : start + LANES], (LANES, LANES))
                rolled = pltpu.roll(spread, 0, 1, stride=1, stride_axis=0)
            else:
                rolled = zeros
            part = jnp.where(lane >= row, rolled, before)
            target[width * LANES : (width + 1) * LANES, start : start + LANES] = part.astype(jnp.bfloat16)
            before = rolled


def trial_kernel(group_count, tile_count, shifts, filters, blocks, out, ping, pong, taps, linear):
    chan_rows, time_len = out.shape
    level_count = shifts.shape[0]
    width_count, tap_count = filters.shape
    bit_count = group_count.bit_length() - 1
    local_count = level_count - bit_count
    block_rows = chan_rows // group_count
    size = block_rows * tile_count
    position = lax.axis_index(CHANNEL_AXES)
    own = reversed_bits(position, bit_count)
    toeplitz(filters, taps)
    for group in range(group_count):
        ping[group * size : (group + 1) * size, :] = blocks[group, :, :].astype(jnp.float32)
    step = rounded_up(tile_count, SUBLANES)
    source, target = ping, pong
    in_step = tile_count
    for section in range(bit_count):
        level = local_count + section
        width = block_rows * 2**section
        needed = time_len + tap_count + 2**level_count - 2 ** (level + 1)
        merge_level(
            source,
            target,
            shifts,
            level,
            group_count >> section + 1,
            width,
            lambda subband: (subband * 2 ** (level + 1) + own * 2 * width, False),
            in_step,
            step,
            rounded_up(-(-needed // LANES), SUBLANES),
        )
        source, target = target, source
        in_step = step
    scale = 1.0 / math.sqrt(shifts.shape[1])
    out_tiles = time_len // LANES
    for first_row in range(0, chan_rows, SUBLANES):
        columns = []
        for offset in range(tap_count // LANES + 1):
            picked = [
                source[pl.ds((first_row + row) * in_step + offset, out_tiles), :] for row in range(SUBLANES)
            ]
            columns.append((jnp.concatenate(picked, axis=0) * scale).astype(jnp.bfloat16))
        windows = jnp.concatenate(columns, axis=1)
        response = lax.dot_general(
            windows, taps[...], (((1,), (1,)), ((), ())), preferred_element_type=jnp.float32
        )
        energies = []
        for width in range(width_count):
            one = response[:, width * LANES : (width + 1) * LANES]
            energies.append(0.5 * one * one)
        highest = functools.reduce(jnp.maximum, energies)
        total = functools.reduce(jnp.add, [jnp.exp(energy - highest) for energy in energies])
        linear[first_row * out_tiles : (first_row + SUBLANES) * out_tiles, :] = jnp.log(total) + highest
        for tile in range(out_tiles):
            out[first_row : first_row + SUBLANES, tile * LANES : (tile + 1) * LANES] = linear[
                pl.ds(first_row * out_tiles + tile, SUBLANES, stride=out_tiles), :
            ]


def local(filterbank, delay_shifts, pulse_filters):
    chan_rows, time_len = filterbank.shape
    group_count = lax.axis_size(CHANNEL_AXES)
    level_count = delay_shifts.shape[0]
    width_count, tap_count = pulse_filters.shape
    margin_len = rounded_up(2**level_count - 1 + tap_count, LANES)
    hop_count = min(lax.axis_size("tm") - 1, -(-margin_len // time_len))
    pieces = [filterbank]
    collected = 0
    for hop_num in range(1, hop_count + 1):
        take_len = min(time_len, margin_len - collected)
        pieces.append(from_behind(filterbank[:, :take_len], "tm", -hop_num))
        collected = collected + take_len
    tile_count = (time_len + margin_len) // LANES
    step = rounded_up(tile_count, SUBLANES)
    block_rows = chan_rows // group_count
    spare = rounded_up(2 ** (level_count - 1) // LANES + 1 + SUBLANES, SUBLANES)
    state = pltpu.VMEM((chan_rows * step + spare, LANES), jnp.float32)
    in_vmem = pl.BlockSpec(memory_space=pltpu.VMEM)
    in_smem = pl.BlockSpec(memory_space=pltpu.SMEM)
    params = pltpu.CompilerParams(vmem_limit_bytes=VMEM_LIMIT)
    blocks = pl.pallas_call(
        functools.partial(local_kernel, group_count, len(pieces), tile_count),
        out_shape=jax.ShapeDtypeStruct((group_count, block_rows * tile_count, LANES), jnp.bfloat16),
        in_specs=[in_smem] + [in_vmem] * len(pieces),
        out_specs=in_vmem,
        scratch_shapes=[state, state],
        compiler_params=params,
    )(delay_shifts, *pieces)
    arrived = lax.all_to_all(blocks, CHANNEL_AXES, 0, 0)
    return pl.pallas_call(
        functools.partial(trial_kernel, group_count, tile_count),
        out_shape=jax.ShapeDtypeStruct((chan_rows, time_len), jnp.float32),
        in_specs=[in_smem, in_vmem] + [in_vmem],
        out_specs=in_vmem,
        scratch_shapes=[
            state,
            state,
            pltpu.VMEM((width_count * LANES, tap_count + LANES), jnp.bfloat16),
            pltpu.VMEM((chan_rows * time_len // LANES, LANES), jnp.float32),
        ],
        compiler_params=params,
    )(delay_shifts, pulse_filters, arrived)


def solution(mesh):
    in_specs = (P(("beams", "freq", "sub"), "tm"), P(), P())
    out_specs = P(("beams", "freq", "sub"), "tm")
    return jax.shard_map(local, mesh=mesh, in_specs=in_specs, out_specs=out_specs, check_vma=False)
```

```python
import functools
import math

import jax
import jax.numpy as jnp
from jax import lax
from jax.experimental import pallas as pl
from jax.experimental.pallas import tpu as pltpu
from jax.sharding import PartitionSpec as P

LANES = 128
SUBLANES = 8
PACKED = 16
VMEM_LIMIT = 48 * 2**20


def rounded_up(value, unit):
    return -(-value // unit) * unit


def reversed_bits(value, bit_count):
    result = 0
    for bit_num in range(bit_count):
        result = result | (value >> bit_num & 1) << bit_count - 1 - bit_num
    return result


def bits_of(count):
    return count.bit_length() - 1


def from_ahead(value, steps, crossed):
    count, cores = lax.axis_size("tm"), lax.axis_size("sub")
    route = [
        ((block + steps) * cores + core, block * cores + (core ^ crossed))
        for block in range(count - steps)
        for core in range(cores)
    ]
    return lax.ppermute(value, ("tm", "sub"), route)


def from_partner(value, axis, mask):
    count = lax.axis_size(axis)
    return lax.ppermute(value, axis, [(source, source ^ mask) for source in range(count)])


def delayed(source, start, tiles, amount, most):
    whole, part = (0, amount) if most < LANES else (amount >> bits_of(LANES), amount & LANES - 1)
    first = source[pl.ds(start + whole, tiles), :]
    second = source[pl.ds(start + whole + 1, tiles), :]
    lane = lax.broadcasted_iota(jnp.int32, first.shape, 1)
    mixed = jnp.where(lane >= part, first, second)
    return pltpu.roll(mixed, LANES - part & LANES - 1, 1)


def merge(source, target, low, high, out, tiles, amounts, most):
    lower = source[pl.ds(low, tiles), :]
    for amount, place in zip(amounts, out):
        target[pl.ds(place, tiles), :] = lower + delayed(source, high, tiles, amount, most)


def chip_kernel(spans, tile_count, out_tiles, group_count, shifts, *refs):
    pieces = (refs[: len(spans)], refs[len(spans) : 2 * len(spans)])
    blocks = refs[2 * len(spans) : 2 * len(spans) + group_count]
    ping, pong = refs[2 * len(spans) + group_count :]
    chan_rows = pieces[0][0].shape[0]
    step = rounded_up(tile_count, SUBLANES)
    chip = lax.axis_index("freq")
    core = lax.axis_index("sub")
    for side in range(2):
        for first_row in range(0, chan_rows, PACKED):
            tile = 0
            for piece, (column, length) in zip(pieces[side], spans):
                for start in range(column, column + length, LANES):
                    part = piece[first_row : first_row + PACKED, start : start + LANES].astype(jnp.float32)
                    for half in range(0, PACKED, SUBLANES):
                        row = side * chan_rows + first_row + half
                        ping[pl.ds(row * step + tile, SUBLANES, stride=step), :] = part[half : half + SUBLANES]
                    tile += 1
            for later in range(tile, tile_count):
                for half in range(0, PACKED, SUBLANES):
                    row = side * chan_rows + first_row + half
                    ping[pl.ds(row * step + later, SUBLANES, stride=step), :] = jnp.zeros(
                        (SUBLANES, LANES), jnp.float32
                    )
    source, target = ping, pong
    local_count = bits_of(chan_rows)
    place = chip * 2 * chan_rows
    for level in range(local_count):
        width = 2**level
        for side in range(2):
            for subband in range(chan_rows // (2 * width)):
                band = (side * chan_rows) // (2 * width) + subband
                table = place + (core ^ side) * chan_rows + subband * 2 * width + core * width
                for pair in range(max(width // 2, 1)):
                    rows = range(band * width + 2 * pair, band * width + min(2 * pair + 2, width))
                    held = max(width // 2, 1)
                    merge(
                        source,
                        target,
                        (2 * band * held + pair) * step,
                        ((2 * band + 1) * held + pair) * step,
                        [row * step for row in rows],
                        step,
                        [shifts[level, table + row - band * width] for row in rows],
                        width,
                    )
        source, target = target, source
    half_rows = chan_rows // 2
    low = pl.multiple_of(core * half_rows * step, SUBLANES)
    high = pl.multiple_of((1 - core) * half_rows * step, SUBLANES)
    for pair in range(half_rows):
        rows = (2 * pair, 2 * pair + 1)
        merge(
            source,
            target,
            low + pair * step,
            high + pair * step,
            [row * out_tiles for row in rows],
            step,
            [shifts[local_count, place + core * chan_rows + row] for row in rows],
            chan_rows,
        )
    size = chan_rows // group_count * out_tiles
    own = reversed_bits(chip, bits_of(group_count))
    for mask, block in enumerate(blocks):
        start = (own ^ reversed_bits(mask, bits_of(group_count))) * size
        if size % SUBLANES == 0:
            start = pl.multiple_of(start, SUBLANES)
        block[...] = target[pl.ds(start, size), :].astype(jnp.bfloat16)


def toeplitz(filters, target):
    width_count, tap_count = filters.shape
    lane = lax.broadcasted_iota(jnp.int32, (LANES, LANES), 1)
    row = lax.broadcasted_iota(jnp.int32, (LANES, LANES), 0)
    taps = filters[...].astype(jnp.float32)
    zeros = jnp.zeros((LANES, LANES), jnp.float32)
    for width in range(width_count):
        before = zeros
        for start in range(0, tap_count + LANES, LANES):
            if start < tap_count:
                spread = jnp.broadcast_to(taps[width : width + 1, start : start + LANES], (LANES, LANES))
                rolled = pltpu.roll(spread, 0, 1, stride=1, stride_axis=0)
            else:
                rolled = zeros
            part = jnp.where(lane >= row, rolled, before)
            target[width * LANES : (width + 1) * LANES, start : start + LANES] = part.astype(jnp.bfloat16)
            before = rolled


def trial_kernel(plan, group_count, level_count, *refs):
    shifts, filters, refs = refs[0], refs[1], refs[2:]
    parts = []
    for _ in plan.tile_counts:
        parts.append(refs[:group_count])
        refs = refs[group_count:]
    if plan.taken:
        carried, so_far, refs = refs[0], refs[1], refs[2:]
    out, refs = refs[0], refs[1:]
    if plan.given:
        handed, refs = refs[0], refs[1:]
    *stages, ping, pong, last, taps, linear, result, arrived = refs
    width_count, tap_count = filters.shape
    chan_rows = result.shape[0]
    block_rows = chan_rows // group_count
    first_level = level_count - bits_of(group_count)
    chip = lax.axis_index("freq")
    core = lax.axis_index("sub")
    own = reversed_bits(chip * 2 + core, bits_of(group_count) + 1)
    toeplitz(filters, taps)
    for blocks, stage, tiles in zip(parts, stages, plan.tile_counts):
        size = block_rows * tiles
        for mask, block in enumerate(blocks):
            start = (chip ^ mask) * size
            if size % SUBLANES == 0:
                start = pl.multiple_of(start, SUBLANES)
            stage[pl.ds(start, size), :] = block[...].astype(jnp.float32)
    step = plan.step
    if len(stages) == 1 and plan.first == 0:
        source, target, spare, in_step = stages[0], ping, pong, plan.tile_counts[0]
    else:
        for row in range(chan_rows):
            at = row * step
            for index, (stage, tiles) in enumerate(zip(stages, plan.tile_counts)):
                skip = plan.first if index == 0 else 0
                span = rounded_up(tiles - skip, SUBLANES)
                ping[pl.ds(at, span), :] = stage[pl.ds(row * tiles + skip, span), :]
                at += tiles - skip
        source, target, spare, in_step = ping, pong, ping, step
    head = tap_count // LANES if plan.taken else 0
    for section in range(bits_of(group_count)):
        level = first_level + section
        width = block_rows * 2**section
        is_last = section == bits_of(group_count) - 1
        tiles = plan.lengths[section]
        for subband in range(group_count >> section + 1):
            table = subband * 2 ** (level + 1) + own * 2 * width
            for pair in range(width):
                rows = [subband * 2 * width + 2 * pair + odd for odd in range(2)]
                low = subband * 2 * width + pair
                merge(
                    source,
                    last if is_last else target,
                    low * in_step,
                    (low + width) * in_step,
                    [row * plan.last_step + head if is_last else row * step for row in rows],
                    tiles,
                    [shifts[level, table + 2 * pair + odd] for odd in range(2)],
                    2**level,
                )
                if is_last and plan.taken:
                    for row in rows:
                        last[pl.ds(row * plan.last_step, head), :] = carried[pl.ds(row * head, head), :]
        source, target, spare, in_step = target, spare, target, step
    count = plan.out_tiles
    if plan.given:
        kept = tap_count // LANES
        for row in range(chan_rows):
            handed[pl.ds(row * kept, kept), :] = last[pl.ds(row * plan.last_step + count, kept), :]
    scale = 1.0 / math.sqrt(shifts.shape[1])
    rows_now = SUBLANES * plan.last_step
    for first_row in range(0, chan_rows, SUBLANES):
        columns = [
            (last[pl.ds(first_row * plan.last_step + offset, rows_now), :] * scale).astype(jnp.bfloat16)
            for offset in range(tap_count // LANES + 1)
        ]
        response = lax.dot_general(
            jnp.concatenate(columns, axis=1),
            taps[...],
            (((1,), (1,)), ((), ())),
            preferred_element_type=jnp.float32,
        )
        energies = []
        for width in range(width_count):
            one = response[:, width * LANES : (width + 1) * LANES]
            energies.append(0.5 * one * one)
        highest = functools.reduce(jnp.maximum, energies)
        total = functools.reduce(jnp.add, [jnp.exp(energy - highest) for energy in energies])
        linear[pl.ds(first_row * plan.last_step, rows_now), :] = jnp.log(total) + highest
        for tile in range(count):
            result[first_row : first_row + SUBLANES, tile * LANES : (tile + 1) * LANES] = linear[
                pl.ds(first_row * plan.last_step + tile, SUBLANES, stride=plan.last_step), :
            ]
    place = out.at[:, pl.ds(plan.out_first * LANES, count * LANES)]
    copy = pltpu.make_async_copy(result, place, arrived)
    copy.start()
    copy.wait()


class Plan:
    def __init__(self, tile_counts, out_first, out_tiles, taken, given, levels, tap_tiles):
        self.tile_counts = tile_counts
        self.out_first, self.out_tiles = out_first, out_tiles
        self.taken, self.given = taken, given
        reaches = [-(-(2**level) // LANES) for level in levels]
        made = out_tiles if taken else out_tiles + tap_tiles
        self.first = out_first + tap_tiles if taken else 0
        self.lengths = [rounded_up(made + sum(reaches[at + 1 :]), SUBLANES) for at in range(len(levels))]
        self.step = rounded_up(sum(tile_counts) - self.first, SUBLANES)
        self.last_step = out_tiles + tap_tiles


def local(filterbank, delay_shifts, pulse_filters):
    chan_rows, time_len = filterbank.shape
    group_count = lax.axis_size("freq")
    assert lax.axis_size("sub") == 2
    level_count = delay_shifts.shape[0]
    width_count, tap_count = pulse_filters.shape
    tap_tiles = tap_count // LANES
    time_tiles = time_len // LANES
    far_levels = range(level_count - bits_of(group_count), level_count)
    near_reach = 2 ** far_levels[0] - 1
    margin_len = rounded_up(2**level_count - 1 + tap_count, LANES)
    main_tiles = time_tiles - -(-near_reach // LANES)
    whole_tiles = (time_len + rounded_up(2**level_count - 1 - near_reach + tap_count, LANES)) // LANES
    late_tiles = whole_tiles - main_tiles
    late_len = margin_len + time_len - main_tiles * LANES
    hop_count = min(lax.axis_size("tm") - 1, -(-margin_len // time_len))

    in_vmem = pl.BlockSpec(memory_space=pltpu.VMEM)
    in_smem = pl.BlockSpec(memory_space=pltpu.SMEM)
    in_any = pl.BlockSpec(memory_space=pl.ANY)
    params = pltpu.CompilerParams(vmem_limit_bytes=VMEM_LIMIT)
    block_rows = chan_rows // group_count

    def within_chip(own, other, spans, tile_count, out_tiles):
        step = rounded_up(tile_count, SUBLANES)
        state = pltpu.VMEM((2 * chan_rows * step + 2 * SUBLANES, LANES), jnp.float32)
        return pl.pallas_call(
            functools.partial(chip_kernel, spans, tile_count, out_tiles, group_count),
            out_shape=[jax.ShapeDtypeStruct((block_rows * out_tiles, LANES), jnp.bfloat16)] * group_count,
            in_specs=[in_smem] + [in_vmem] * (2 * len(spans)),
            out_specs=[in_vmem] * group_count,
            scratch_shapes=[state, state],
            compiler_params=params,
        )(delay_shifts, *own, *other)

    def exchanged(blocks):
        order = sorted(range(1, group_count), key=lambda mask: -mask)
        received = {mask: from_partner(blocks[mask], "freq", mask) for mask in order}
        return [blocks[0]] + [received[mask] for mask in range(1, group_count)]

    def between_chips(plan, parts, carried=None, so_far=None):
        spare = 2 ** (level_count - 1) // LANES + 2 * SUBLANES
        state = pltpu.VMEM((chan_rows * plan.step + spare, LANES), jnp.float32)
        stages = [
            pltpu.VMEM((chan_rows * tiles + spare + SUBLANES, LANES), jnp.float32) for tiles in plan.tile_counts
        ]
        operands = [delay_shifts, pulse_filters] + [block for blocks in parts for block in blocks]
        in_specs = [in_smem, in_vmem] + [in_vmem] * (len(operands) - 2)
        aliases = {}
        if plan.taken:
            operands += [carried, so_far]
            in_specs += [in_vmem, in_any]
            aliases = {len(operands) - 1: 0}
        out_shape = [jax.ShapeDtypeStruct((chan_rows, time_len), jnp.float32)]
        out_specs = [in_any]
        if plan.given:
            out_shape.append(jax.ShapeDtypeStruct((chan_rows * tap_tiles, LANES), jnp.float32))
            out_specs.append(in_vmem)
        return pl.pallas_call(
            functools.partial(trial_kernel, plan, group_count, level_count),
            out_shape=out_shape,
            in_specs=in_specs,
            out_specs=out_specs,
            scratch_shapes=stages
            + [
                state,
                state,
                pltpu.VMEM((chan_rows * plan.last_step + 4 * SUBLANES + spare, LANES), jnp.float32),
                pltpu.VMEM((width_count * LANES, tap_count + LANES), jnp.bfloat16),
                pltpu.VMEM((chan_rows * plan.last_step, LANES), jnp.float32),
                pltpu.VMEM((chan_rows, plan.out_tiles * LANES), jnp.float32),
                pltpu.SemaphoreType.DMA,
            ],
            input_output_aliases=aliases,
            compiler_params=params,
        )(*operands)

    other_core = from_partner(filterbank, "sub", 1)
    halos, spans = ([], []), [(main_tiles * LANES, time_len - main_tiles * LANES)]
    collected = 0
    for hop in range(1, hop_count + 1):
        take_len = min(time_len, margin_len - collected)
        ahead = filterbank[:, :take_len]
        for crossed in range(2):
            halos[crossed].append(from_ahead(ahead, hop, crossed))
        spans.append((0, take_len))
        collected += take_len
    main = within_chip([filterbank], [other_core], [(0, time_len)], time_tiles, main_tiles)
    main = exchanged(main)
    late = within_chip(
        [filterbank] + halos[0], [other_core] + halos[1], spans, late_len // LANES, late_tiles
    )
    late = exchanged(late)
    lost = sum(-(-(2**level) // LANES) for level in far_levels) + tap_tiles
    early_tiles = main_tiles - lost
    if early_tiles <= 0:
        plan = Plan([main_tiles, late_tiles], 0, time_tiles, False, False, far_levels, tap_tiles)
        return between_chips(plan, [main, late])[0]
    plan = Plan([main_tiles], 0, early_tiles, False, True, far_levels, tap_tiles)
    out, carried = between_chips(plan, [main])
    plan = Plan(
        [main_tiles, late_tiles], early_tiles, time_tiles - early_tiles, True, False, far_levels, tap_tiles
    )
    return between_chips(plan, [main, late], carried, out)[0]


def solution(mesh):
    in_specs = (P(("beams", "freq", "sub"), "tm"), P(), P())
    out_specs = P(("beams", "freq", "sub"), "tm")
    return jax.shard_map(local, mesh=mesh, in_specs=in_specs, out_specs=out_specs, check_vma=False)
```

```python
import functools
import math

import jax
import jax.numpy as jnp
from jax import lax
from jax.experimental import pallas as pl
from jax.experimental.pallas import tpu as pltpu
from jax.sharding import PartitionSpec as P

LANES = 128
SUBLANES = 8
PACKED = 16
LOG2_E = 1.4426950408889634
VMEM_LIMIT = 48 * 2**20


def rounded_up(value, unit):
    return -(-value // unit) * unit


def reversed_bits(value, bit_count):
    result = 0
    for bit_num in range(bit_count):
        result = result | (value >> bit_num & 1) << bit_count - 1 - bit_num
    return result


def bits_of(count):
    return count.bit_length() - 1


def from_ahead(value, steps, crossed):
    count, cores = lax.axis_size("tm"), lax.axis_size("sub")
    route = [
        ((block + steps) % count * cores + core, block * cores + (core ^ crossed))
        for block in range(count)
        for core in range(cores)
    ]
    return lax.ppermute(value, ("tm", "sub"), route)


def from_partner(value, axis, mask):
    count = lax.axis_size(axis)
    return lax.ppermute(value, axis, [(source, source ^ mask) for source in range(count)])


def lanes():
    return lax.broadcasted_iota(jnp.int32, (SUBLANES, LANES), 1)


def gathered(value, index):
    return jnp.take_along_axis(value, index, axis=1, mode="promise_in_bounds")


def transposed_table(rows, table, columns):
    for index, row in enumerate(rows):
        table[index : index + 1, :] = row.astype(jnp.float32)
    columns[...] = table[...].T


def merge(source, target, low, high, outs, tiles, most):
    lane = lanes()
    apart = max(most // LANES, 1)
    chosen = []
    for amount, place in outs:
        part = amount if most < LANES else amount & LANES - 1
        moved = (lane < part).astype(jnp.int32)
        if most >= LANES:
            moved = moved + (amount >> bits_of(LANES))
        masks = [moved == offset for offset in range(1, apart + 1)]
        chosen.append((masks, lane + part & LANES - 1, place))
    upper = [source[offset, high, :] for offset in range(apart)]
    for tile in range(tiles):
        upper.append(source[tile + apart, high, :])
        lower = source[tile, low, :]
        for masks, index, place in chosen:
            mixed = upper[0]
            for mask, other in zip(masks, upper[1:]):
                mixed = jnp.where(mask, other, mixed)
            target[tile, place, :] = lower + gathered(mixed, index)
        upper = upper[1:]


def tree_levels(state, other, columns, first, levels, held, lengths):
    rows = columns.shape[0] // 2
    source, target = state, other
    done = 0
    while done < len(levels):
        narrow = held < SUBLANES
        bits = min(bits_of(SUBLANES // held), len(levels) - done) if narrow else len(levels) - done
        for turn in range(bits):
            level = levels[done + turn]
            inner = turn + 1 < bits

            def rows_in(vector, start, stride):
                return pl.ds(start, SUBLANES, stride=stride) if turn == 0 else pl.ds(vector * SUBLANES, SUBLANES)

            def rows_out(vector, start, stride):
                return pl.ds(vector * SUBLANES, SUBLANES) if inner else pl.ds(start, SUBLANES, stride=stride)

            def amounts(start, stride):
                column = columns[pl.ds(start, SUBLANES, stride=stride), :]
                one = column[:, first + done + turn : first + done + turn + 1]
                return jnp.broadcast_to(one, (SUBLANES, LANES)).astype(jnp.int32)

            if narrow:
                now = held << turn
                for band in range(SUBLANES // (2 * now)):
                    for trial in range(now):
                        low, high = 2 * band * now + trial, (2 * band + 1) * now + trial
                        outs = [band * 2 * now + 2 * trial + odd for odd in range(2)]
                        merge(
                            source,
                            target,
                            rows_in(low, low, SUBLANES),
                            rows_in(high, high, SUBLANES),
                            [(amounts(out, SUBLANES), rows_out(out, out, SUBLANES)) for out in outs],
                            lengths[done + turn],
                            2**level,
                        )
            else:
                groups, split = held // SUBLANES, 2**turn
                for band in range(rows // (2 * held * split)):
                    for group in range(groups):
                        for place in range(split):
                            low, high = [
                                ((2 * band + upper) * groups + group) * split + place for upper in range(2)
                            ]
                            outs = []
                            for odd in range(2):
                                vector = (band * groups + group) * 2 * split + 2 * place + odd
                                start = (band * groups + group) * SUBLANES * 2 * split + 2 * place + odd
                                outs.append((amounts(start, 2 * split), rows_out(vector, start, 2 * split)))
                            merge(
                                source,
                                target,
                                rows_in(low, low * SUBLANES, 1),
                                rows_in(high, high * SUBLANES, 1),
                                outs,
                                lengths[done + turn],
                                2**level,
                            )
            source, target = target, source
        held <<= bits
        done += bits
    return source


def lengths_of(made, levels):
    return [made + -(-sum(2**later for later in levels if later > level) // LANES) for level in levels]


def chip_kernel(spans, out_tiles, group_count, shifts, *refs):
    pieces = (refs[: len(spans)], refs[len(spans) : 2 * len(spans)])
    blocks = refs[2 * len(spans) : 2 * len(spans) + group_count]
    raw, ping, pong, table, columns = refs[2 * len(spans) + group_count :]
    chan_rows = pieces[0][0].shape[0]
    local_count = bits_of(chan_rows)
    chip, core = lax.axis_index("freq"), lax.axis_index("sub")
    chunk = shifts[0:SUBLANES, pl.ds(pl.multiple_of(chip * LANES, LANES), LANES)]
    lane, level = lanes(), lax.broadcasted_iota(jnp.int32, (SUBLANES, LANES), 0)
    kept = lane & (1 << level) - 1
    picked = gathered(chunk, (2 * (lane - kept) + (core << level) + kept) & LANES - 1)
    transposed_table([picked[at : at + 1, :] for at in range(local_count + 1)], table, columns)
    for side in range(2):
        place = pl.multiple_of((core ^ side) * chan_rows, chan_rows)
        tile = 0
        for piece, (column, length, ahead) in zip(pieces[side], spans):
            there = lax.axis_index("tm") + ahead < lax.axis_size("tm")
            for start in range(column, column + length, LANES):
                part = piece[:, start : start + LANES].astype(jnp.float32)
                if ahead:
                    part = jnp.where(there, part, 0.0)
                raw[tile, pl.ds(place, chan_rows), :] = part
                tile += 1
        for later in range(tile, raw.shape[0] - 1):
            raw[later, pl.ds(place, chan_rows), :] = jnp.zeros((chan_rows, LANES), jnp.float32)
    levels = list(range(local_count + 1))
    lengths = lengths_of(out_tiles, levels)
    for vector in range(SUBLANES):
        column = columns[pl.ds(vector, SUBLANES, stride=SUBLANES), :]
        amount = jnp.broadcast_to(column[:, 0:1], (SUBLANES, LANES)).astype(jnp.int32)
        merge(
            raw,
            ping,
            pl.ds(2 * vector, SUBLANES, stride=2 * SUBLANES),
            pl.ds(2 * vector + 1, SUBLANES, stride=2 * SUBLANES),
            [(amount, pl.ds(vector, SUBLANES, stride=SUBLANES))],
            lengths[0],
            1,
        )
    last = tree_levels(ping, pong, columns, 1, levels[1:], 1, lengths[1:])
    size = chan_rows // group_count
    own = reversed_bits(chip, bits_of(group_count))
    for mask, block in enumerate(blocks):
        start = pl.multiple_of((own ^ reversed_bits(mask, bits_of(group_count))) * size, size)
        for tile in range(out_tiles):
            block[tile, :, :] = last[tile, pl.ds(start, size), :].astype(jnp.bfloat16)


def toeplitz(filters, target):
    width_count, tap_count = filters.shape
    lane = lax.broadcasted_iota(jnp.int32, (LANES, LANES), 1)
    row = lax.broadcasted_iota(jnp.int32, (LANES, LANES), 0)
    taps = filters[...].astype(jnp.float32)
    zeros = jnp.zeros((LANES, LANES), jnp.float32)
    for width in range(width_count):
        before = zeros
        for start in range(0, tap_count + LANES, LANES):
            if start < tap_count:
                spread = jnp.broadcast_to(taps[width : width + 1, start : start + LANES], (LANES, LANES))
                rolled = pltpu.roll(spread, 0, 1, stride=1, stride_axis=0)
            else:
                rolled = zeros
            part = jnp.where(lane >= row, rolled, before)
            target[width * LANES : (width + 1) * LANES, start : start + LANES] = part.astype(jnp.bfloat16)
            before = rolled


def trial_kernel(plan, group_count, level_count, *refs):
    shifts, filters, refs = refs[0], refs[1], refs[2:]
    parts = []
    for _ in plan.tile_counts:
        parts.append(refs[:group_count])
        refs = refs[group_count:]
    if plan.taken:
        carried, taps, so_far, refs = refs[0], refs[1], refs[2], refs[3:]
    out, refs = refs[0], refs[1:]
    if plan.given:
        handed, taps, refs = refs[0], refs[1], refs[2:]
    state, other, table, columns, normal, responses, result, arrived = refs[:8]
    if not plan.given and not plan.taken:
        taps = refs[8]
    width_count, tap_count = filters.shape
    chan_rows = result.shape[0]
    block_rows = chan_rows // group_count
    levels = list(range(level_count - bits_of(group_count), level_count))
    chip, core = lax.axis_index("freq"), lax.axis_index("sub")
    own = reversed_bits(chip * 2 + core, bits_of(group_count) + 1)
    lane = lax.broadcasted_iota(jnp.int32, (1, LANES), 1)
    rows = []
    for section, level in enumerate(levels):
        wide = block_rows * 2 ** (section + 1)
        row = jnp.zeros((1, LANES), jnp.int32)
        for subband in range(chan_rows // wide):
            start = subband * 2 ** (level + 1) + own * wide
            tile = pl.multiple_of(start >> bits_of(LANES) << bits_of(LANES), LANES)
            chunk = shifts[level : level + 1, pl.ds(tile, LANES)]
            moved = pltpu.roll(chunk, subband * wide - (start & LANES - 1) & LANES - 1, 1)
            row = jnp.where(lane >= subband * wide, moved, row)
        rows.append(row)
    transposed_table(rows, table, columns)
    if not plan.taken:
        toeplitz(filters, taps)
    at = 0
    for index, (blocks, tiles) in enumerate(zip(parts, plan.tile_counts)):
        skip = plan.first if index == 0 else 0
        for mask, block in enumerate(blocks):
            start = pl.multiple_of((chip ^ mask) * block_rows, block_rows)
            for tile in range(skip, tiles):
                state[at + tile - skip, pl.ds(start, block_rows), :] = block[tile, :, :].astype(jnp.float32)
        at += tiles - skip
    last = tree_levels(state, other, columns, 0, levels, block_rows, plan.lengths)
    scale = 1.0 / math.sqrt(shifts.shape[1])
    kept = tap_count // LANES
    head = kept if plan.taken else 0
    for tile in range(head):
        normal[tile, :, :] = carried[tile, :, :]
    for tile in range(plan.made):
        normal[head + tile, :, :] = (last[tile, :, :] * scale).astype(jnp.bfloat16)
    count = plan.out_tiles
    if plan.given:
        for tile in range(kept):
            handed[tile, :, :] = normal[count + tile, :, :]
    copies = []
    for turn, (first_tile, some) in enumerate(plan.chunks):
        size = some * chan_rows
        windows = [
            normal[first_tile + offset : first_tile + offset + some, :, :].reshape(size, LANES)
            for offset in range(kept + 1)
        ]
        responses[0:size, :] = lax.dot_general(
            jnp.concatenate(windows, axis=1),
            taps[...],
            (((1,), (1,)), ((), ())),
            preferred_element_type=jnp.float32,
        )
        for first_row in range(0, size, PACKED):
            energies = []
            for width in range(width_count):
                one = responses[first_row : first_row + PACKED, width * LANES : (width + 1) * LANES]
                energies.append((0.5 * LOG2_E) * one * one)
            highest = functools.reduce(jnp.maximum, energies)
            total = functools.reduce(jnp.add, [jnp.exp2(energy - highest) for energy in energies])
            tile, row = first_tile + first_row // chan_rows, first_row % chan_rows
            result[row : row + PACKED, tile * LANES : (tile + 1) * LANES] = (
                jnp.log2(total) + highest
            ) * (1.0 / LOG2_E)
        columns_now = pl.ds(first_tile * LANES, some * LANES)
        place = out.at[:, pl.ds((plan.out_first + first_tile) * LANES, some * LANES)]
        copies.append(pltpu.make_async_copy(result.at[:, columns_now], place, arrived.at[turn]))
        copies[-1].start()
    for copy in copies:
        copy.wait()


class Plan:
    def __init__(self, tile_counts, out_first, out_tiles, taken, given, levels, tap_tiles):
        self.tile_counts = tile_counts
        self.out_first, self.out_tiles = out_first, out_tiles
        self.taken, self.given = taken, given
        self.made = out_tiles if taken else out_tiles + tap_tiles
        self.first = out_first + tap_tiles if taken else 0
        self.lengths = lengths_of(self.made, levels)
        turns = -(-out_tiles // 6)
        ends = [out_tiles * turn // turns for turn in range(turns + 1)]
        self.chunks = [(start, end - start) for start, end in zip(ends, ends[1:])]
        self.state_tiles = sum(tile_counts) - self.first + max(2 ** levels[-1] // LANES, 1) + 1


def local(filterbank, delay_shifts, pulse_filters):
    chan_rows, time_len = filterbank.shape
    group_count = lax.axis_size("freq")
    assert lax.axis_size("sub") == 2 and 2 * chan_rows == LANES
    level_count = delay_shifts.shape[0]
    width_count, tap_count = pulse_filters.shape
    tap_tiles = tap_count // LANES
    time_tiles = time_len // LANES
    far_levels = range(level_count - bits_of(group_count), level_count)
    near_reach = 2 ** far_levels[0] - 1
    margin_len = rounded_up(2**level_count - 1 + tap_count, LANES)
    main_tiles = time_tiles - -(-near_reach // LANES)
    whole_tiles = (time_len + rounded_up(2**level_count - 1 - near_reach + tap_count, LANES)) // LANES
    late_tiles = whole_tiles - main_tiles
    late_len = margin_len + time_len - main_tiles * LANES
    hop_count = min(lax.axis_size("tm") - 1, -(-margin_len // time_len))

    in_vmem = pl.BlockSpec(memory_space=pltpu.VMEM)
    in_any = pl.BlockSpec(memory_space=pl.ANY)
    params = pltpu.CompilerParams(vmem_limit_bytes=VMEM_LIMIT)
    block_rows = chan_rows // group_count
    table = pltpu.VMEM((LANES, LANES), jnp.float32)

    def within_chip(own, other, spans, tile_count, out_tiles):
        state = pltpu.VMEM((tile_count + 1, chan_rows, LANES), jnp.float32)
        block = jax.ShapeDtypeStruct((out_tiles, block_rows, LANES), jnp.bfloat16)
        return pl.pallas_call(
            functools.partial(chip_kernel, spans, out_tiles, group_count),
            out_shape=[block] * group_count,
            in_specs=[in_vmem] * (1 + 2 * len(spans)),
            out_specs=[in_vmem] * group_count,
            scratch_shapes=[
                pltpu.VMEM((tile_count + 1, 2 * chan_rows, LANES), jnp.float32),
                state,
                state,
                table,
                table,
            ],
            compiler_params=params,
        )(delay_shifts, *own, *other)

    def exchanged(blocks):
        order = sorted(range(1, group_count), key=lambda mask: -mask)
        received = {mask: from_partner(blocks[mask], "freq", mask) for mask in order}
        return [blocks[0]] + [received[mask] for mask in range(1, group_count)]

    def between_chips(plan, parts, carried=()):
        state = pltpu.VMEM((plan.state_tiles, chan_rows, LANES), jnp.float32)
        taps = ((width_count * LANES, tap_count + LANES), jnp.bfloat16)
        operands = [delay_shifts, pulse_filters] + [block for blocks in parts for block in blocks]
        operands += carried
        in_specs = [in_vmem] * len(operands)
        aliases = {}
        if plan.taken:
            in_specs[-1] = in_any
            aliases = {len(operands) - 1: 0}
        out_shape = [jax.ShapeDtypeStruct((chan_rows, time_len), jnp.float32)]
        out_specs = [in_any]
        scratch = []
        if plan.given:
            out_shape += [
                jax.ShapeDtypeStruct((tap_tiles, chan_rows, LANES), jnp.bfloat16),
                jax.ShapeDtypeStruct(*taps),
            ]
            out_specs += [in_vmem] * 2
        elif not plan.taken:
            scratch = [pltpu.VMEM(*taps)]
        most = max(some for _, some in plan.chunks)
        return pl.pallas_call(
            functools.partial(trial_kernel, plan, group_count, level_count),
            out_shape=out_shape,
            in_specs=in_specs,
            out_specs=out_specs,
            scratch_shapes=[
                state,
                state,
                table,
                table,
                pltpu.VMEM((plan.out_tiles + tap_tiles, chan_rows, LANES), jnp.bfloat16),
                pltpu.VMEM((most * chan_rows, width_count * LANES), jnp.float32),
                pltpu.VMEM((chan_rows, plan.out_tiles * LANES), jnp.float32),
                pltpu.SemaphoreType.DMA((len(plan.chunks),)),
            ]
            + scratch,
            input_output_aliases=aliases,
            compiler_params=params,
        )(*operands)

    other_core = from_partner(filterbank, "sub", 1)
    halos, spans = ([], []), [(main_tiles * LANES, time_len - main_tiles * LANES, 0)]
    collected = 0
    for hop in range(1, hop_count + 1):
        take_len = min(time_len, margin_len - collected)
        ahead = filterbank[:, :take_len]
        for crossed in range(2):
            halos[crossed].append(from_ahead(ahead, hop, crossed))
        spans.append((0, take_len, hop))
        collected += take_len
    main = within_chip([filterbank], [other_core], [(0, time_len, 0)], time_tiles, main_tiles)
    main = exchanged(main)
    late = within_chip(
        [filterbank] + halos[0], [other_core] + halos[1], spans, late_len // LANES, late_tiles
    )
    late = exchanged(late)
    lost = -(-sum(2**level for level in far_levels) // LANES) + tap_tiles
    early_tiles = main_tiles - lost
    if early_tiles <= 0:
        plan = Plan([main_tiles, late_tiles], 0, time_tiles, False, False, far_levels, tap_tiles)
        return between_chips(plan, [main, late])[0]
    plan = Plan([main_tiles], 0, early_tiles, False, True, far_levels, tap_tiles)
    out, *carried = between_chips(plan, [main])
    plan = Plan(
        [main_tiles, late_tiles], early_tiles, time_tiles - early_tiles, True, False, far_levels, tap_tiles
    )
    return between_chips(plan, [main, late], [*carried, out])[0]


def solution(mesh):
    in_specs = (P(("beams", "freq", "sub"), "tm"), P(), P())
    out_specs = P(("beams", "freq", "sub"), "tm")
    return jax.shard_map(local, mesh=mesh, in_specs=in_specs, out_specs=out_specs, check_vma=False)
```

```python
import functools
import math

import jax
import jax.numpy as jnp
from jax import lax
from jax.experimental import pallas as pl
from jax.experimental.pallas import tpu as pltpu
from jax.sharding import PartitionSpec as P

LANES = 128
SUBLANES = 8
PACKED = 16
LOG2_E = 1.4426950408889634
VMEM_LIMIT = 48 * 2**20


def rounded_up(value, unit):
    return -(-value // unit) * unit


def reversed_bits(value, bit_count):
    result = 0
    for bit_num in range(bit_count):
        result = result | (value >> bit_num & 1) << bit_count - 1 - bit_num
    return result


def bits_of(count):
    return count.bit_length() - 1


def from_ahead(value, steps, crossed):
    count, cores = lax.axis_size("tm"), lax.axis_size("sub")
    route = [
        ((block + steps) % count * cores + core, block * cores + (core ^ crossed))
        for block in range(count)
        for core in range(cores)
    ]
    return lax.ppermute(value, ("tm", "sub"), route)


def from_partner(value, axis, mask):
    count = lax.axis_size(axis)
    return lax.ppermute(value, axis, [(source, source ^ mask) for source in range(count)])


def mask_orders(group_count):
    order = list(range(group_count - 1, 0, -1))
    return order, order[-1:] + order[:-1]


def step_masks(group_count, core):
    orders = mask_orders(group_count)
    return [0] + [jnp.where(core == 0, first, second) for first, second in zip(*orders)]


def exchanged(blocks):
    count = lax.axis_size("freq")
    received = [blocks[0]]
    for block, masks in zip(blocks[1:], zip(*mask_orders(count))):
        route = [
            (chip * 2 + core, (chip ^ masks[core]) * 2 + core) for chip in range(count) for core in range(2)
        ]
        received.append(lax.ppermute(block, ("freq", "sub"), route))
    return received


def lanes():
    return lax.broadcasted_iota(jnp.int32, (SUBLANES, LANES), 1)


def gathered(value, index):
    return jnp.take_along_axis(value, index, axis=1, mode="promise_in_bounds")


def transposed_table(rows, table, columns):
    for index, row in enumerate(rows):
        table[index : index + 1, :] = row.astype(jnp.float32)
    columns[...] = table[...].T


def merge(source, target, low, high, outs, tiles, most):
    lane = lanes()
    apart = max(most // LANES, 1)
    chosen = []
    for amount, place in outs:
        part = amount if most < LANES else amount & LANES - 1
        moved = (lane < part).astype(jnp.int32)
        if most >= LANES:
            moved = moved + (amount >> bits_of(LANES))
        masks = [moved == offset for offset in range(1, apart + 1)]
        chosen.append((masks, lane + part & LANES - 1, place))
    for masks, index, place in chosen:
        upper = [source[offset, high, :] for offset in range(apart)]
        for tile in range(tiles):
            upper.append(source[tile + apart, high, :])
            mixed = upper[0]
            for mask, other in zip(masks, upper[1:]):
                mixed = jnp.where(mask, other, mixed)
            target[tile, place, :] = source[tile, low, :] + gathered(mixed, index)
            upper = upper[1:]


def tree_levels(state, other, columns, first, levels, held, lengths):
    rows = columns.shape[0] // 2
    source, target = state, other
    done = 0
    while done < len(levels):
        narrow = held < SUBLANES
        bits = min(bits_of(SUBLANES // held), len(levels) - done) if narrow else len(levels) - done
        for turn in range(bits):
            level = levels[done + turn]
            inner = turn + 1 < bits

            def rows_in(vector, start, stride):
                return pl.ds(start, SUBLANES, stride=stride) if turn == 0 else pl.ds(vector * SUBLANES, SUBLANES)

            def rows_out(vector, start, stride):
                return pl.ds(vector * SUBLANES, SUBLANES) if inner else pl.ds(start, SUBLANES, stride=stride)

            def amounts(start, stride):
                column = columns[pl.ds(start, SUBLANES, stride=stride), :]
                one = column[:, first + done + turn : first + done + turn + 1]
                return jnp.broadcast_to(one, (SUBLANES, LANES)).astype(jnp.int32)

            if narrow:
                now = held << turn
                for band in range(SUBLANES // (2 * now)):
                    for trial in range(now):
                        low, high = 2 * band * now + trial, (2 * band + 1) * now + trial
                        outs = [band * 2 * now + 2 * trial + odd for odd in range(2)]
                        merge(
                            source,
                            target,
                            rows_in(low, low, SUBLANES),
                            rows_in(high, high, SUBLANES),
                            [(amounts(out, SUBLANES), rows_out(out, out, SUBLANES)) for out in outs],
                            lengths[done + turn],
                            2**level,
                        )
            else:
                groups, split = held // SUBLANES, 2**turn
                for band in range(rows // (2 * held * split)):
                    for group in range(groups):
                        for place in range(split):
                            low, high = [
                                ((2 * band + upper) * groups + group) * split + place for upper in range(2)
                            ]
                            outs = []
                            for odd in range(2):
                                vector = (band * groups + group) * 2 * split + 2 * place + odd
                                start = (band * groups + group) * SUBLANES * 2 * split + 2 * place + odd
                                outs.append((amounts(start, 2 * split), rows_out(vector, start, 2 * split)))
                            merge(
                                source,
                                target,
                                rows_in(low, low * SUBLANES, 1),
                                rows_in(high, high * SUBLANES, 1),
                                outs,
                                lengths[done + turn],
                                2**level,
                            )
            source, target = target, source
        held <<= bits
        done += bits
    return source


def lengths_of(made, levels):
    return [made + -(-sum(2**later for later in levels if later > level) // LANES) for level in levels]


def load_kernel(whole, copied, ahead):
    copied[...] = whole[...]
    ahead[...] = whole[:, : ahead.shape[1]]


def placed(target, blocks, tiles, skip):
    chip, core = lax.axis_index("freq"), lax.axis_index("sub")
    rows = blocks[0].shape[1]
    for mask, block in zip(step_masks(len(blocks), core), blocks):
        start = pl.multiple_of((chip ^ mask) * rows, rows)
        for tile in range(skip, tiles):
            target[tile - skip, pl.ds(start, rows), :] = block[tile, :, :].astype(jnp.float32)


def gather_kernel(*refs):
    *blocks, out, state = refs
    placed(state, blocks, out.shape[0], 0)
    for tile in range(out.shape[0]):
        out[tile, :, :] = state[tile, :, :].astype(jnp.bfloat16)


def chip_kernel(spans, out_tiles, group_count, shifts, *refs):
    pieces = (refs[: len(spans)], refs[len(spans) : 2 * len(spans)])
    blocks = refs[2 * len(spans) : 2 * len(spans) + group_count]
    raw, ping, pong, table, columns = refs[2 * len(spans) + group_count :]
    chan_rows = pieces[0][0].shape[0]
    local_count = bits_of(chan_rows)
    chip, core = lax.axis_index("freq"), lax.axis_index("sub")
    chunk = shifts[0:SUBLANES, pl.ds(pl.multiple_of(chip * LANES, LANES), LANES)]
    lane, level = lanes(), lax.broadcasted_iota(jnp.int32, (SUBLANES, LANES), 0)
    kept = lane & (1 << level) - 1
    picked = gathered(chunk, (2 * (lane - kept) + (core << level) + kept) & LANES - 1)
    transposed_table([picked[at : at + 1, :] for at in range(local_count + 1)], table, columns)
    for side in range(2):
        place = pl.multiple_of((core ^ side) * chan_rows, chan_rows)
        tile = 0
        for piece, (column, length, ahead) in zip(pieces[side], spans):
            there = lax.axis_index("tm") + ahead < lax.axis_size("tm")
            for start in range(column, column + length, LANES):
                part = piece[:, start : start + LANES].astype(jnp.float32)
                if ahead:
                    part = jnp.where(there, part, 0.0)
                raw[tile, pl.ds(place, chan_rows), :] = part
                tile += 1
        for later in range(tile, raw.shape[0] - 1):
            raw[later, pl.ds(place, chan_rows), :] = jnp.zeros((chan_rows, LANES), jnp.float32)
    levels = list(range(local_count + 1))
    lengths = lengths_of(out_tiles, levels)
    mask = lanes() >= core
    for vector in range(SUBLANES):
        low, high = [pl.ds(2 * vector + odd, SUBLANES, stride=2 * SUBLANES) for odd in range(2)]
        upper = raw[0, high, :]
        for tile in range(lengths[0]):
            later = raw[tile + 1, high, :]
            moved = pltpu.roll(jnp.where(mask, upper, later), LANES - core & LANES - 1, 1)
            ping[tile, pl.ds(vector, SUBLANES, stride=SUBLANES), :] = raw[tile, low, :] + moved
            upper = later
    last = tree_levels(ping, pong, columns, 1, levels[1:], 1, lengths[1:])
    size = chan_rows // group_count
    own = reversed_bits(chip, bits_of(group_count))
    for mask, block in zip(step_masks(group_count, core), blocks):
        start = pl.multiple_of((own ^ reversed_bits(mask, bits_of(group_count))) * size, size)
        for tile in range(out_tiles):
            block[tile, :, :] = last[tile, pl.ds(start, size), :].astype(jnp.bfloat16)


def toeplitz(filters, target):
    width_count, tap_count = filters.shape
    lane = lax.broadcasted_iota(jnp.int32, (LANES, LANES), 1)
    row = lax.broadcasted_iota(jnp.int32, (LANES, LANES), 0)
    taps = filters[...].astype(jnp.float32)
    zeros = jnp.zeros((LANES, LANES), jnp.float32)
    for width in range(width_count):
        before = zeros
        for start in range(0, tap_count + LANES, LANES):
            if start < tap_count:
                spread = jnp.broadcast_to(taps[width : width + 1, start : start + LANES], (LANES, LANES))
                rolled = pltpu.roll(spread, 0, 1, stride=1, stride_axis=0)
            else:
                rolled = zeros
            part = jnp.where(lane >= row, rolled, before)
            target[width * LANES : (width + 1) * LANES, start : start + LANES] = part.astype(jnp.bfloat16)
            before = rolled


def trial_kernel(plan, group_count, level_count, *refs):
    shifts, filters, refs = refs[0], refs[1], refs[2:]
    blocks, refs = refs[:group_count], refs[group_count:]
    halos, refs = refs[: len(plan.halos)], refs[len(plan.halos) :]
    if plan.taken:
        carried, taps, so_far, refs = refs[0], refs[1], refs[2], refs[3:]
    out, refs = refs[0], refs[1:]
    if plan.given:
        handed, taps, refs = refs[0], refs[1], refs[2:]
    state, other, table, columns, normal, responses, result, arrived = refs[:8]
    if not plan.given and not plan.taken:
        taps = refs[8]
    width_count, tap_count = filters.shape
    chan_rows = result.shape[0]
    block_rows = chan_rows // group_count
    levels = list(range(level_count - bits_of(group_count), level_count))
    chip, core = lax.axis_index("freq"), lax.axis_index("sub")
    own = reversed_bits(chip * 2 + core, bits_of(group_count) + 1)
    lane = lax.broadcasted_iota(jnp.int32, (1, LANES), 1)
    rows = []
    for section, level in enumerate(levels):
        wide = block_rows * 2 ** (section + 1)
        row = jnp.zeros((1, LANES), jnp.int32)
        for subband in range(chan_rows // wide):
            start = subband * 2 ** (level + 1) + own * wide
            tile = pl.multiple_of(start >> bits_of(LANES) << bits_of(LANES), LANES)
            chunk = shifts[level : level + 1, pl.ds(tile, LANES)]
            moved = pltpu.roll(chunk, subband * wide - (start & LANES - 1) & LANES - 1, 1)
            row = jnp.where(lane >= subband * wide, moved, row)
        rows.append(row)
    transposed_table(rows, table, columns)
    if not plan.taken:
        toeplitz(filters, taps)
    placed(state, blocks, plan.main_tiles, plan.first)
    at = plan.main_tiles - plan.first
    for hop, (halo, tiles) in enumerate(zip(halos, plan.halos), 1):
        there = lax.axis_index("tm") + hop < lax.axis_size("tm")
        for tile in range(tiles):
            state[at, :, :] = jnp.where(there, halo[tile, :, :].astype(jnp.float32), 0.0)
            at += 1
    for tile in range(at, at + plan.empty_tiles):
        state[tile, :, :] = jnp.zeros((chan_rows, LANES), jnp.float32)
    last = tree_levels(state, other, columns, 0, levels, block_rows, plan.lengths)
    scale = 1.0 / math.sqrt(shifts.shape[1])
    kept = tap_count // LANES
    head = kept if plan.taken else 0
    for tile in range(head):
        normal[tile, :, :] = carried[tile, :, :]
    for tile in range(plan.made):
        normal[head + tile, :, :] = (last[tile, :, :] * scale).astype(jnp.bfloat16)
    count = plan.out_tiles
    if plan.given:
        for tile in range(kept):
            handed[tile, :, :] = normal[count + tile, :, :]
    copies = []
    for turn, (first_tile, some) in enumerate(plan.chunks):
        size = some * chan_rows
        windows = [
            normal[first_tile + offset : first_tile + offset + some, :, :].reshape(size, LANES)
            for offset in range(kept + 1)
        ]
        responses[0:size, :] = lax.dot_general(
            jnp.concatenate(windows, axis=1),
            taps[...],
            (((1,), (1,)), ((), ())),
            preferred_element_type=jnp.float32,
        )
        for first_row in range(0, size, PACKED):
            energies = []
            for width in range(width_count):
                one = responses[first_row : first_row + PACKED, width * LANES : (width + 1) * LANES]
                energies.append((0.5 * LOG2_E) * one * one)
            highest = functools.reduce(jnp.maximum, energies)
            total = functools.reduce(jnp.add, [jnp.exp2(energy - highest) for energy in energies])
            tile, row = first_tile + first_row // chan_rows, first_row % chan_rows
            result[row : row + PACKED, tile * LANES : (tile + 1) * LANES] = (
                jnp.log2(total) + highest
            ) * (1.0 / LOG2_E)
        columns_now = pl.ds(first_tile * LANES, some * LANES)
        place = out.at[:, pl.ds((plan.out_first + first_tile) * LANES, some * LANES)]
        copies.append(pltpu.make_async_copy(result.at[:, columns_now], place, arrived.at[turn]))
        copies[-1].start()
    for copy in copies:
        copy.wait()


class Plan:
    def __init__(self, main_tiles, halos, empty_tiles, out_first, out_tiles, taken, given, levels, tap_tiles):
        self.main_tiles, self.halos, self.empty_tiles = main_tiles, halos, empty_tiles
        self.out_first, self.out_tiles = out_first, out_tiles
        self.taken, self.given = taken, given
        self.made = out_tiles if taken else out_tiles + tap_tiles
        self.first = out_first + tap_tiles if taken else 0
        self.lengths = lengths_of(self.made, levels)
        turns = -(-out_tiles // 6)
        ends = [out_tiles * turn // turns for turn in range(turns + 1)]
        self.chunks = [(start, end - start) for start, end in zip(ends, ends[1:])]
        self.state_tiles = main_tiles + sum(halos) + empty_tiles - self.first + max(2 ** levels[-1] // LANES, 1) + 1


def local(filterbank, delay_shifts, pulse_filters):
    chan_rows, time_len = filterbank.shape
    group_count = lax.axis_size("freq")
    assert lax.axis_size("sub") == 2 and 2 * chan_rows == LANES
    level_count = delay_shifts.shape[0]
    width_count, tap_count = pulse_filters.shape
    tap_tiles = tap_count // LANES
    time_tiles = time_len // LANES
    far_levels = range(level_count - bits_of(group_count), level_count)
    near_reach = 2 ** far_levels[0] - 1
    near_len = rounded_up(near_reach, LANES)
    far_tiles = -(-(2**level_count - 1 - near_reach + tap_count) // LANES)

    in_vmem = pl.BlockSpec(memory_space=pltpu.VMEM)
    in_any = pl.BlockSpec(memory_space=pl.ANY)
    params = pltpu.CompilerParams(vmem_limit_bytes=VMEM_LIMIT)
    block_rows = chan_rows // group_count
    table = pltpu.VMEM((LANES, LANES), jnp.float32)

    def within_chip(own, other, spans, tile_count, out_tiles):
        state = pltpu.VMEM((tile_count + 1, chan_rows, LANES), jnp.float32)
        block = jax.ShapeDtypeStruct((out_tiles, block_rows, LANES), jnp.bfloat16)
        return pl.pallas_call(
            functools.partial(chip_kernel, spans, out_tiles, group_count),
            out_shape=[block] * group_count,
            in_specs=[in_vmem] * (1 + 2 * len(spans)),
            out_specs=[in_vmem] * group_count,
            scratch_shapes=[
                pltpu.VMEM((tile_count + 1, 2 * chan_rows, LANES), jnp.float32),
                state,
                state,
                table,
                table,
            ],
            compiler_params=params,
        )(delay_shifts, *own, *other)

    def between_chips(plan, blocks, halos, carried=()):
        state = pltpu.VMEM((plan.state_tiles, chan_rows, LANES), jnp.float32)
        taps = ((width_count * LANES, tap_count + LANES), jnp.bfloat16)
        operands = [delay_shifts, pulse_filters, *blocks, *halos, *carried]
        in_specs = [in_vmem] * len(operands)
        aliases = {}
        if plan.taken:
            in_specs[-1] = in_any
            aliases = {len(operands) - 1: 0}
        out_shape = [jax.ShapeDtypeStruct((chan_rows, time_len), jnp.float32)]
        out_specs = [in_any]
        scratch = []
        if plan.given:
            out_shape += [
                jax.ShapeDtypeStruct((tap_tiles, chan_rows, LANES), jnp.bfloat16),
                jax.ShapeDtypeStruct(*taps),
            ]
            out_specs += [in_vmem] * 2
        elif not plan.taken:
            scratch = [pltpu.VMEM(*taps)]
        most = max(some for _, some in plan.chunks)
        return pl.pallas_call(
            functools.partial(trial_kernel, plan, group_count, level_count),
            out_shape=out_shape,
            in_specs=in_specs,
            out_specs=out_specs,
            scratch_shapes=[
                state,
                state,
                table,
                table,
                pltpu.VMEM((plan.out_tiles + tap_tiles, chan_rows, LANES), jnp.bfloat16),
                pltpu.VMEM((most * chan_rows, width_count * LANES), jnp.float32),
                pltpu.VMEM((chan_rows, plan.out_tiles * LANES), jnp.float32),
                pltpu.SemaphoreType.DMA((len(plan.chunks),)),
            ]
            + scratch,
            input_output_aliases=aliases,
            compiler_params=params,
        )(*operands)

    other_core = from_partner(filterbank, "sub", 1)
    own, ahead = pl.pallas_call(
        load_kernel,
        out_shape=[
            jax.ShapeDtypeStruct(filterbank.shape, filterbank.dtype),
            jax.ShapeDtypeStruct((chan_rows, near_len), filterbank.dtype),
        ],
        in_specs=[in_vmem],
        out_specs=[in_vmem] * 2,
        compiler_params=params,
    )(filterbank)
    both, spans = ([own], [other_core]), [(0, time_len, 0)]
    if lax.axis_size("tm") > 1:
        for crossed in range(2):
            both[crossed].append(from_ahead(ahead, 1, crossed))
        spans.append((0, near_len, 1))
    main = exchanged(within_chip(*both, spans, time_tiles + near_len // LANES, time_tiles))

    halos, takes = [], []
    rest = far_tiles
    if lax.axis_size("tm") > 1:
        first_tiles = min(time_tiles, far_tiles)
        gathered_rows = pl.pallas_call(
            gather_kernel,
            out_shape=jax.ShapeDtypeStruct((first_tiles, chan_rows, LANES), jnp.bfloat16),
            in_specs=[in_vmem] * group_count,
            out_specs=in_vmem,
            scratch_shapes=[pltpu.VMEM((first_tiles, chan_rows, LANES), jnp.float32)],
            compiler_params=params,
        )(*main)
        for hop in range(1, lax.axis_size("tm")):
            if rest > 0:
                takes.append(min(time_tiles, rest))
                halos.append(from_ahead(gathered_rows[: takes[-1]], hop, 0))
                rest -= takes[-1]
    lost = -(-sum(2**level for level in far_levels) // LANES) + tap_tiles
    early_tiles = time_tiles - lost
    if early_tiles <= 0:
        plan = Plan(time_tiles, takes, rest, 0, time_tiles, False, False, far_levels, tap_tiles)
        return between_chips(plan, main, halos)[0]
    plan = Plan(time_tiles, [], 0, 0, early_tiles, False, True, far_levels, tap_tiles)
    out, *carried = between_chips(plan, main, [])
    late_tiles = time_tiles - early_tiles
    plan = Plan(time_tiles, takes, rest, early_tiles, late_tiles, True, False, far_levels, tap_tiles)
    return between_chips(plan, main, halos, [*carried, out])[0]


def solution(mesh):
    in_specs = (P(("beams", "freq", "sub"), "tm"), P(), P())
    out_specs = P(("beams", "freq", "sub"), "tm")
    return jax.shard_map(local, mesh=mesh, in_specs=in_specs, out_specs=out_specs, check_vma=False)
```

```python
import functools
import math

import jax
import jax.numpy as jnp
from jax import lax
from jax.experimental import pallas as pl
from jax.experimental.pallas import tpu as pltpu
from jax.sharding import PartitionSpec as P

LANES = 128
SUBLANES = 8
PACKED = 16
LOG2_E = 1.4426950408889634
VMEM_LIMIT = 48 * 2**20


def rounded_up(value, unit):
    return -(-value // unit) * unit


def reversed_bits(value, bit_count):
    result = 0
    for bit_num in range(bit_count):
        result = result | (value >> bit_num & 1) << bit_count - 1 - bit_num
    return result


def bits_of(count):
    return count.bit_length() - 1


def from_ahead(value, steps, crossed):
    count, cores = lax.axis_size("tm"), lax.axis_size("sub")
    route = [
        ((block + steps) % count * cores + core, block * cores + (core ^ crossed))
        for block in range(count)
        for core in range(cores)
    ]
    return lax.ppermute(value, ("tm", "sub"), route)


def from_partner(value, axis, mask):
    count = lax.axis_size(axis)
    return lax.ppermute(value, axis, [(source, source ^ mask) for source in range(count)])


def mask_orders(group_count):
    order = list(range(group_count - 1, 0, -1))
    return order, order[-1:] + order[:-1]


def step_masks(group_count, core):
    orders = mask_orders(group_count)
    return [0] + [jnp.where(core == 0, first, second) for first, second in zip(*orders)]


def exchanged(blocks):
    count = lax.axis_size("freq")
    received = [blocks[0]]
    for block, masks in zip(blocks[1:], zip(*mask_orders(count))):
        route = [
            (chip * 2 + core, (chip ^ masks[core]) * 2 + core) for chip in range(count) for core in range(2)
        ]
        received.append(lax.ppermute(block, ("freq", "sub"), route))
    return received


def lanes():
    return lax.broadcasted_iota(jnp.int32, (SUBLANES, LANES), 1)


def gathered(value, index):
    return jnp.take_along_axis(value, index, axis=1, mode="promise_in_bounds")


def transposed_table(rows, table, columns):
    for index, row in enumerate(rows):
        table[index : index + 1, :] = row.astype(jnp.float32)
    columns[...] = table[...].T


def merge(source, target, low, high, outs, tiles, most):
    lane = lanes()
    apart = max(most // LANES, 1)
    chosen = []
    for amount, place in outs:
        part = amount if most < LANES else amount & LANES - 1
        moved = (lane < part).astype(jnp.int32)
        if most >= LANES:
            moved = moved + (amount >> bits_of(LANES))
        masks = [moved == offset for offset in range(1, apart + 1)]
        chosen.append((masks, lane + part & LANES - 1, place))
    for masks, index, place in chosen:
        upper = [source[offset, high, :] for offset in range(apart)]
        for tile in range(tiles):
            upper.append(source[tile + apart, high, :])
            mixed = upper[0]
            for mask, other in zip(masks, upper[1:]):
                mixed = jnp.where(mask, other, mixed)
            target[tile, place, :] = source[tile, low, :] + gathered(mixed, index)
            upper = upper[1:]


def tree_levels(state, other, columns, first, levels, held, lengths, packed=False):
    rows = columns.shape[0] // 2
    source, target = state, other
    done = 0
    while done < len(levels):
        narrow = held < SUBLANES
        bits = min(bits_of(SUBLANES // held), len(levels) - done) if narrow else len(levels) - done
        for turn in range(bits):
            level = levels[done + turn]
            inner = turn + 1 < bits
            natural = turn == 0 and not (packed and done == 0)

            def rows_in(vector, start, stride):
                return pl.ds(start, SUBLANES, stride=stride) if natural else pl.ds(vector * SUBLANES, SUBLANES)

            def rows_out(vector, start, stride):
                return pl.ds(vector * SUBLANES, SUBLANES) if inner else pl.ds(start, SUBLANES, stride=stride)

            def amounts(start, stride):
                column = columns[pl.ds(start, SUBLANES, stride=stride), :]
                one = column[:, first + done + turn : first + done + turn + 1]
                return jnp.broadcast_to(one, (SUBLANES, LANES)).astype(jnp.int32)

            if narrow:
                now = held << turn
                for band in range(SUBLANES // (2 * now)):
                    for trial in range(now):
                        low, high = 2 * band * now + trial, (2 * band + 1) * now + trial
                        outs = [band * 2 * now + 2 * trial + odd for odd in range(2)]
                        merge(
                            source,
                            target,
                            rows_in(low, low, SUBLANES),
                            rows_in(high, high, SUBLANES),
                            [(amounts(out, SUBLANES), rows_out(out, out, SUBLANES)) for out in outs],
                            lengths[done + turn],
                            2**level,
                        )
            else:
                groups, split = held // SUBLANES, 2**turn
                for band in range(rows // (2 * held * split)):
                    for group in range(groups):
                        for place in range(split):
                            low, high = [
                                ((2 * band + upper) * groups + group) * split + place for upper in range(2)
                            ]
                            outs = []
                            for odd in range(2):
                                vector = (band * groups + group) * 2 * split + 2 * place + odd
                                start = (band * groups + group) * SUBLANES * 2 * split + 2 * place + odd
                                outs.append((amounts(start, 2 * split), rows_out(vector, start, 2 * split)))
                            merge(
                                source,
                                target,
                                rows_in(low, low * SUBLANES, 1),
                                rows_in(high, high * SUBLANES, 1),
                                outs,
                                lengths[done + turn],
                                2**level,
                            )
            source, target = target, source
        held <<= bits
        done += bits
    return source


def lengths_of(made, levels):
    return [made + -(-sum(2**later for later in levels if later > level) // LANES) for level in levels]


def load_kernel(whole, copied, ahead):
    copied[...] = whole[...]
    ahead[...] = whole[:, : ahead.shape[1]]


def placed(target, blocks, tiles, skip):
    chip, core = lax.axis_index("freq"), lax.axis_index("sub")
    rows = blocks[0].shape[1]
    for mask, block in zip(step_masks(len(blocks), core), blocks):
        start = pl.multiple_of((chip ^ mask) * rows, rows)
        for tile in range(skip, tiles):
            target[tile - skip, pl.ds(start, rows), :] = block[tile, :, :].astype(jnp.float32)


def gather_kernel(*refs):
    *blocks, out, state = refs
    placed(state, blocks, out.shape[0], 0)
    for tile in range(out.shape[0]):
        out[tile, :, :] = state[tile, :, :].astype(jnp.bfloat16)


def chip_kernel(spans, out_tiles, group_count, *refs):
    pieces = (refs[: len(spans)], refs[len(spans) : 2 * len(spans)])
    refs = refs[2 * len(spans) :]
    chan_rows = pieces[0][0].shape[0]
    local_count = bits_of(chan_rows)
    chip, core = lax.axis_index("freq"), lax.axis_index("sub")
    if group_count:
        (earlier, columns), blocks, (raw, ping, pong) = refs[:2], refs[2:-3], refs[-3:]
    else:
        shifts, rows, columns, raw, ping, pong, table = refs
        chunk = shifts[0:SUBLANES, pl.ds(pl.multiple_of(chip * LANES, LANES), LANES)]
        lane, level = lanes(), lax.broadcasted_iota(jnp.int32, (SUBLANES, LANES), 0)
        kept = lane & (1 << level) - 1
        picked = gathered(chunk, (2 * (lane - kept) + (core << level) + kept) & LANES - 1)
        transposed_table([picked[at : at + 1, :] for at in range(local_count + 1)], table, columns)
    for side in range(2):
        place = pl.multiple_of((core ^ side) * chan_rows, chan_rows)
        tile = 0
        for piece, (column, length, ahead) in zip(pieces[side], spans):
            there = lax.axis_index("tm") + ahead < lax.axis_size("tm")
            for start in range(column, column + length, LANES):
                part = piece[:, start : start + LANES].astype(jnp.float32)
                if ahead:
                    part = jnp.where(there, part, 0.0)
                raw[tile, pl.ds(place, chan_rows), :] = part
                tile += 1
        for later in range(tile, raw.shape[0] - 1):
            raw[later, pl.ds(place, chan_rows), :] = jnp.zeros((chan_rows, LANES), jnp.float32)
    levels = list(range(local_count + 1))
    lengths = lengths_of(out_tiles, levels)
    mask = lanes() >= core
    for vector in range(SUBLANES):
        low, high = [pl.ds(2 * vector + odd, SUBLANES, stride=2 * SUBLANES) for odd in range(2)]
        upper = raw[0, high, :]
        for tile in range(lengths[0]):
            later = raw[tile + 1, high, :]
            moved = pltpu.roll(jnp.where(mask, upper, later), LANES - core & LANES - 1, 1)
            ping[tile, pl.ds(vector * SUBLANES, SUBLANES), :] = raw[tile, low, :] + moved
            upper = later
    last = tree_levels(ping, pong, columns, 1, levels[1:], 1, lengths[1:], packed=True)
    if not group_count:
        for tile in range(out_tiles):
            rows[tile, :, :] = last[tile, :, :]
        return
    size = chan_rows // group_count
    own = reversed_bits(chip, bits_of(group_count))
    first = earlier.shape[0]
    for mask, block in zip(step_masks(group_count, core), blocks):
        start = pl.multiple_of((own ^ reversed_bits(mask, bits_of(group_count))) * size, size)
        for tile in range(first):
            block[tile, :, :] = earlier[tile, pl.ds(start, size), :].astype(jnp.bfloat16)
        for tile in range(out_tiles):
            block[first + tile, :, :] = last[tile, pl.ds(start, size), :].astype(jnp.bfloat16)


def toeplitz(filters, target):
    width_count, tap_count = filters.shape
    lane = lax.broadcasted_iota(jnp.int32, (LANES, LANES), 1)
    row = lax.broadcasted_iota(jnp.int32, (LANES, LANES), 0)
    taps = filters[...].astype(jnp.float32)
    zeros = jnp.zeros((LANES, LANES), jnp.float32)
    for width in range(width_count):
        before = zeros
        for start in range(0, tap_count + LANES, LANES):
            if start < tap_count:
                spread = jnp.broadcast_to(taps[width : width + 1, start : start + LANES], (LANES, LANES))
                rolled = pltpu.roll(spread, 0, 1, stride=1, stride_axis=0)
            else:
                rolled = zeros
            part = jnp.where(lane >= row, rolled, before)
            target[width * LANES : (width + 1) * LANES, start : start + LANES] = part.astype(jnp.bfloat16)
            before = rolled


def table_kernel(group_count, block_rows, shifts, filters, columns, taps, table):
    level_count = shifts.shape[0]
    chip, core = lax.axis_index("freq"), lax.axis_index("sub")
    own = reversed_bits(chip * 2 + core, bits_of(group_count) + 1)
    lane = lax.broadcasted_iota(jnp.int32, (1, LANES), 1)
    rows = []
    for section in range(bits_of(group_count)):
        level = level_count - bits_of(group_count) + section
        wide = block_rows * 2 ** (section + 1)
        row = jnp.zeros((1, LANES), jnp.int32)
        for subband in range(block_rows * group_count // wide):
            start = subband * 2 ** (level + 1) + own * wide
            tile = pl.multiple_of(start >> bits_of(LANES) << bits_of(LANES), LANES)
            chunk = shifts[level : level + 1, pl.ds(tile, LANES)]
            moved = pltpu.roll(chunk, subband * wide - (start & LANES - 1) & LANES - 1, 1)
            row = jnp.where(lane >= subband * wide, moved, row)
        rows.append(row)
    transposed_table(rows, table, columns)
    toeplitz(filters, taps)


def trial_kernel(plan, group_count, level_count, scale, columns, taps, *refs):
    blocks, refs = refs[:group_count], refs[group_count:]
    halos, refs = refs[: len(plan.halos)], refs[len(plan.halos) :]
    if plan.taken:
        carried, so_far, refs = refs[0], refs[1], refs[2:]
    out, refs = refs[0], refs[1:]
    if plan.given:
        handed, refs = refs[0], refs[1:]
    state, other, normal, responses, result, arrived = refs
    chan_rows = result.shape[0]
    block_rows = chan_rows // group_count
    width_count, kept = taps.shape[0] // LANES, taps.shape[1] // LANES - 1
    levels = list(range(level_count - bits_of(group_count), level_count))
    placed(state, blocks, plan.main_tiles, plan.first)
    at = plan.main_tiles - plan.first
    for hop, (halo, tiles) in enumerate(zip(halos, plan.halos), 1):
        there = lax.axis_index("tm") + hop < lax.axis_size("tm")
        for tile in range(tiles):
            state[at, :, :] = jnp.where(there, halo[tile, :, :].astype(jnp.float32), 0.0)
            at += 1
    for tile in range(at, at + plan.empty_tiles):
        state[tile, :, :] = jnp.zeros((chan_rows, LANES), jnp.float32)
    last = tree_levels(state, other, columns, 0, levels, block_rows, plan.lengths)
    head = kept if plan.taken else 0
    for tile in range(head):
        normal[tile, :, :] = carried[tile, :, :]
    for tile in range(plan.made):
        normal[head + tile, :, :] = (last[tile, :, :] * scale).astype(jnp.bfloat16)
    count = plan.out_tiles
    if plan.given:
        for tile in range(kept):
            handed[tile, :, :] = normal[count + tile, :, :]
    copies = []
    for turn, (first_tile, some) in enumerate(plan.chunks):
        size = some * chan_rows
        windows = [
            normal[first_tile + offset : first_tile + offset + some, :, :].reshape(size, LANES)
            for offset in range(kept + 1)
        ]
        responses[0:size, :] = lax.dot_general(
            jnp.concatenate(windows, axis=1),
            taps[...],
            (((1,), (1,)), ((), ())),
            preferred_element_type=jnp.float32,
        )
        for first_row in range(0, size, PACKED):
            energies = []
            for width in range(width_count):
                one = responses[first_row : first_row + PACKED, width * LANES : (width + 1) * LANES]
                energies.append((0.5 * LOG2_E) * one * one)
            highest = functools.reduce(jnp.maximum, energies)
            total = functools.reduce(jnp.add, [jnp.exp2(energy - highest) for energy in energies])
            tile, row = first_tile + first_row // chan_rows, first_row % chan_rows
            result[row : row + PACKED, tile * LANES : (tile + 1) * LANES] = (
                jnp.log2(total) + highest
            ) * (1.0 / LOG2_E)
        columns_now = pl.ds(first_tile * LANES, some * LANES)
        place = out.at[:, pl.ds((plan.out_first + first_tile) * LANES, some * LANES)]
        copies.append(pltpu.make_async_copy(result.at[:, columns_now], place, arrived.at[turn]))
        copies[-1].start()
    for copy in copies:
        copy.wait()


class Plan:
    def __init__(self, main_tiles, halos, empty_tiles, out_first, out_tiles, taken, given, levels, tap_tiles):
        self.main_tiles, self.halos, self.empty_tiles = main_tiles, halos, empty_tiles
        self.out_first, self.out_tiles = out_first, out_tiles
        self.taken, self.given = taken, given
        self.made = out_tiles if taken else out_tiles + tap_tiles
        self.first = out_first + tap_tiles if taken else 0
        self.lengths = lengths_of(self.made, levels)
        turns = -(-out_tiles // 6)
        ends = [out_tiles * turn // turns for turn in range(turns + 1)]
        self.chunks = [(start, end - start) for start, end in zip(ends, ends[1:])]
        self.state_tiles = main_tiles + sum(halos) + empty_tiles - self.first + max(2 ** levels[-1] // LANES, 1) + 1


def local(filterbank, delay_shifts, pulse_filters):
    chan_rows, time_len = filterbank.shape
    group_count = lax.axis_size("freq")
    assert lax.axis_size("sub") == 2 and 2 * chan_rows == LANES
    level_count = delay_shifts.shape[0]
    width_count, tap_count = pulse_filters.shape
    tap_tiles = tap_count // LANES
    time_tiles = time_len // LANES
    far_levels = range(level_count - bits_of(group_count), level_count)
    near_reach = 2 ** far_levels[0] - 1
    near_len = rounded_up(near_reach, LANES)
    far_tiles = -(-(2**level_count - 1 - near_reach + tap_count) // LANES)

    in_vmem = pl.BlockSpec(memory_space=pltpu.VMEM)
    in_any = pl.BlockSpec(memory_space=pl.ANY)
    params = pltpu.CompilerParams(vmem_limit_bytes=VMEM_LIMIT)
    block_rows = chan_rows // group_count
    table = pltpu.VMEM((LANES, LANES), jnp.float32)

    def within_chip(operands, spans, raw_tiles, out_tiles, sending):
        state = pltpu.VMEM((raw_tiles + 1, chan_rows, LANES), jnp.float32)
        if sending:
            block = jax.ShapeDtypeStruct((time_tiles, block_rows, LANES), jnp.bfloat16)
            out_shape = [block] * group_count
        else:
            out_shape = [
                jax.ShapeDtypeStruct((out_tiles, chan_rows, LANES), jnp.float32),
                jax.ShapeDtypeStruct((LANES, LANES), jnp.float32),
            ]
        return pl.pallas_call(
            functools.partial(chip_kernel, spans, out_tiles, group_count if sending else 0),
            out_shape=out_shape,
            in_specs=[in_vmem] * len(operands),
            out_specs=[in_vmem] * len(out_shape),
            scratch_shapes=[pltpu.VMEM((raw_tiles + 1, 2 * chan_rows, LANES), jnp.float32), state, state]
            + ([] if sending else [table]),
            compiler_params=params,
        )(*operands)

    def between_chips(plan, blocks, halos, carried=()):
        state = pltpu.VMEM((plan.state_tiles, chan_rows, LANES), jnp.float32)
        operands = [columns, taps, *blocks, *halos, *carried]
        in_specs = [in_vmem] * len(operands)
        aliases = {}
        if plan.taken:
            in_specs[-1] = in_any
            aliases = {len(operands) - 1: 0}
        out_shape = [jax.ShapeDtypeStruct((chan_rows, time_len), jnp.float32)]
        out_specs = [in_any]
        if plan.given:
            out_shape.append(jax.ShapeDtypeStruct((tap_tiles, chan_rows, LANES), jnp.bfloat16))
            out_specs.append(in_vmem)
        most = max(some for _, some in plan.chunks)
        scale = 1.0 / math.sqrt(delay_shifts.shape[1])
        return pl.pallas_call(
            functools.partial(trial_kernel, plan, group_count, level_count, scale),
            out_shape=out_shape,
            in_specs=in_specs,
            out_specs=out_specs,
            scratch_shapes=[
                state,
                state,
                pltpu.VMEM((plan.out_tiles + tap_tiles, chan_rows, LANES), jnp.bfloat16),
                pltpu.VMEM((most * chan_rows, width_count * LANES), jnp.float32),
                pltpu.VMEM((chan_rows, plan.out_tiles * LANES), jnp.float32),
                pltpu.SemaphoreType.DMA((len(plan.chunks),)),
            ],
            input_output_aliases=aliases,
            compiler_params=params,
        )(*operands)

    other_core = from_partner(filterbank, "sub", 1)
    own, ahead = pl.pallas_call(
        load_kernel,
        out_shape=[
            jax.ShapeDtypeStruct(filterbank.shape, filterbank.dtype),
            jax.ShapeDtypeStruct((chan_rows, near_len), filterbank.dtype),
        ],
        in_specs=[in_vmem],
        out_specs=[in_vmem] * 2,
        compiler_params=params,
    )(filterbank)
    near_tiles = near_len // LANES
    early = time_tiles - near_tiles
    rows, delays = within_chip(
        [own, other_core, delay_shifts], [(0, time_len, 0)], time_tiles, early, False
    )
    both, spans = ([own], [other_core]), [(early * LANES, near_len, 0)]
    if lax.axis_size("tm") > 1:
        for crossed in range(2):
            both[crossed].append(from_ahead(ahead, 1, crossed))
        spans.append((0, near_len, 1))
    main = list(within_chip([*both[0], *both[1], rows, delays], spans, 2 * near_tiles, near_tiles, True))
    late_shifts, late_filters, main[0] = lax.optimization_barrier((delay_shifts, pulse_filters, main[0]))
    columns, taps = pl.pallas_call(
        functools.partial(table_kernel, group_count, block_rows),
        out_shape=[
            jax.ShapeDtypeStruct((LANES, LANES), jnp.float32),
            jax.ShapeDtypeStruct((width_count * LANES, tap_count + LANES), jnp.bfloat16),
        ],
        in_specs=[in_vmem] * 2,
        out_specs=[in_vmem] * 2,
        scratch_shapes=[table],
        compiler_params=params,
    )(late_shifts, late_filters)
    *main, last = exchanged(main)
    columns, taps, last = lax.optimization_barrier((columns, taps, last))
    main.append(last)

    halos, takes = [], []
    rest = far_tiles
    if lax.axis_size("tm") > 1:
        first_tiles = min(time_tiles, far_tiles)
        gathered_rows = pl.pallas_call(
            gather_kernel,
            out_shape=jax.ShapeDtypeStruct((first_tiles, chan_rows, LANES), jnp.bfloat16),
            in_specs=[in_vmem] * group_count,
            out_specs=in_vmem,
            scratch_shapes=[pltpu.VMEM((first_tiles, chan_rows, LANES), jnp.float32)],
            compiler_params=params,
        )(*main)
        for hop in range(1, lax.axis_size("tm")):
            if rest > 0:
                takes.append(min(time_tiles, rest))
                halos.append(from_ahead(gathered_rows[: takes[-1]], hop, 0))
                rest -= takes[-1]
    lost = -(-sum(2**level for level in far_levels) // LANES) + tap_tiles
    early_tiles = time_tiles - lost
    if early_tiles <= 0:
        plan = Plan(time_tiles, takes, rest, 0, time_tiles, False, False, far_levels, tap_tiles)
        return between_chips(plan, main, halos)[0]
    plan = Plan(time_tiles, [], 0, 0, early_tiles, False, True, far_levels, tap_tiles)
    out, *carried = between_chips(plan, main, [])
    late_tiles = time_tiles - early_tiles
    plan = Plan(time_tiles, takes, rest, early_tiles, late_tiles, True, False, far_levels, tap_tiles)
    return between_chips(plan, main, halos, [*carried, out])[0]


def solution(mesh):
    in_specs = (P(("beams", "freq", "sub"), "tm"), P(), P())
    out_specs = P(("beams", "freq", "sub"), "tm")
    return jax.shard_map(local, mesh=mesh, in_specs=in_specs, out_specs=out_specs, check_vma=False)
```

```python
import functools
import math

import jax
import jax.numpy as jnp
from jax import lax
from jax.experimental import pallas as pl
from jax.experimental.pallas import tpu as pltpu
from jax.sharding import PartitionSpec as P

LANES = 128
SUBLANES = 8
PACKED = 16
LOG2_E = 1.4426950408889634
VMEM_LIMIT = 48 * 2**20


def rounded_up(value, unit):
    return -(-value // unit) * unit


def reversed_bits(value, bit_count):
    result = 0
    for bit_num in range(bit_count):
        result = result | (value >> bit_num & 1) << bit_count - 1 - bit_num
    return result


def bits_of(count):
    return count.bit_length() - 1


def from_ahead(value, steps, crossed):
    count, cores = lax.axis_size("tm"), lax.axis_size("sub")
    route = [
        ((block + steps) % count * cores + core, block * cores + (core ^ crossed))
        for block in range(count)
        for core in range(cores)
    ]
    return lax.ppermute(value, ("tm", "sub"), route)


def from_partner(value, axis, mask):
    count = lax.axis_size(axis)
    return lax.ppermute(value, axis, [(source, source ^ mask) for source in range(count)])


def mask_orders(group_count):
    order = list(range(group_count - 1, 0, -1))
    return order, order[-1:] + order[:-1]


def step_masks(group_count, core):
    orders = mask_orders(group_count)
    return [0] + [jnp.where(core == 0, first, second) for first, second in zip(*orders)]


def exchanged(blocks):
    count = lax.axis_size("freq")
    received = [blocks[0]]
    for block, masks in zip(blocks[1:], zip(*mask_orders(count))):
        route = [
            (chip * 2 + core, (chip ^ masks[core]) * 2 + core) for chip in range(count) for core in range(2)
        ]
        received.append(lax.ppermute(block, ("freq", "sub"), route))
    return received


def lanes():
    return lax.broadcasted_iota(jnp.int32, (SUBLANES, LANES), 1)


def gathered(value, index):
    return jnp.take_along_axis(value, index, axis=1, mode="promise_in_bounds")


def transposed_table(rows, table, columns):
    for index, row in enumerate(rows):
        table[index : index + 1, :] = row.astype(jnp.float32)
    columns[...] = table[...].T


def merge(source, target, low, high, outs, tiles, most):
    lane = lanes()
    apart = max(most // LANES, 1)
    chosen = []
    for amount, place in outs:
        part = amount if most < LANES else amount & LANES - 1
        moved = (lane < part).astype(jnp.int32)
        if most >= LANES:
            moved = moved + (amount >> bits_of(LANES))
        masks = [moved == offset for offset in range(1, apart + 1)]
        chosen.append((masks, lane + part & LANES - 1, place))
    for masks, index, place in chosen:
        upper = [source[offset, high, :] for offset in range(apart)]
        for tile in range(tiles):
            upper.append(source[tile + apart, high, :])
            mixed = upper[0]
            for mask, other in zip(masks, upper[1:]):
                mixed = jnp.where(mask, other, mixed)
            target[tile, place, :] = source[tile, low, :] + gathered(mixed, index)
            upper = upper[1:]


def tree_levels(state, other, columns, first, levels, held, lengths, packed=False):
    rows = columns.shape[0] // 2
    source, target = state, other
    done = 0
    while done < len(levels):
        narrow = held < SUBLANES
        bits = min(bits_of(SUBLANES // held), len(levels) - done) if narrow else len(levels) - done
        for turn in range(bits):
            level = levels[done + turn]
            inner = turn + 1 < bits
            natural = turn == 0 and not (packed and done == 0)

            def rows_in(vector, start, stride):
                return pl.ds(start, SUBLANES, stride=stride) if natural else pl.ds(vector * SUBLANES, SUBLANES)

            def rows_out(vector, start, stride):
                return pl.ds(vector * SUBLANES, SUBLANES) if inner else pl.ds(start, SUBLANES, stride=stride)

            def amounts(start, stride):
                column = columns[pl.ds(start, SUBLANES, stride=stride), :]
                one = column[:, first + done + turn : first + done + turn + 1]
                return jnp.broadcast_to(one, (SUBLANES, LANES)).astype(jnp.int32)

            if narrow:
                now = held << turn
                for band in range(SUBLANES // (2 * now)):
                    for trial in range(now):
                        low, high = 2 * band * now + trial, (2 * band + 1) * now + trial
                        outs = [band * 2 * now + 2 * trial + odd for odd in range(2)]
                        merge(
                            source,
                            target,
                            rows_in(low, low, SUBLANES),
                            rows_in(high, high, SUBLANES),
                            [(amounts(out, SUBLANES), rows_out(out, out, SUBLANES)) for out in outs],
                            lengths[done + turn],
                            2**level,
                        )
            else:
                groups, split = held // SUBLANES, 2**turn
                for band in range(rows // (2 * held * split)):
                    for group in range(groups):
                        for place in range(split):
                            low, high = [
                                ((2 * band + upper) * groups + group) * split + place for upper in range(2)
                            ]
                            outs = []
                            for odd in range(2):
                                vector = (band * groups + group) * 2 * split + 2 * place + odd
                                start = (band * groups + group) * SUBLANES * 2 * split + 2 * place + odd
                                outs.append((amounts(start, 2 * split), rows_out(vector, start, 2 * split)))
                            merge(
                                source,
                                target,
                                rows_in(low, low * SUBLANES, 1),
                                rows_in(high, high * SUBLANES, 1),
                                outs,
                                lengths[done + turn],
                                2**level,
                            )
            source, target = target, source
        held <<= bits
        done += bits
    return source


def lengths_of(made, levels):
    return [made + -(-sum(2**later for later in levels if later > level) // LANES) for level in levels]


def load_kernel(whole, copied, ahead):
    copied[...] = whole[...]
    ahead[...] = whole[:, : ahead.shape[1]]


def placed(target, blocks, tiles, skip):
    chip, core = lax.axis_index("freq"), lax.axis_index("sub")
    rows = blocks[0].shape[1]
    for mask, block in zip(step_masks(len(blocks), core), blocks):
        start = pl.multiple_of((chip ^ mask) * rows, rows)
        for tile in range(skip, tiles):
            target[tile - skip, pl.ds(start, rows), :] = block[tile, :, :].astype(jnp.float32)


def join_kernel(*refs):
    *blocks, out, state = refs
    rows = blocks[0].shape[1]
    for tile in range(out.shape[0]):
        for index, block in enumerate(blocks):
            state[tile, index * rows : (index + 1) * rows, :] = block[tile, :, :].astype(jnp.float32)
        out[tile, :, :] = state[tile, :, :].astype(jnp.bfloat16)


def chip_kernel(spans, out_tiles, group_count, *refs):
    pieces = (refs[: len(spans)], refs[len(spans) : 2 * len(spans)])
    refs = refs[2 * len(spans) :]
    chan_rows = pieces[0][0].shape[0]
    local_count = bits_of(chan_rows)
    chip, core = lax.axis_index("freq"), lax.axis_index("sub")
    if group_count:
        (earlier, columns), blocks, (raw, ping, pong) = refs[:2], refs[2:-3], refs[-3:]
    else:
        shifts, rows, columns, raw, ping, pong, table = refs
        chunk = shifts[0:SUBLANES, pl.ds(pl.multiple_of(chip * LANES, LANES), LANES)]
        lane, level = lanes(), lax.broadcasted_iota(jnp.int32, (SUBLANES, LANES), 0)
        kept = lane & (1 << level) - 1
        picked = gathered(chunk, (2 * (lane - kept) + (core << level) + kept) & LANES - 1)
        transposed_table([picked[at : at + 1, :] for at in range(local_count + 1)], table, columns)
    for side in range(2):
        place = pl.multiple_of((core ^ side) * chan_rows, chan_rows)
        tile = 0
        for piece, (column, length, ahead) in zip(pieces[side], spans):
            there = lax.axis_index("tm") + ahead < lax.axis_size("tm")
            for start in range(column, column + length, LANES):
                part = piece[:, start : start + LANES].astype(jnp.float32)
                if ahead:
                    part = jnp.where(there, part, 0.0)
                raw[tile, pl.ds(place, chan_rows), :] = part
                tile += 1
        for later in range(tile, raw.shape[0] - 1):
            raw[later, pl.ds(place, chan_rows), :] = jnp.zeros((chan_rows, LANES), jnp.float32)
    levels = list(range(local_count + 1))
    lengths = lengths_of(out_tiles, levels)
    mask = lanes() >= core
    for vector in range(SUBLANES):
        low, high = [pl.ds(2 * vector + odd, SUBLANES, stride=2 * SUBLANES) for odd in range(2)]
        upper = raw[0, high, :]
        for tile in range(lengths[0]):
            later = raw[tile + 1, high, :]
            moved = pltpu.roll(jnp.where(mask, upper, later), LANES - core & LANES - 1, 1)
            ping[tile, pl.ds(vector * SUBLANES, SUBLANES), :] = raw[tile, low, :] + moved
            upper = later
    last = tree_levels(ping, pong, columns, 1, levels[1:], 1, lengths[1:], packed=True)
    if not group_count:
        for tile in range(out_tiles):
            rows[tile, :, :] = last[tile, :, :]
        return
    size = chan_rows // group_count
    own = reversed_bits(chip, bits_of(group_count))
    first = earlier.shape[0]
    for mask, block in zip(step_masks(group_count, core), blocks):
        start = pl.multiple_of((own ^ reversed_bits(mask, bits_of(group_count))) * size, size)
        for tile in range(first):
            block[tile, :, :] = earlier[tile, pl.ds(start, size), :].astype(jnp.bfloat16)
        for tile in range(out_tiles):
            block[first + tile, :, :] = last[tile, pl.ds(start, size), :].astype(jnp.bfloat16)


def toeplitz(filters, target):
    width_count, tap_count = filters.shape
    lane = lax.broadcasted_iota(jnp.int32, (LANES, LANES), 1)
    row = lax.broadcasted_iota(jnp.int32, (LANES, LANES), 0)
    taps = filters[...].astype(jnp.float32)
    zeros = jnp.zeros((LANES, LANES), jnp.float32)
    for width in range(width_count):
        before = zeros
        for start in range(0, tap_count + LANES, LANES):
            if start < tap_count:
                spread = jnp.broadcast_to(taps[width : width + 1, start : start + LANES], (LANES, LANES))
                rolled = pltpu.roll(spread, 0, 1, stride=1, stride_axis=0)
            else:
                rolled = zeros
            part = jnp.where(lane >= row, rolled, before)
            target[width * LANES : (width + 1) * LANES, start : start + LANES] = part.astype(jnp.bfloat16)
            before = rolled


def table_kernel(group_count, block_rows, shifts, filters, columns, taps, table):
    level_count = shifts.shape[0]
    chip, core = lax.axis_index("freq"), lax.axis_index("sub")
    own = reversed_bits(chip * 2 + core, bits_of(group_count) + 1)
    lane = lax.broadcasted_iota(jnp.int32, (1, LANES), 1)
    rows = []
    for section in range(bits_of(group_count)):
        level = level_count - bits_of(group_count) + section
        wide = block_rows * 2 ** (section + 1)
        row = jnp.zeros((1, LANES), jnp.int32)
        for subband in range(block_rows * group_count // wide):
            start = subband * 2 ** (level + 1) + own * wide
            tile = pl.multiple_of(start >> bits_of(LANES) << bits_of(LANES), LANES)
            chunk = shifts[level : level + 1, pl.ds(tile, LANES)]
            moved = pltpu.roll(chunk, subband * wide - (start & LANES - 1) & LANES - 1, 1)
            row = jnp.where(lane >= subband * wide, moved, row)
        rows.append(row)
    transposed_table(rows, table, columns)
    toeplitz(filters, taps)


def trial_kernel(plan, group_count, level_count, scale, columns, taps, *refs):
    blocks, refs = refs[:group_count], refs[group_count:]
    halos, refs = refs[: 2 * len(plan.halos)], refs[2 * len(plan.halos) :]
    if plan.taken:
        carried, so_far, refs = refs[0], refs[1], refs[2:]
    out, refs = refs[0], refs[1:]
    if plan.given:
        handed, refs = refs[0], refs[1:]
    state, other, normal, responses, *refs = refs
    if plan.given:
        result = out
    else:
        result, arrived = refs
    chan_rows = result.shape[0]
    block_rows = chan_rows // group_count
    width_count, kept = taps.shape[0] // LANES, taps.shape[1] // LANES - 1
    levels = list(range(level_count - bits_of(group_count), level_count))
    copies = []
    if plan.taken:
        place = out.at[:, pl.ds(0, plan.out_first * LANES)]
        copies.append(pltpu.make_async_copy(so_far, place, arrived.at[len(plan.chunks)]))
        copies[0].start()
    placed(state, blocks, plan.main_tiles, plan.first)
    at = plan.main_tiles - plan.first
    chip, core = lax.axis_index("freq"), lax.axis_index("sub")
    for hop, tiles in enumerate(plan.halos, 1):
        there = lax.axis_index("tm") + hop < lax.axis_size("tm")
        for tile in range(tiles):
            joined, single = [
                jnp.where(there, halo[tile, :, :].astype(jnp.float32), 0.0)
                for halo in halos[2 * hop - 2 : 2 * hop]
            ]
            for index, mask in enumerate(step_masks(group_count, core)):
                start = pl.multiple_of((chip ^ mask) * block_rows, block_rows)
                if index + 1 < group_count:
                    part = joined[index * block_rows : (index + 1) * block_rows]
                else:
                    part = single
                state[at, pl.ds(start, block_rows), :] = part
            at += 1
    for tile in range(at, at + plan.empty_tiles):
        state[tile, :, :] = jnp.zeros((chan_rows, LANES), jnp.float32)
    last = tree_levels(state, other, columns, 0, levels, block_rows, plan.lengths)
    head = kept if plan.taken else 0
    for tile in range(head):
        normal[tile, :, :] = carried[tile, :, :]
    for tile in range(plan.made):
        normal[head + tile, :, :] = (last[tile, :, :] * scale).astype(jnp.bfloat16)
    count = plan.out_tiles
    if plan.given:
        for tile in range(kept):
            handed[tile, :, :] = normal[count + tile, :, :]
    for turn, (first_tile, some) in enumerate(plan.chunks):
        size = some * chan_rows
        windows = [
            normal[first_tile + offset : first_tile + offset + some, :, :].reshape(size, LANES)
            for offset in range(kept + 1)
        ]
        responses[0:size, :] = lax.dot_general(
            jnp.concatenate(windows, axis=1),
            taps[...],
            (((1,), (1,)), ((), ())),
            preferred_element_type=jnp.float32,
        )
        for first_row in range(0, size, PACKED):
            energies = []
            for width in range(width_count):
                one = responses[first_row : first_row + PACKED, width * LANES : (width + 1) * LANES]
                energies.append((0.5 * LOG2_E) * one * one)
            highest = functools.reduce(jnp.maximum, energies)
            total = functools.reduce(jnp.add, [jnp.exp2(energy - highest) for energy in energies])
            tile, row = first_tile + first_row // chan_rows, first_row % chan_rows
            result[row : row + PACKED, tile * LANES : (tile + 1) * LANES] = (
                jnp.log2(total) + highest
            ) * (1.0 / LOG2_E)
        if plan.given:
            continue
        columns_now = pl.ds(first_tile * LANES, some * LANES)
        place = out.at[:, pl.ds((plan.out_first + first_tile) * LANES, some * LANES)]
        copies.append(pltpu.make_async_copy(result.at[:, columns_now], place, arrived.at[turn]))
        copies[-1].start()
    for copy in copies:
        copy.wait()


class Plan:
    def __init__(self, main_tiles, halos, empty_tiles, out_first, out_tiles, taken, given, levels, tap_tiles):
        self.main_tiles, self.halos, self.empty_tiles = main_tiles, halos, empty_tiles
        self.out_first, self.out_tiles = out_first, out_tiles
        self.taken, self.given = taken, given
        self.made = out_tiles if taken else out_tiles + tap_tiles
        self.first = out_first + tap_tiles if taken else 0
        self.lengths = lengths_of(self.made, levels)
        turns = -(-out_tiles // 6)
        ends = [out_tiles * turn // turns for turn in range(turns + 1)]
        self.chunks = [(start, end - start) for start, end in zip(ends, ends[1:])]
        self.state_tiles = main_tiles + sum(halos) + empty_tiles - self.first + max(2 ** levels[-1] // LANES, 1) + 1


def local(filterbank, delay_shifts, pulse_filters):
    chan_rows, time_len = filterbank.shape
    group_count = lax.axis_size("freq")
    assert lax.axis_size("sub") == 2 and 2 * chan_rows == LANES
    level_count = delay_shifts.shape[0]
    width_count, tap_count = pulse_filters.shape
    tap_tiles = tap_count // LANES
    time_tiles = time_len // LANES
    far_levels = range(level_count - bits_of(group_count), level_count)
    near_reach = 2 ** far_levels[0] - 1
    near_len = rounded_up(near_reach, LANES)
    far_tiles = -(-(2**level_count - 1 - near_reach + tap_count) // LANES)

    in_vmem = pl.BlockSpec(memory_space=pltpu.VMEM)
    in_any = pl.BlockSpec(memory_space=pl.ANY)
    params = pltpu.CompilerParams(vmem_limit_bytes=VMEM_LIMIT)
    block_rows = chan_rows // group_count
    table = pltpu.VMEM((LANES, LANES), jnp.float32)

    def within_chip(operands, spans, raw_tiles, out_tiles, sending):
        state = pltpu.VMEM((raw_tiles + 1, chan_rows, LANES), jnp.float32)
        if sending:
            block = jax.ShapeDtypeStruct((time_tiles, block_rows, LANES), jnp.bfloat16)
            out_shape = [block] * group_count
        else:
            out_shape = [
                jax.ShapeDtypeStruct((out_tiles, chan_rows, LANES), jnp.float32),
                jax.ShapeDtypeStruct((LANES, LANES), jnp.float32),
            ]
        return pl.pallas_call(
            functools.partial(chip_kernel, spans, out_tiles, group_count if sending else 0),
            out_shape=out_shape,
            in_specs=[in_vmem] * len(operands),
            out_specs=[in_vmem] * len(out_shape),
            scratch_shapes=[pltpu.VMEM((raw_tiles + 1, 2 * chan_rows, LANES), jnp.float32), state, state]
            + ([] if sending else [table]),
            compiler_params=params,
        )(*operands)

    def between_chips(plan, blocks, halos, carried=()):
        state = pltpu.VMEM((plan.state_tiles, chan_rows, LANES), jnp.float32)
        operands = [columns, taps, *blocks, *halos, *carried]
        result = (chan_rows, plan.out_tiles * LANES)
        if plan.given:
            out_shape = [
                jax.ShapeDtypeStruct(result, jnp.float32),
                jax.ShapeDtypeStruct((tap_tiles, chan_rows, LANES), jnp.bfloat16),
            ]
            out_specs, scratch = [in_vmem] * 2, []
        else:
            out_shape, out_specs = [jax.ShapeDtypeStruct((chan_rows, time_len), jnp.float32)], [in_any]
            scratch = [pltpu.VMEM(result, jnp.float32), pltpu.SemaphoreType.DMA((len(plan.chunks) + 1,))]
        most = max(some for _, some in plan.chunks)
        scale = 1.0 / math.sqrt(delay_shifts.shape[1])
        return pl.pallas_call(
            functools.partial(trial_kernel, plan, group_count, level_count, scale),
            out_shape=out_shape,
            in_specs=[in_vmem] * len(operands),
            out_specs=out_specs,
            scratch_shapes=[
                state,
                state,
                pltpu.VMEM((plan.out_tiles + tap_tiles, chan_rows, LANES), jnp.bfloat16),
                pltpu.VMEM((most * chan_rows, width_count * LANES), jnp.float32),
            ]
            + scratch,
            compiler_params=params,
        )(*operands)

    other_core = from_partner(filterbank, "sub", 1)
    own, ahead = pl.pallas_call(
        load_kernel,
        out_shape=[
            jax.ShapeDtypeStruct(filterbank.shape, filterbank.dtype),
            jax.ShapeDtypeStruct((chan_rows, near_len), filterbank.dtype),
        ],
        in_specs=[in_vmem],
        out_specs=[in_vmem] * 2,
        compiler_params=params,
    )(filterbank)
    near_tiles = near_len // LANES
    early = time_tiles - near_tiles
    rows, delays = within_chip(
        [own, other_core, delay_shifts], [(0, time_len, 0)], time_tiles, early, False
    )
    both, spans = ([own], [other_core]), [(early * LANES, near_len, 0)]
    if lax.axis_size("tm") > 1:
        for crossed in range(2):
            both[crossed].append(from_ahead(ahead, 1, crossed))
        spans.append((0, near_len, 1))
    main = list(within_chip([*both[0], *both[1], rows, delays], spans, 2 * near_tiles, near_tiles, True))
    late_shifts, late_filters, main[0] = lax.optimization_barrier((delay_shifts, pulse_filters, main[0]))
    columns, taps = pl.pallas_call(
        functools.partial(table_kernel, group_count, block_rows),
        out_shape=[
            jax.ShapeDtypeStruct((LANES, LANES), jnp.float32),
            jax.ShapeDtypeStruct((width_count * LANES, tap_count + LANES), jnp.bfloat16),
        ],
        in_specs=[in_vmem] * 2,
        out_specs=[in_vmem] * 2,
        scratch_shapes=[table],
        compiler_params=params,
    )(late_shifts, late_filters)
    *main, last = exchanged(main)
    columns, taps, last = lax.optimization_barrier((columns, taps, last))
    main.append(last)

    halos, takes = [], []
    rest = far_tiles
    if lax.axis_size("tm") > 1:
        first_tiles = min(time_tiles, far_tiles)
        joined = pl.pallas_call(
            join_kernel,
            out_shape=jax.ShapeDtypeStruct(
                (first_tiles, chan_rows - block_rows, LANES), jnp.bfloat16
            ),
            in_specs=[in_vmem] * (group_count - 1),
            out_specs=in_vmem,
            scratch_shapes=[pltpu.VMEM((first_tiles, chan_rows - block_rows, LANES), jnp.float32)],
            compiler_params=params,
        )(*main[:-1])
        for hop in range(1, lax.axis_size("tm")):
            if rest > 0:
                takes.append(min(time_tiles, rest))
                halos.append(from_ahead(joined[: takes[-1]], hop, 0))
                halos.append(from_ahead(main[-1][: takes[-1]], hop, 0))
                rest -= takes[-1]
    lost = -(-sum(2**level for level in far_levels) // LANES) + tap_tiles
    early_tiles = time_tiles - lost
    if early_tiles <= 0:
        plan = Plan(time_tiles, takes, rest, 0, time_tiles, False, False, far_levels, tap_tiles)
        return between_chips(plan, main, halos)[0]
    plan = Plan(time_tiles, [], 0, 0, early_tiles, False, True, far_levels, tap_tiles)
    out, *carried = between_chips(plan, main, [])
    late_tiles = time_tiles - early_tiles
    plan = Plan(time_tiles, takes, rest, early_tiles, late_tiles, True, False, far_levels, tap_tiles)
    return between_chips(plan, main, halos, [*carried, out])[0]


def solution(mesh):
    in_specs = (P(("beams", "freq", "sub"), "tm"), P(), P())
    out_specs = P(("beams", "freq", "sub"), "tm")
    return jax.shard_map(local, mesh=mesh, in_specs=in_specs, out_specs=out_specs, check_vma=False)
```

```python
import functools
import math

import jax
import jax.numpy as jnp
from jax import lax
from jax.experimental import pallas as pl
from jax.experimental.pallas import tpu as pltpu
from jax.sharding import PartitionSpec as P

LANES = 128
SUBLANES = 8
PACKED = 16
LOG2_E = 1.4426950408889634
VMEM_LIMIT = 48 * 2**20


def rounded_up(value, unit):
    return -(-value // unit) * unit


def reversed_bits(value, bit_count):
    result = 0
    for bit_num in range(bit_count):
        result = result | (value >> bit_num & 1) << bit_count - 1 - bit_num
    return result


def bits_of(count):
    return count.bit_length() - 1


def from_ahead(value, steps, crossed):
    count, cores = lax.axis_size("tm"), lax.axis_size("sub")
    route = [
        ((block + steps) % count * cores + core, block * cores + (core ^ crossed))
        for block in range(count)
        for core in range(cores)
    ]
    return lax.ppermute(value, ("tm", "sub"), route)


def from_partner(value, axis, mask):
    count = lax.axis_size(axis)
    return lax.ppermute(value, axis, [(source, source ^ mask) for source in range(count)])


def mask_orders(group_count):
    order = [1, *range(group_count - 1, 1, -1)]
    return order, order[-1:] + order[:-1]


def step_masks(group_count, core):
    orders = mask_orders(group_count)
    return [0] + [jnp.where(core == 0, first, second) for first, second in zip(*orders)]


def exchanged(blocks):
    count = lax.axis_size("freq")
    received = [blocks[0]]
    for block, masks in zip(blocks[1:], zip(*mask_orders(count))):
        route = [
            (chip * 2 + core, (chip ^ masks[core]) * 2 + core) for chip in range(count) for core in range(2)
        ]
        received.append(lax.ppermute(block, ("freq", "sub"), route))
    return received


def from_ahead_chip(block, steps):
    chips, times = lax.axis_size("freq"), lax.axis_size("tm")
    last = [order[-1] for order in mask_orders(chips)]
    route = [
        (
            ((chip ^ last[core]) * times + (time + steps) % times) * 2 + core,
            (chip * times + time) * 2 + core,
        )
        for chip in range(chips)
        for time in range(times)
        for core in range(2)
    ]
    return lax.ppermute(block, ("freq", "tm", "sub"), route)


def lanes():
    return lax.broadcasted_iota(jnp.int32, (SUBLANES, LANES), 1)


def gathered(value, index):
    return jnp.take_along_axis(value, index, axis=1, mode="promise_in_bounds")


def transposed_table(rows, table, columns):
    for index, row in enumerate(rows):
        table[index : index + 1, :] = row.astype(jnp.float32)
    columns[...] = table[...].T


def merge(source, target, low, high, outs, tiles, most):
    lane = lanes()
    apart = max(most // LANES, 1)
    chosen = []
    for amount, place in outs:
        part = amount if most < LANES else amount & LANES - 1
        moved = (lane < part).astype(jnp.int32)
        if most >= LANES:
            moved = moved + (amount >> bits_of(LANES))
        masks = [moved == offset for offset in range(1, apart + 1)]
        chosen.append((masks, lane + part & LANES - 1, place))
    for masks, index, place in chosen:
        upper = [source[offset, high, :] for offset in range(apart)]
        for tile in range(tiles):
            upper.append(source[tile + apart, high, :])
            mixed = upper[0]
            for mask, other in zip(masks, upper[1:]):
                mixed = jnp.where(mask, other, mixed)
            target[tile, place, :] = source[tile, low, :] + gathered(mixed, index)
            upper = upper[1:]


def tree_levels(state, other, columns, first, levels, held, lengths, packed=False):
    rows = columns.shape[0] // 2
    source, target = state, other
    done = 0
    while done < len(levels):
        narrow = held < SUBLANES
        bits = min(bits_of(SUBLANES // held), len(levels) - done) if narrow else len(levels) - done
        for turn in range(bits):
            level = levels[done + turn]
            inner = turn + 1 < bits
            natural = turn == 0 and not (packed and done == 0)

            def rows_in(vector, start, stride):
                return pl.ds(start, SUBLANES, stride=stride) if natural else pl.ds(vector * SUBLANES, SUBLANES)

            def rows_out(vector, start, stride):
                return pl.ds(vector * SUBLANES, SUBLANES) if inner else pl.ds(start, SUBLANES, stride=stride)

            def amounts(start, stride):
                column = columns[pl.ds(start, SUBLANES, stride=stride), :]
                one = column[:, first + done + turn : first + done + turn + 1]
                return jnp.broadcast_to(one, (SUBLANES, LANES)).astype(jnp.int32)

            if narrow:
                now = held << turn
                for band in range(SUBLANES // (2 * now)):
                    for trial in range(now):
                        low, high = 2 * band * now + trial, (2 * band + 1) * now + trial
                        outs = [band * 2 * now + 2 * trial + odd for odd in range(2)]
                        merge(
                            source,
                            target,
                            rows_in(low, low, SUBLANES),
                            rows_in(high, high, SUBLANES),
                            [(amounts(out, SUBLANES), rows_out(out, out, SUBLANES)) for out in outs],
                            lengths[done + turn],
                            2**level,
                        )
            else:
                groups, split = held // SUBLANES, 2**turn
                for band in range(rows // (2 * held * split)):
                    for group in range(groups):
                        for place in range(split):
                            low, high = [
                                ((2 * band + upper) * groups + group) * split + place for upper in range(2)
                            ]
                            outs = []
                            for odd in range(2):
                                vector = (band * groups + group) * 2 * split + 2 * place + odd
                                start = (band * groups + group) * SUBLANES * 2 * split + 2 * place + odd
                                outs.append((amounts(start, 2 * split), rows_out(vector, start, 2 * split)))
                            merge(
                                source,
                                target,
                                rows_in(low, low * SUBLANES, 1),
                                rows_in(high, high * SUBLANES, 1),
                                outs,
                                lengths[done + turn],
                                2**level,
                            )
            source, target = target, source
        held <<= bits
        done += bits
    return source


def lengths_of(made, levels):
    return [made + -(-sum(2**later for later in levels if later > level) // LANES) for level in levels]


def load_kernel(whole, copied, ahead):
    copied[...] = whole[...]
    ahead[...] = whole[:, : ahead.shape[1]]


def placed(target, blocks, tiles, skip):
    chip, core = lax.axis_index("freq"), lax.axis_index("sub")
    rows = blocks[0].shape[1]
    for mask, block in zip(step_masks(len(blocks), core), blocks):
        start = pl.multiple_of((chip ^ mask) * rows, rows)
        for tile in range(skip, tiles):
            target[tile - skip, pl.ds(start, rows), :] = block[tile, :, :].astype(jnp.float32)


def join_kernel(*refs):
    *blocks, out, state = refs
    rows = blocks[0].shape[1]
    for tile in range(out.shape[0]):
        for index, block in enumerate(blocks):
            state[tile, index * rows : (index + 1) * rows, :] = block[tile, :, :].astype(jnp.float32)
        out[tile, :, :] = state[tile, :, :].astype(jnp.bfloat16)


def chip_kernel(spans, out_tiles, group_count, *refs):
    pieces = (refs[: len(spans)], refs[len(spans) : 2 * len(spans)])
    refs = refs[2 * len(spans) :]
    chan_rows = pieces[0][0].shape[0]
    local_count = bits_of(chan_rows)
    chip, core = lax.axis_index("freq"), lax.axis_index("sub")
    if group_count:
        (earlier, columns), blocks, (raw, ping, pong) = refs[:2], refs[2:-3], refs[-3:]
    else:
        shifts, rows, columns, raw, ping, pong, table = refs
        chunk = shifts[0:SUBLANES, pl.ds(pl.multiple_of(chip * LANES, LANES), LANES)]
        lane, level = lanes(), lax.broadcasted_iota(jnp.int32, (SUBLANES, LANES), 0)
        kept = lane & (1 << level) - 1
        picked = gathered(chunk, (2 * (lane - kept) + (core << level) + kept) & LANES - 1)
        transposed_table([picked[at : at + 1, :] for at in range(local_count + 1)], table, columns)
    for side in range(2):
        place = pl.multiple_of((core ^ side) * chan_rows, chan_rows)
        tile = 0
        for piece, (column, length, ahead) in zip(pieces[side], spans):
            there = lax.axis_index("tm") + ahead < lax.axis_size("tm")
            for start in range(column, column + length, LANES):
                part = piece[:, start : start + LANES].astype(jnp.float32)
                if ahead:
                    part = jnp.where(there, part, 0.0)
                raw[tile, pl.ds(place, chan_rows), :] = part
                tile += 1
        for later in range(tile, raw.shape[0] - 1):
            raw[later, pl.ds(place, chan_rows), :] = jnp.zeros((chan_rows, LANES), jnp.float32)
    levels = list(range(local_count + 1))
    lengths = lengths_of(out_tiles, levels)
    mask = lanes() >= core
    for vector in range(SUBLANES):
        low, high = [pl.ds(2 * vector + odd, SUBLANES, stride=2 * SUBLANES) for odd in range(2)]
        upper = raw[0, high, :]
        for tile in range(lengths[0]):
            later = raw[tile + 1, high, :]
            moved = pltpu.roll(jnp.where(mask, upper, later), LANES - core & LANES - 1, 1)
            ping[tile, pl.ds(vector * SUBLANES, SUBLANES), :] = raw[tile, low, :] + moved
            upper = later
    last = tree_levels(ping, pong, columns, 1, levels[1:], 1, lengths[1:], packed=True)
    if not group_count:
        for tile in range(out_tiles):
            rows[tile, :, :] = last[tile, :, :]
        return
    size = chan_rows // group_count
    own = reversed_bits(chip, bits_of(group_count))
    first = earlier.shape[0]
    for mask, block in zip(step_masks(group_count, core), blocks):
        start = pl.multiple_of((own ^ reversed_bits(mask, bits_of(group_count))) * size, size)
        for tile in range(first):
            block[tile, :, :] = earlier[tile, pl.ds(start, size), :].astype(jnp.bfloat16)
        for tile in range(out_tiles):
            block[first + tile, :, :] = last[tile, pl.ds(start, size), :].astype(jnp.bfloat16)


def toeplitz(filters, target):
    width_count, tap_count = filters.shape
    lane = lax.broadcasted_iota(jnp.int32, (LANES, LANES), 1)
    row = lax.broadcasted_iota(jnp.int32, (LANES, LANES), 0)
    taps = filters[...].astype(jnp.float32)
    zeros = jnp.zeros((LANES, LANES), jnp.float32)
    for width in range(width_count):
        before = zeros
        for start in range(0, tap_count + LANES, LANES):
            if start < tap_count:
                spread = jnp.broadcast_to(taps[width : width + 1, start : start + LANES], (LANES, LANES))
                rolled = pltpu.roll(spread, 0, 1, stride=1, stride_axis=0)
            else:
                rolled = zeros
            part = jnp.where(lane >= row, rolled, before)
            target[width * LANES : (width + 1) * LANES, start : start + LANES] = part.astype(jnp.bfloat16)
            before = rolled


def table_kernel(group_count, block_rows, shifts, filters, columns, taps, table):
    level_count = shifts.shape[0]
    chip, core = lax.axis_index("freq"), lax.axis_index("sub")
    own = reversed_bits(chip * 2 + core, bits_of(group_count) + 1)
    lane = lax.broadcasted_iota(jnp.int32, (1, LANES), 1)
    rows = []
    for section in range(bits_of(group_count)):
        level = level_count - bits_of(group_count) + section
        wide = block_rows * 2 ** (section + 1)
        row = jnp.zeros((1, LANES), jnp.int32)
        for subband in range(block_rows * group_count // wide):
            start = subband * 2 ** (level + 1) + own * wide
            tile = pl.multiple_of(start >> bits_of(LANES) << bits_of(LANES), LANES)
            chunk = shifts[level : level + 1, pl.ds(tile, LANES)]
            moved = pltpu.roll(chunk, subband * wide - (start & LANES - 1) & LANES - 1, 1)
            row = jnp.where(lane >= subband * wide, moved, row)
        rows.append(row)
    transposed_table(rows, table, columns)
    toeplitz(filters, taps)


def trial_kernel(plan, group_count, level_count, scale, columns, taps, *refs):
    blocks, refs = refs[:group_count], refs[group_count:]
    halos, refs = refs[: 2 * len(plan.halos)], refs[2 * len(plan.halos) :]
    if plan.taken:
        carried, so_far, refs = refs[0], refs[1], refs[2:]
    out, refs = refs[0], refs[1:]
    if plan.given:
        handed, refs = refs[0], refs[1:]
    state, other, normal, responses, *refs = refs
    if plan.given:
        result = out
    else:
        result, arrived = refs
    chan_rows = result.shape[0]
    block_rows = chan_rows // group_count
    width_count, kept = taps.shape[0] // LANES, taps.shape[1] // LANES - 1
    levels = list(range(level_count - bits_of(group_count), level_count))
    copies = []
    if plan.taken:
        place = out.at[:, pl.ds(0, plan.out_first * LANES)]
        copies.append(pltpu.make_async_copy(so_far, place, arrived.at[len(plan.chunks)]))
        copies[0].start()
    placed(state, blocks, plan.main_tiles, plan.first)
    at = plan.main_tiles - plan.first
    chip, core = lax.axis_index("freq"), lax.axis_index("sub")
    for hop, tiles in enumerate(plan.halos, 1):
        there = lax.axis_index("tm") + hop < lax.axis_size("tm")
        for tile in range(tiles):
            joined, single = [
                jnp.where(there, halo[tile, :, :].astype(jnp.float32), 0.0)
                for halo in halos[2 * hop - 2 : 2 * hop]
            ]
            for index, mask in enumerate(step_masks(group_count, core)):
                start = pl.multiple_of((chip ^ mask) * block_rows, block_rows)
                if index + 1 < group_count:
                    part = joined[index * block_rows : (index + 1) * block_rows]
                else:
                    part = single
                state[at, pl.ds(start, block_rows), :] = part
            at += 1
    for tile in range(at, at + plan.empty_tiles):
        state[tile, :, :] = jnp.zeros((chan_rows, LANES), jnp.float32)
    last = tree_levels(state, other, columns, 0, levels, block_rows, plan.lengths)
    head = kept if plan.taken else 0
    for tile in range(head):
        normal[tile, :, :] = carried[tile, :, :]
    for tile in range(plan.made):
        normal[head + tile, :, :] = (last[tile, :, :] * scale).astype(jnp.bfloat16)
    count = plan.out_tiles
    if plan.given:
        for tile in range(kept):
            handed[tile, :, :] = normal[count + tile, :, :]
    for turn, (first_tile, some) in enumerate(plan.chunks):
        size = some * chan_rows
        windows = [
            normal[first_tile + offset : first_tile + offset + some, :, :].reshape(size, LANES)
            for offset in range(kept + 1)
        ]
        responses[0:size, :] = lax.dot_general(
            jnp.concatenate(windows, axis=1),
            taps[...],
            (((1,), (1,)), ((), ())),
            preferred_element_type=jnp.float32,
        )
        for first_row in range(0, size, PACKED):
            energies = []
            for width in range(width_count):
                one = responses[first_row : first_row + PACKED, width * LANES : (width + 1) * LANES]
                energies.append((0.5 * LOG2_E) * one * one)
            highest = functools.reduce(jnp.maximum, energies)
            total = functools.reduce(jnp.add, [jnp.exp2(energy - highest) for energy in energies])
            tile, row = first_tile + first_row // chan_rows, first_row % chan_rows
            result[row : row + PACKED, tile * LANES : (tile + 1) * LANES] = (
                jnp.log2(total) + highest
            ) * (1.0 / LOG2_E)
        if plan.given:
            continue
        columns_now = pl.ds(first_tile * LANES, some * LANES)
        place = out.at[:, pl.ds((plan.out_first + first_tile) * LANES, some * LANES)]
        copies.append(pltpu.make_async_copy(result.at[:, columns_now], place, arrived.at[turn]))
        copies[-1].start()
    for copy in copies:
        copy.wait()


class Plan:
    def __init__(self, main_tiles, halos, empty_tiles, out_first, out_tiles, taken, given, levels, tap_tiles):
        self.main_tiles, self.halos, self.empty_tiles = main_tiles, halos, empty_tiles
        self.out_first, self.out_tiles = out_first, out_tiles
        self.taken, self.given = taken, given
        self.made = out_tiles if taken else out_tiles + tap_tiles
        self.first = out_first + tap_tiles if taken else 0
        self.lengths = lengths_of(self.made, levels)
        turns = -(-out_tiles // 6)
        ends = [out_tiles * turn // turns for turn in range(turns + 1)]
        self.chunks = [(start, end - start) for start, end in zip(ends, ends[1:])]
        self.state_tiles = main_tiles + sum(halos) + empty_tiles - self.first + max(2 ** levels[-1] // LANES, 1) + 1


def local(filterbank, delay_shifts, pulse_filters):
    chan_rows, time_len = filterbank.shape
    group_count = lax.axis_size("freq")
    assert lax.axis_size("sub") == 2 and 2 * chan_rows == LANES
    level_count = delay_shifts.shape[0]
    width_count, tap_count = pulse_filters.shape
    tap_tiles = tap_count // LANES
    time_tiles = time_len // LANES
    far_levels = range(level_count - bits_of(group_count), level_count)
    near_reach = 2 ** far_levels[0] - 1
    near_len = rounded_up(near_reach, LANES)
    far_tiles = -(-(2**level_count - 1 - near_reach + tap_count) // LANES)

    in_vmem = pl.BlockSpec(memory_space=pltpu.VMEM)
    in_any = pl.BlockSpec(memory_space=pl.ANY)
    params = pltpu.CompilerParams(vmem_limit_bytes=VMEM_LIMIT)
    block_rows = chan_rows // group_count
    table = pltpu.VMEM((LANES, LANES), jnp.float32)

    def within_chip(operands, spans, raw_tiles, out_tiles, sending):
        state = pltpu.VMEM((raw_tiles + 1, chan_rows, LANES), jnp.float32)
        if sending:
            block = jax.ShapeDtypeStruct((time_tiles, block_rows, LANES), jnp.bfloat16)
            out_shape = [block] * group_count
        else:
            out_shape = [
                jax.ShapeDtypeStruct((out_tiles, chan_rows, LANES), jnp.float32),
                jax.ShapeDtypeStruct((LANES, LANES), jnp.float32),
            ]
        return pl.pallas_call(
            functools.partial(chip_kernel, spans, out_tiles, group_count if sending else 0),
            out_shape=out_shape,
            in_specs=[in_vmem] * len(operands),
            out_specs=[in_vmem] * len(out_shape),
            scratch_shapes=[pltpu.VMEM((raw_tiles + 1, 2 * chan_rows, LANES), jnp.float32), state, state]
            + ([] if sending else [table]),
            compiler_params=params,
        )(*operands)

    def between_chips(plan, blocks, halos, carried=()):
        state = pltpu.VMEM((plan.state_tiles, chan_rows, LANES), jnp.float32)
        operands = [columns, taps, *blocks, *halos, *carried]
        result = (chan_rows, plan.out_tiles * LANES)
        if plan.given:
            out_shape = [
                jax.ShapeDtypeStruct(result, jnp.float32),
                jax.ShapeDtypeStruct((tap_tiles, chan_rows, LANES), jnp.bfloat16),
            ]
            out_specs, scratch = [in_vmem] * 2, []
        else:
            out_shape, out_specs = [jax.ShapeDtypeStruct((chan_rows, time_len), jnp.float32)], [in_any]
            scratch = [pltpu.VMEM(result, jnp.float32), pltpu.SemaphoreType.DMA((len(plan.chunks) + 1,))]
        most = max(some for _, some in plan.chunks)
        scale = 1.0 / math.sqrt(delay_shifts.shape[1])
        return pl.pallas_call(
            functools.partial(trial_kernel, plan, group_count, level_count, scale),
            out_shape=out_shape,
            in_specs=[in_vmem] * len(operands),
            out_specs=out_specs,
            scratch_shapes=[
                state,
                state,
                pltpu.VMEM((plan.out_tiles + tap_tiles, chan_rows, LANES), jnp.bfloat16),
                pltpu.VMEM((most * chan_rows, width_count * LANES), jnp.float32),
            ]
            + scratch,
            compiler_params=params,
        )(*operands)

    other_core = from_partner(filterbank, "sub", 1)
    own, ahead = pl.pallas_call(
        load_kernel,
        out_shape=[
            jax.ShapeDtypeStruct(filterbank.shape, filterbank.dtype),
            jax.ShapeDtypeStruct((chan_rows, near_len), filterbank.dtype),
        ],
        in_specs=[in_vmem],
        out_specs=[in_vmem] * 2,
        compiler_params=params,
    )(filterbank)
    near_tiles = near_len // LANES
    early = time_tiles - near_tiles
    rows, delays = within_chip(
        [own, other_core, delay_shifts], [(0, time_len, 0)], time_tiles, early, False
    )
    both, spans = ([own], [other_core]), [(early * LANES, near_len, 0)]
    if lax.axis_size("tm") > 1:
        for crossed in range(2):
            both[crossed].append(from_ahead(ahead, 1, crossed))
        spans.append((0, near_len, 1))
    main = list(within_chip([*both[0], *both[1], rows, delays], spans, 2 * near_tiles, near_tiles, True))
    late_shifts, late_filters, main[0] = lax.optimization_barrier((delay_shifts, pulse_filters, main[0]))
    columns, taps = pl.pallas_call(
        functools.partial(table_kernel, group_count, block_rows),
        out_shape=[
            jax.ShapeDtypeStruct((LANES, LANES), jnp.float32),
            jax.ShapeDtypeStruct((width_count * LANES, tap_count + LANES), jnp.bfloat16),
        ],
        in_specs=[in_vmem] * 2,
        out_specs=[in_vmem] * 2,
        scratch_shapes=[table],
        compiler_params=params,
    )(late_shifts, late_filters)
    sent = main[-1]
    *main, last = exchanged(main)
    columns, taps, last = lax.optimization_barrier((columns, taps, last))
    main.append(last)

    halos, takes = [], []
    rest = far_tiles
    if lax.axis_size("tm") > 1:
        first_tiles = min(time_tiles, far_tiles)
        joined = pl.pallas_call(
            join_kernel,
            out_shape=jax.ShapeDtypeStruct(
                (first_tiles, chan_rows - block_rows, LANES), jnp.bfloat16
            ),
            in_specs=[in_vmem] * (group_count - 1),
            out_specs=in_vmem,
            scratch_shapes=[pltpu.VMEM((first_tiles, chan_rows - block_rows, LANES), jnp.float32)],
            compiler_params=params,
        )(*main[:-1])
        for hop in range(1, lax.axis_size("tm")):
            if rest > 0:
                takes.append(min(time_tiles, rest))
                halos.append(from_ahead(joined[: takes[-1]], hop, 0))
                halos.append(from_ahead_chip(sent[: takes[-1]], hop))
                rest -= takes[-1]
    lost = -(-sum(2**level for level in far_levels) // LANES) + tap_tiles
    early_tiles = time_tiles - lost
    if early_tiles <= 0:
        plan = Plan(time_tiles, takes, rest, 0, time_tiles, False, False, far_levels, tap_tiles)
        return between_chips(plan, main, halos)[0]
    plan = Plan(time_tiles, [], 0, 0, early_tiles, False, True, far_levels, tap_tiles)
    out, *carried = between_chips(plan, main, [])
    late_tiles = time_tiles - early_tiles
    plan = Plan(time_tiles, takes, rest, early_tiles, late_tiles, True, False, far_levels, tap_tiles)
    return between_chips(plan, main, halos, [*carried, out])[0]


def solution(mesh):
    in_specs = (P(("beams", "freq", "sub"), "tm"), P(), P())
    out_specs = P(("beams", "freq", "sub"), "tm")
    return jax.shard_map(local, mesh=mesh, in_specs=in_specs, out_specs=out_specs, check_vma=False)
```

```python
import functools
import math

import jax
import jax.numpy as jnp
from jax import lax
from jax.experimental import pallas as pl
from jax.experimental.pallas import tpu as pltpu
from jax.sharding import PartitionSpec as P

LANES = 128
SUBLANES = 8
PACKED = 16
LOG2_E = 1.4426950408889634
VMEM_LIMIT = 48 * 2**20


def rounded_up(value, unit):
    return -(-value // unit) * unit


def reversed_bits(value, bit_count):
    result = 0
    for bit_num in range(bit_count):
        result = result | (value >> bit_num & 1) << bit_count - 1 - bit_num
    return result


def bits_of(count):
    return count.bit_length() - 1


def from_ahead(value, steps, crossed):
    count, cores = lax.axis_size("tm"), lax.axis_size("sub")
    route = [
        ((block + steps) % count * cores + core, block * cores + (core ^ crossed))
        for block in range(count)
        for core in range(cores)
    ]
    return lax.ppermute(value, ("tm", "sub"), route)


def from_partner(value, axis, mask):
    count = lax.axis_size(axis)
    return lax.ppermute(value, axis, [(source, source ^ mask) for source in range(count)])


def mask_orders(group_count):
    order = [1, *range(group_count - 1, 1, -1)]
    return order, order[-1:] + order[:-1]


def step_masks(group_count, core):
    orders = mask_orders(group_count)
    return [0] + [jnp.where(core == 0, first, second) for first, second in zip(*orders)]


def exchanged(blocks):
    count = lax.axis_size("freq")
    received = [blocks[0]]
    for block, masks in zip(blocks[1:], zip(*mask_orders(count))):
        route = [
            (chip * 2 + core, (chip ^ masks[core]) * 2 + core) for chip in range(count) for core in range(2)
        ]
        received.append(lax.ppermute(block, ("freq", "sub"), route))
    return received


def lanes():
    return lax.broadcasted_iota(jnp.int32, (SUBLANES, LANES), 1)


def gathered(value, index):
    return jnp.take_along_axis(value, index, axis=1, mode="promise_in_bounds")


def transposed_table(rows, table, columns):
    for index, row in enumerate(rows):
        table[index : index + 1, :] = row.astype(jnp.float32)
    columns[...] = table[...].T


def merge(source, target, low, high, outs, tiles, most):
    lane = lanes()
    apart = max(most // LANES, 1)
    chosen = []
    for amount, place in outs:
        part = amount if most < LANES else amount & LANES - 1
        moved = (lane < part).astype(jnp.int32)
        if most >= LANES:
            moved = moved + (amount >> bits_of(LANES))
        masks = [moved == offset for offset in range(1, apart + 1)]
        chosen.append((masks, lane + part & LANES - 1, place))
    for masks, index, place in chosen:
        upper = [source[offset, high, :] for offset in range(apart)]
        for tile in range(tiles):
            upper.append(source[tile + apart, high, :])
            mixed = upper[0]
            for mask, other in zip(masks, upper[1:]):
                mixed = jnp.where(mask, other, mixed)
            target[tile, place, :] = source[tile, low, :] + gathered(mixed, index)
            upper = upper[1:]


def tree_levels(state, other, columns, first, levels, held, lengths, packed=False):
    rows = columns.shape[0] // 2
    source, target = state, other
    done = 0
    while done < len(levels):
        narrow = held < SUBLANES
        bits = min(bits_of(SUBLANES // held), len(levels) - done) if narrow else len(levels) - done
        for turn in range(bits):
            level = levels[done + turn]
            inner = turn + 1 < bits
            natural = turn == 0 and not (packed and done == 0)

            def rows_in(vector, start, stride):
                return pl.ds(start, SUBLANES, stride=stride) if natural else pl.ds(vector * SUBLANES, SUBLANES)

            def rows_out(vector, start, stride):
                return pl.ds(vector * SUBLANES, SUBLANES) if inner else pl.ds(start, SUBLANES, stride=stride)

            def amounts(start, stride):
                column = columns[pl.ds(start, SUBLANES, stride=stride), :]
                one = column[:, first + done + turn : first + done + turn + 1]
                return jnp.broadcast_to(one, (SUBLANES, LANES)).astype(jnp.int32)

            if narrow:
                now = held << turn
                for band in range(SUBLANES // (2 * now)):
                    for trial in range(now):
                        low, high = 2 * band * now + trial, (2 * band + 1) * now + trial
                        outs = [band * 2 * now + 2 * trial + odd for odd in range(2)]
                        merge(
                            source,
                            target,
                            rows_in(low, low, SUBLANES),
                            rows_in(high, high, SUBLANES),
                            [(amounts(out, SUBLANES), rows_out(out, out, SUBLANES)) for out in outs],
                            lengths[done + turn],
                            2**level,
                        )
            else:
                groups, split = held // SUBLANES, 2**turn
                for band in range(rows // (2 * held * split)):
                    for group in range(groups):
                        for place in range(split):
                            low, high = [
                                ((2 * band + upper) * groups + group) * split + place for upper in range(2)
                            ]
                            outs = []
                            for odd in range(2):
                                vector = (band * groups + group) * 2 * split + 2 * place + odd
                                start = (band * groups + group) * SUBLANES * 2 * split + 2 * place + odd
                                outs.append((amounts(start, 2 * split), rows_out(vector, start, 2 * split)))
                            merge(
                                source,
                                target,
                                rows_in(low, low * SUBLANES, 1),
                                rows_in(high, high * SUBLANES, 1),
                                outs,
                                lengths[done + turn],
                                2**level,
                            )
            source, target = target, source
        held <<= bits
        done += bits
    return source


def lengths_of(made, levels):
    return [made + -(-sum(2**later for later in levels if later > level) // LANES) for level in levels]


def load_kernel(whole, copied, ahead):
    copied[...] = whole[...]
    ahead[...] = whole[:, : ahead.shape[1]]


def placed(target, blocks, first, skip):
    chip, core = lax.axis_index("freq"), lax.axis_index("sub")
    tiles, rows = blocks[0].shape[:2]
    for mask, block in zip(step_masks(len(blocks), core), blocks):
        start = pl.multiple_of((chip ^ mask) * rows, rows)
        for tile in range(max(skip - first, 0), tiles):
            target[first + tile - skip, pl.ds(start, rows), :] = block[tile, :, :].astype(jnp.float32)


def join_kernel(group_count, *refs):
    *blocks, out, state = refs
    split, rows = blocks[0].shape[:2]
    for tile in range(out.shape[0]):
        for index in range(group_count):
            block = blocks[tile // split * group_count + index]
            state[tile, index * rows : (index + 1) * rows, :] = block[tile % split, :, :].astype(jnp.float32)
        out[tile, :, :] = state[tile, :, :].astype(jnp.bfloat16)


def chip_kernel(spans, out_tiles, group_count, tabled, *refs):
    pieces = (refs[: len(spans)], refs[len(spans) : 2 * len(spans)])
    given, *refs = refs[2 * len(spans) :]
    blocks, refs = refs[:group_count], refs[group_count:]
    chan_rows = pieces[0][0].shape[0]
    local_count = bits_of(chan_rows)
    chip, core = lax.axis_index("freq"), lax.axis_index("sub")
    if tabled:
        columns, (raw, ping, pong) = given, refs
    else:
        shifts, (columns, raw, ping, pong, table) = given, refs
        chunk = shifts[0:SUBLANES, pl.ds(pl.multiple_of(chip * LANES, LANES), LANES)]
        lane, level = lanes(), lax.broadcasted_iota(jnp.int32, (SUBLANES, LANES), 0)
        kept = lane & (1 << level) - 1
        picked = gathered(chunk, (2 * (lane - kept) + (core << level) + kept) & LANES - 1)
        transposed_table([picked[at : at + 1, :] for at in range(local_count + 1)], table, columns)
    for side in range(2):
        place = pl.multiple_of((core ^ side) * chan_rows, chan_rows)
        tile = 0
        for piece, (column, length, ahead) in zip(pieces[side], spans):
            there = lax.axis_index("tm") + ahead < lax.axis_size("tm")
            for start in range(column, column + length, LANES):
                part = piece[:, start : start + LANES].astype(jnp.float32)
                if ahead:
                    part = jnp.where(there, part, 0.0)
                raw[tile, pl.ds(place, chan_rows), :] = part
                tile += 1
        for later in range(tile, raw.shape[0] - 1):
            raw[later, pl.ds(place, chan_rows), :] = jnp.zeros((chan_rows, LANES), jnp.float32)
    levels = list(range(local_count + 1))
    lengths = lengths_of(out_tiles, levels)
    mask = lanes() >= core
    for vector in range(SUBLANES):
        low, high = [pl.ds(2 * vector + odd, SUBLANES, stride=2 * SUBLANES) for odd in range(2)]
        upper = raw[0, high, :]
        for tile in range(lengths[0]):
            later = raw[tile + 1, high, :]
            moved = pltpu.roll(jnp.where(mask, upper, later), LANES - core & LANES - 1, 1)
            ping[tile, pl.ds(vector * SUBLANES, SUBLANES), :] = raw[tile, low, :] + moved
            upper = later
    last = tree_levels(ping, pong, columns, 1, levels[1:], 1, lengths[1:], packed=True)
    size = chan_rows // group_count
    own = reversed_bits(chip, bits_of(group_count))
    for mask, block in zip(step_masks(group_count, core), blocks):
        start = pl.multiple_of((own ^ reversed_bits(mask, bits_of(group_count))) * size, size)
        for tile in range(out_tiles):
            block[tile, :, :] = last[tile, pl.ds(start, size), :].astype(jnp.bfloat16)


def toeplitz(filters, target):
    width_count, tap_count = filters.shape
    lane = lax.broadcasted_iota(jnp.int32, (LANES, LANES), 1)
    row = lax.broadcasted_iota(jnp.int32, (LANES, LANES), 0)
    taps = filters[...].astype(jnp.float32)
    zeros = jnp.zeros((LANES, LANES), jnp.float32)
    for width in range(width_count):
        before = zeros
        for start in range(0, tap_count + LANES, LANES):
            if start < tap_count:
                spread = jnp.broadcast_to(taps[width : width + 1, start : start + LANES], (LANES, LANES))
                rolled = pltpu.roll(spread, 0, 1, stride=1, stride_axis=0)
            else:
                rolled = zeros
            part = jnp.where(lane >= row, rolled, before)
            target[width * LANES : (width + 1) * LANES, start : start + LANES] = part.astype(jnp.bfloat16)
            before = rolled


def table_kernel(group_count, block_rows, shifts, filters, columns, taps, table):
    level_count = shifts.shape[0]
    chip, core = lax.axis_index("freq"), lax.axis_index("sub")
    own = reversed_bits(chip * 2 + core, bits_of(group_count) + 1)
    lane = lax.broadcasted_iota(jnp.int32, (1, LANES), 1)
    rows = []
    for section in range(bits_of(group_count)):
        level = level_count - bits_of(group_count) + section
        wide = block_rows * 2 ** (section + 1)
        row = jnp.zeros((1, LANES), jnp.int32)
        for subband in range(block_rows * group_count // wide):
            start = subband * 2 ** (level + 1) + own * wide
            tile = pl.multiple_of(start >> bits_of(LANES) << bits_of(LANES), LANES)
            chunk = shifts[level : level + 1, pl.ds(tile, LANES)]
            moved = pltpu.roll(chunk, subband * wide - (start & LANES - 1) & LANES - 1, 1)
            row = jnp.where(lane >= subband * wide, moved, row)
        rows.append(row)
    transposed_table(rows, table, columns)
    toeplitz(filters, taps)


def trial_kernel(plan, group_count, level_count, scale, columns, taps, *refs):
    parts = []
    for first in plan.parts:
        parts.append((first, refs[:group_count]))
        refs = refs[group_count:]
    halos, refs = refs[: len(plan.halos)], refs[len(plan.halos) :]
    if plan.taken:
        carried, so_far, refs = refs[0], refs[1], refs[2:]
    out, refs = refs[0], refs[1:]
    if plan.given:
        handed, refs = refs[0], refs[1:]
    state, other, normal, responses, *refs = refs
    if plan.given:
        result = out
    else:
        result, arrived = refs
    chan_rows = result.shape[0]
    block_rows = chan_rows // group_count
    width_count, kept = taps.shape[0] // LANES, taps.shape[1] // LANES - 1
    levels = list(range(level_count - bits_of(group_count), level_count))
    copies = []
    if plan.taken:
        place = out.at[:, pl.ds(0, plan.out_first * LANES)]
        copies.append(pltpu.make_async_copy(so_far, place, arrived.at[len(plan.chunks)]))
        copies[0].start()
    for first, blocks in parts:
        placed(state, blocks, first, plan.first)
    at = plan.main_tiles - plan.first
    chip, core = lax.axis_index("freq"), lax.axis_index("sub")
    for hop, tiles in enumerate(plan.halos, 1):
        there = lax.axis_index("tm") + hop < lax.axis_size("tm")
        for tile in range(tiles):
            joined = jnp.where(there, halos[hop - 1][tile, :, :].astype(jnp.float32), 0.0)
            for index, mask in enumerate(step_masks(group_count, core)):
                start = pl.multiple_of((chip ^ mask) * block_rows, block_rows)
                part = joined[index * block_rows : (index + 1) * block_rows]
                state[at, pl.ds(start, block_rows), :] = part
            at += 1
    for tile in range(at, at + plan.empty_tiles):
        state[tile, :, :] = jnp.zeros((chan_rows, LANES), jnp.float32)
    last = tree_levels(state, other, columns, 0, levels, block_rows, plan.lengths)
    head = kept if plan.taken else 0
    for tile in range(head):
        normal[tile, :, :] = carried[tile, :, :]
    for tile in range(plan.made):
        normal[head + tile, :, :] = (last[tile, :, :] * scale).astype(jnp.bfloat16)
    count = plan.out_tiles
    if plan.given:
        for tile in range(kept):
            handed[tile, :, :] = normal[count + tile, :, :]
    for turn, (first_tile, some) in enumerate(plan.chunks):
        size = some * chan_rows
        windows = [
            normal[first_tile + offset : first_tile + offset + some, :, :].reshape(size, LANES)
            for offset in range(kept + 1)
        ]
        responses[0:size, :] = lax.dot_general(
            jnp.concatenate(windows, axis=1),
            taps[...],
            (((1,), (1,)), ((), ())),
            preferred_element_type=jnp.float32,
        )
        for first_row in range(0, size, PACKED):
            energies = []
            for width in range(width_count):
                one = responses[first_row : first_row + PACKED, width * LANES : (width + 1) * LANES]
                energies.append((0.5 * LOG2_E) * one * one)
            highest = functools.reduce(jnp.maximum, energies)
            total = functools.reduce(jnp.add, [jnp.exp2(energy - highest) for energy in energies])
            tile, row = first_tile + first_row // chan_rows, first_row % chan_rows
            result[row : row + PACKED, tile * LANES : (tile + 1) * LANES] = (
                jnp.log2(total) + highest
            ) * (1.0 / LOG2_E)
        if plan.given:
            continue
        columns_now = pl.ds(first_tile * LANES, some * LANES)
        place = out.at[:, pl.ds((plan.out_first + first_tile) * LANES, some * LANES)]
        copies.append(pltpu.make_async_copy(result.at[:, columns_now], place, arrived.at[turn]))
        copies[-1].start()
    for copy in copies:
        copy.wait()


class Plan:
    def __init__(self, parts, main_tiles, halos, empty_tiles, out_first, out_tiles, taken, given, levels, tap_tiles):
        self.parts = parts
        self.main_tiles, self.halos, self.empty_tiles = main_tiles, halos, empty_tiles
        self.out_first, self.out_tiles = out_first, out_tiles
        self.taken, self.given = taken, given
        self.made = out_tiles if taken else out_tiles + tap_tiles
        self.first = out_first + tap_tiles if taken else 0
        self.lengths = lengths_of(self.made, levels)
        turns = -(-out_tiles // 6)
        ends = [out_tiles * turn // turns for turn in range(turns + 1)]
        self.chunks = [(start, end - start) for start, end in zip(ends, ends[1:])]
        self.state_tiles = main_tiles + sum(halos) + empty_tiles - self.first + max(2 ** levels[-1] // LANES, 1) + 1


def local(filterbank, delay_shifts, pulse_filters):
    chan_rows, time_len = filterbank.shape
    group_count = lax.axis_size("freq")
    assert lax.axis_size("sub") == 2 and 2 * chan_rows == LANES
    level_count = delay_shifts.shape[0]
    width_count, tap_count = pulse_filters.shape
    tap_tiles = tap_count // LANES
    time_tiles = time_len // LANES
    far_levels = range(level_count - bits_of(group_count), level_count)
    near_reach = 2 ** far_levels[0] - 1
    near_len = rounded_up(near_reach, LANES)
    far_tiles = -(-(2**level_count - 1 - near_reach + tap_count) // LANES)

    in_vmem = pl.BlockSpec(memory_space=pltpu.VMEM)
    in_any = pl.BlockSpec(memory_space=pl.ANY)
    params = pltpu.CompilerParams(vmem_limit_bytes=VMEM_LIMIT)
    block_rows = chan_rows // group_count
    table = pltpu.VMEM((LANES, LANES), jnp.float32)

    def within_chip(operands, spans, raw_tiles, out_tiles, tabled):
        state = pltpu.VMEM((raw_tiles + 1, chan_rows, LANES), jnp.float32)
        out_shape = [jax.ShapeDtypeStruct((out_tiles, block_rows, LANES), jnp.bfloat16)] * group_count
        if not tabled:
            out_shape.append(jax.ShapeDtypeStruct((LANES, LANES), jnp.float32))
        return pl.pallas_call(
            functools.partial(chip_kernel, spans, out_tiles, group_count, tabled),
            out_shape=out_shape,
            in_specs=[in_vmem] * len(operands),
            out_specs=[in_vmem] * len(out_shape),
            scratch_shapes=[pltpu.VMEM((raw_tiles + 1, 2 * chan_rows, LANES), jnp.float32), state, state]
            + ([] if tabled else [table]),
            compiler_params=params,
        )(*operands)

    def between_chips(plan, blocks, halos, carried=()):
        state = pltpu.VMEM((plan.state_tiles, chan_rows, LANES), jnp.float32)
        operands = [columns, taps, *blocks, *halos, *carried]
        result = (chan_rows, plan.out_tiles * LANES)
        if plan.given:
            out_shape = [
                jax.ShapeDtypeStruct(result, jnp.float32),
                jax.ShapeDtypeStruct((tap_tiles, chan_rows, LANES), jnp.bfloat16),
            ]
            out_specs, scratch = [in_vmem] * 2, []
        else:
            out_shape, out_specs = [jax.ShapeDtypeStruct((chan_rows, time_len), jnp.float32)], [in_any]
            scratch = [pltpu.VMEM(result, jnp.float32), pltpu.SemaphoreType.DMA((len(plan.chunks) + 1,))]
        most = max(some for _, some in plan.chunks)
        scale = 1.0 / math.sqrt(delay_shifts.shape[1])
        return pl.pallas_call(
            functools.partial(trial_kernel, plan, group_count, level_count, scale),
            out_shape=out_shape,
            in_specs=[in_vmem] * len(operands),
            out_specs=out_specs,
            scratch_shapes=[
                state,
                state,
                pltpu.VMEM((plan.out_tiles + tap_tiles, chan_rows, LANES), jnp.bfloat16),
                pltpu.VMEM((most * chan_rows, width_count * LANES), jnp.float32),
            ]
            + scratch,
            compiler_params=params,
        )(*operands)

    other_core = from_partner(filterbank, "sub", 1)
    own, ahead = pl.pallas_call(
        load_kernel,
        out_shape=[
            jax.ShapeDtypeStruct(filterbank.shape, filterbank.dtype),
            jax.ShapeDtypeStruct((chan_rows, near_len), filterbank.dtype),
        ],
        in_specs=[in_vmem],
        out_specs=[in_vmem] * 2,
        compiler_params=params,
    )(filterbank)
    near_tiles = near_len // LANES
    split = time_tiles * 5 // 8
    *front, delays = within_chip(
        [own, other_core, delay_shifts], [(0, (split + near_tiles) * LANES, 0)], split + near_tiles, split, False
    )
    front = exchanged(front)
    both, spans = ([own], [other_core]), [(split * LANES, time_len - split * LANES, 0)]
    if lax.axis_size("tm") > 1:
        for crossed in range(2):
            both[crossed].append(from_ahead(ahead, 1, crossed))
        spans.append((0, near_len, 1))
    back_tiles = time_tiles - split
    back = within_chip([*both[0], *both[1], delays], spans, back_tiles + near_tiles, back_tiles, True)
    back = list(back)
    late_shifts, late_filters, back[0] = lax.optimization_barrier((delay_shifts, pulse_filters, back[0]))
    front = list(lax.optimization_barrier((*front, back[0])))
    back[0] = front.pop()
    columns, taps = pl.pallas_call(
        functools.partial(table_kernel, group_count, block_rows),
        out_shape=[
            jax.ShapeDtypeStruct((LANES, LANES), jnp.float32),
            jax.ShapeDtypeStruct((width_count * LANES, tap_count + LANES), jnp.bfloat16),
        ],
        in_specs=[in_vmem] * 2,
        out_specs=[in_vmem] * 2,
        scratch_shapes=[table],
        compiler_params=params,
    )(late_shifts, late_filters)
    *back, last = exchanged(back)
    columns, taps, last = lax.optimization_barrier((columns, taps, last))
    back.append(last)

    halos, takes = [], []
    rest = far_tiles
    if lax.axis_size("tm") > 1:
        first_tiles = min(time_tiles, far_tiles)
        blocks = front if first_tiles <= split else front + back
        joined = pl.pallas_call(
            functools.partial(join_kernel, group_count),
            out_shape=jax.ShapeDtypeStruct((first_tiles, chan_rows, LANES), jnp.bfloat16),
            in_specs=[in_vmem] * len(blocks),
            out_specs=in_vmem,
            scratch_shapes=[pltpu.VMEM((first_tiles, chan_rows, LANES), jnp.float32)],
            compiler_params=params,
        )(*blocks)
        for hop in range(1, lax.axis_size("tm")):
            if rest > 0:
                takes.append(min(time_tiles, rest))
                halos.append(from_ahead(joined[: takes[-1]], hop, 0))
                rest -= takes[-1]
    lost = -(-sum(2**level for level in far_levels) // LANES) + tap_tiles
    early_tiles = time_tiles - lost
    if early_tiles <= 0:
        plan = Plan([0, split], time_tiles, takes, rest, 0, time_tiles, False, False, far_levels, tap_tiles)
        return between_chips(plan, front + back, halos)[0]
    plan = Plan([0, split], time_tiles, [], 0, 0, early_tiles, False, True, far_levels, tap_tiles)
    out, *carried = between_chips(plan, front + back, [])
    late_tiles = time_tiles - early_tiles
    parts, blocks = ([split], back) if early_tiles + tap_tiles >= split else ([0, split], front + back)
    plan = Plan(parts, time_tiles, takes, rest, early_tiles, late_tiles, True, False, far_levels, tap_tiles)
    return between_chips(plan, blocks, halos, [*carried, out])[0]


def solution(mesh):
    in_specs = (P(("beams", "freq", "sub"), "tm"), P(), P())
    out_specs = P(("beams", "freq", "sub"), "tm")
    return jax.shard_map(local, mesh=mesh, in_specs=in_specs, out_specs=out_specs, check_vma=False)
```

```python
import functools
import math

import jax
import jax.numpy as jnp
from jax import lax
from jax.experimental import pallas as pl
from jax.experimental.pallas import tpu as pltpu
from jax.sharding import PartitionSpec as P

LANES = 128
SUBLANES = 8
PACKED = 16
SHORT = 4
LOG2_E = 1.4426950408889634
VMEM_LIMIT = 48 * 2**20


def rounded_up(value, unit):
    return -(-value // unit) * unit


def reversed_bits(value, bit_count):
    result = 0
    for bit_num in range(bit_count):
        result = result | (value >> bit_num & 1) << bit_count - 1 - bit_num
    return result


def bits_of(count):
    return count.bit_length() - 1


def from_ahead(value, steps, crossed):
    count, cores = lax.axis_size("tm"), lax.axis_size("sub")
    route = [
        ((block + steps) % count * cores + core, block * cores + (core ^ crossed))
        for block in range(count)
        for core in range(cores)
    ]
    return lax.ppermute(value, ("tm", "sub"), route)


def from_partner(value, axis, mask):
    count = lax.axis_size(axis)
    return lax.ppermute(value, axis, [(source, source ^ mask) for source in range(count)])


def mask_orders(group_count):
    order = [1, *range(group_count - 1, 1, -1)]
    return order, order[-1:] + order[:-1]


def step_masks(group_count, core):
    orders = mask_orders(group_count)
    return [0] + [jnp.where(core == 0, first, second) for first, second in zip(*orders)]


def exchanged(blocks):
    count = lax.axis_size("freq")
    received = [blocks[0]]
    for block, masks in zip(blocks[1:], zip(*mask_orders(count))):
        route = [
            (chip * 2 + core, (chip ^ masks[core]) * 2 + core) for chip in range(count) for core in range(2)
        ]
        received.append(lax.ppermute(block, ("freq", "sub"), route))
    return received


def lanes():
    return lax.broadcasted_iota(jnp.int32, (SUBLANES, LANES), 1)


def gathered(value, index):
    return jnp.take_along_axis(value, index, axis=1, mode="promise_in_bounds")


def transposed_table(rows, table, columns):
    for index, row in enumerate(rows):
        table[index : index + 1, :] = row.astype(jnp.float32)
    columns[...] = table[...].T


def merge_short(source, target, low, high, outs, tiles, most):
    inside = [lanes() < LANES - delay for delay in range(1, most + 1)]
    chosen = [([amount == delay for delay in range(1, most + 1)], place) for amount, place in outs]

    def rolled(tile):
        value = source[tile, high, :]
        return value, [pltpu.roll(value, LANES - delay, 1) for delay in range(1, most + 1)]

    now = rolled(0)
    for tile in range(tiles):
        later = rolled(tile + 1)
        copies = [jnp.where(*parts) for parts in zip(inside, now[1], later[1])]
        lower = source[tile, low, :]
        for masks, place in chosen:
            moved = now[0]
            for mask, copy in zip(masks, copies):
                moved = jnp.where(mask, copy, moved)
            target[tile, place, :] = lower + moved
        now = later


def merge(source, target, low, high, outs, tiles, most):
    if most <= SHORT:
        return merge_short(source, target, low, high, outs, tiles, most)
    lane = lanes()
    apart = max(most // LANES, 1)
    chosen = []
    for amount, place in outs:
        part = amount if most < LANES else amount & LANES - 1
        moved = (lane < part).astype(jnp.int32)
        if most >= LANES:
            moved = moved + (amount >> bits_of(LANES))
        masks = [moved == offset for offset in range(1, apart + 1)]
        chosen.append((masks, lane + part & LANES - 1, place))
    for masks, index, place in chosen:
        upper = [source[offset, high, :] for offset in range(apart)]
        for tile in range(tiles):
            upper.append(source[tile + apart, high, :])
            mixed = upper[0]
            for mask, other in zip(masks, upper[1:]):
                mixed = jnp.where(mask, other, mixed)
            target[tile, place, :] = source[tile, low, :] + gathered(mixed, index)
            upper = upper[1:]


def tree_levels(state, other, columns, first, levels, held, lengths, packed=False):
    rows = columns.shape[0] // 2
    source, target = state, other
    done = 0
    while done < len(levels):
        narrow = held < SUBLANES
        bits = min(bits_of(SUBLANES // held), len(levels) - done) if narrow else len(levels) - done
        for turn in range(bits):
            level = levels[done + turn]
            inner = turn + 1 < bits
            natural = turn == 0 and not (packed and done == 0)

            def rows_in(vector, start, stride):
                return pl.ds(start, SUBLANES, stride=stride) if natural else pl.ds(vector * SUBLANES, SUBLANES)

            def rows_out(vector, start, stride):
                return pl.ds(vector * SUBLANES, SUBLANES) if inner else pl.ds(start, SUBLANES, stride=stride)

            def amounts(start, stride):
                column = columns[pl.ds(start, SUBLANES, stride=stride), :]
                one = column[:, first + done + turn : first + done + turn + 1]
                return jnp.broadcast_to(one, (SUBLANES, LANES)).astype(jnp.int32)

            if narrow:
                now = held << turn
                for band in range(SUBLANES // (2 * now)):
                    for trial in range(now):
                        low, high = 2 * band * now + trial, (2 * band + 1) * now + trial
                        outs = [band * 2 * now + 2 * trial + odd for odd in range(2)]
                        merge(
                            source,
                            target,
                            rows_in(low, low, SUBLANES),
                            rows_in(high, high, SUBLANES),
                            [(amounts(out, SUBLANES), rows_out(out, out, SUBLANES)) for out in outs],
                            lengths[done + turn],
                            2**level,
                        )
            else:
                groups, split = held // SUBLANES, 2**turn
                for band in range(rows // (2 * held * split)):
                    for group in range(groups):
                        for place in range(split):
                            low, high = [
                                ((2 * band + upper) * groups + group) * split + place for upper in range(2)
                            ]
                            outs = []
                            for odd in range(2):
                                vector = (band * groups + group) * 2 * split + 2 * place + odd
                                start = (band * groups + group) * SUBLANES * 2 * split + 2 * place + odd
                                outs.append((amounts(start, 2 * split), rows_out(vector, start, 2 * split)))
                            merge(
                                source,
                                target,
                                rows_in(low, low * SUBLANES, 1),
                                rows_in(high, high * SUBLANES, 1),
                                outs,
                                lengths[done + turn],
                                2**level,
                            )
            source, target = target, source
        held <<= bits
        done += bits
    return source


def lengths_of(made, levels):
    return [made + -(-sum(2**later for later in levels if later > level) // LANES) for level in levels]


def load_kernel(whole, copied, ahead):
    copied[...] = whole[...]
    ahead[...] = whole[:, : ahead.shape[1]]


def placed(target, blocks, tiles, skip):
    chip, core = lax.axis_index("freq"), lax.axis_index("sub")
    rows = blocks[0].shape[1]
    for mask, block in zip(step_masks(len(blocks), core), blocks):
        start = pl.multiple_of((chip ^ mask) * rows, rows)
        for tile in range(skip, tiles):
            target[tile - skip, pl.ds(start, rows), :] = block[tile, :, :].astype(jnp.float32)


def join_kernel(*refs):
    *blocks, out, state = refs
    rows = blocks[0].shape[1]
    for tile in range(out.shape[0]):
        for index, block in enumerate(blocks):
            state[tile, index * rows : (index + 1) * rows, :] = block[tile, :, :].astype(jnp.float32)
        out[tile, :, :] = state[tile, :, :].astype(jnp.bfloat16)


def chip_kernel(spans, out_tiles, group_count, *refs):
    pieces = (refs[: len(spans)], refs[len(spans) : 2 * len(spans)])
    refs = refs[2 * len(spans) :]
    chan_rows = pieces[0][0].shape[0]
    local_count = bits_of(chan_rows)
    chip, core = lax.axis_index("freq"), lax.axis_index("sub")
    if group_count:
        (earlier, columns), blocks, (raw, ping, pong) = refs[:2], refs[2:-3], refs[-3:]
    else:
        shifts, rows, columns, raw, ping, pong, table = refs
        chunk = shifts[0:SUBLANES, pl.ds(pl.multiple_of(chip * LANES, LANES), LANES)]
        lane, level = lanes(), lax.broadcasted_iota(jnp.int32, (SUBLANES, LANES), 0)
        kept = lane & (1 << level) - 1
        picked = gathered(chunk, (2 * (lane - kept) + (core << level) + kept) & LANES - 1)
        transposed_table([picked[at : at + 1, :] for at in range(local_count + 1)], table, columns)
    for side in range(2):
        place = pl.multiple_of((core ^ side) * chan_rows, chan_rows)
        tile = 0
        for piece, (column, length, ahead) in zip(pieces[side], spans):
            there = lax.axis_index("tm") + ahead < lax.axis_size("tm")
            for start in range(column, column + length, LANES):
                part = piece[:, start : start + LANES].astype(jnp.float32)
                if ahead:
                    part = jnp.where(there, part, 0.0)
                raw[tile, pl.ds(place, chan_rows), :] = part
                tile += 1
        for later in range(tile, raw.shape[0] - 1):
            raw[later, pl.ds(place, chan_rows), :] = jnp.zeros((chan_rows, LANES), jnp.float32)
    levels = list(range(local_count + 1))
    lengths = lengths_of(out_tiles, levels)
    mask = lanes() >= core
    for vector in range(SUBLANES):
        low, high = [pl.ds(2 * vector + odd, SUBLANES, stride=2 * SUBLANES) for odd in range(2)]
        upper = raw[0, high, :]
        for tile in range(lengths[0]):
            later = raw[tile + 1, high, :]
            moved = pltpu.roll(jnp.where(mask, upper, later), LANES - core & LANES - 1, 1)
            ping[tile, pl.ds(vector * SUBLANES, SUBLANES), :] = raw[tile, low, :] + moved
            upper = later
    last = tree_levels(ping, pong, columns, 1, levels[1:], 1, lengths[1:], packed=True)
    if not group_count:
        for tile in range(out_tiles):
            rows[tile, :, :] = last[tile, :, :]
        return
    size = chan_rows // group_count
    own = reversed_bits(chip, bits_of(group_count))
    first = earlier.shape[0]
    for mask, block in zip(step_masks(group_count, core), blocks):
        start = pl.multiple_of((own ^ reversed_bits(mask, bits_of(group_count))) * size, size)
        for tile in range(first):
            block[tile, :, :] = earlier[tile, pl.ds(start, size), :].astype(jnp.bfloat16)
        for tile in range(out_tiles):
            block[first + tile, :, :] = last[tile, pl.ds(start, size), :].astype(jnp.bfloat16)


def toeplitz(filters, target):
    width_count, tap_count = filters.shape
    lane = lax.broadcasted_iota(jnp.int32, (LANES, LANES), 1)
    row = lax.broadcasted_iota(jnp.int32, (LANES, LANES), 0)
    taps = filters[...].astype(jnp.float32)
    zeros = jnp.zeros((LANES, LANES), jnp.float32)
    for width in range(width_count):
        before = zeros
        for start in range(0, tap_count + LANES, LANES):
            if start < tap_count:
                spread = jnp.broadcast_to(taps[width : width + 1, start : start + LANES], (LANES, LANES))
                rolled = pltpu.roll(spread, 0, 1, stride=1, stride_axis=0)
            else:
                rolled = zeros
            part = jnp.where(lane >= row, rolled, before)
            target[width * LANES : (width + 1) * LANES, start : start + LANES] = part.astype(jnp.bfloat16)
            before = rolled


def table_kernel(group_count, block_rows, shifts, filters, columns, taps, table):
    level_count = shifts.shape[0]
    chip, core = lax.axis_index("freq"), lax.axis_index("sub")
    own = reversed_bits(chip * 2 + core, bits_of(group_count) + 1)
    lane = lax.broadcasted_iota(jnp.int32, (1, LANES), 1)
    rows = []
    for section in range(bits_of(group_count)):
        level = level_count - bits_of(group_count) + section
        wide = block_rows * 2 ** (section + 1)
        row = jnp.zeros((1, LANES), jnp.int32)
        for subband in range(block_rows * group_count // wide):
            start = subband * 2 ** (level + 1) + own * wide
            tile = pl.multiple_of(start >> bits_of(LANES) << bits_of(LANES), LANES)
            chunk = shifts[level : level + 1, pl.ds(tile, LANES)]
            moved = pltpu.roll(chunk, subband * wide - (start & LANES - 1) & LANES - 1, 1)
            row = jnp.where(lane >= subband * wide, moved, row)
        rows.append(row)
    transposed_table(rows, table, columns)
    toeplitz(filters, taps)


def trial_kernel(plan, group_count, level_count, scale, columns, taps, *refs):
    blocks, refs = refs[:group_count], refs[group_count:]
    halos, refs = refs[: 2 * len(plan.halos)], refs[2 * len(plan.halos) :]
    if plan.taken:
        carried, so_far, refs = refs[0], refs[1], refs[2:]
    out, refs = refs[0], refs[1:]
    if plan.given:
        handed, refs = refs[0], refs[1:]
    state, other, normal, responses, *refs = refs
    if plan.given:
        result = out
    else:
        result, arrived = refs
    chan_rows = result.shape[0]
    block_rows = chan_rows // group_count
    width_count, kept = taps.shape[0] // LANES, taps.shape[1] // LANES - 1
    levels = list(range(level_count - bits_of(group_count), level_count))
    copies = []
    if plan.taken:
        place = out.at[:, pl.ds(0, plan.out_first * LANES)]
        copies.append(pltpu.make_async_copy(so_far, place, arrived.at[len(plan.chunks)]))
        copies[0].start()
    placed(state, blocks, plan.main_tiles, plan.first)
    at = plan.main_tiles - plan.first
    chip, core = lax.axis_index("freq"), lax.axis_index("sub")
    for hop, tiles in enumerate(plan.halos, 1):
        there = lax.axis_index("tm") + hop < lax.axis_size("tm")
        for tile in range(tiles):
            joined, single = [
                jnp.where(there, halo[tile, :, :].astype(jnp.float32), 0.0)
                for halo in halos[2 * hop - 2 : 2 * hop]
            ]
            for index, mask in enumerate(step_masks(group_count, core)):
                start = pl.multiple_of((chip ^ mask) * block_rows, block_rows)
                if index + 1 < group_count:
                    part = joined[index * block_rows : (index + 1) * block_rows]
                else:
                    part = single
                state[at, pl.ds(start, block_rows), :] = part
            at += 1
    for tile in range(at, at + plan.empty_tiles):
        state[tile, :, :] = jnp.zeros((chan_rows, LANES), jnp.float32)
    last = tree_levels(state, other, columns, 0, levels, block_rows, plan.lengths)
    head = kept if plan.taken else 0
    for tile in range(head):
        normal[tile, :, :] = carried[tile, :, :]
    for tile in range(plan.made):
        normal[head + tile, :, :] = (last[tile, :, :] * scale).astype(jnp.bfloat16)
    count = plan.out_tiles
    if plan.given:
        for tile in range(kept):
            handed[tile, :, :] = normal[count + tile, :, :]
    for turn, (first_tile, some) in enumerate(plan.chunks):
        size = some * chan_rows
        windows = [
            normal[first_tile + offset : first_tile + offset + some, :, :].reshape(size, LANES)
            for offset in range(kept + 1)
        ]
        responses[0:size, :] = lax.dot_general(
            jnp.concatenate(windows, axis=1),
            taps[...],
            (((1,), (1,)), ((), ())),
            preferred_element_type=jnp.float32,
        )
        for first_row in range(0, size, PACKED):
            energies = []
            for width in range(width_count):
                one = responses[first_row : first_row + PACKED, width * LANES : (width + 1) * LANES]
                energies.append((0.5 * LOG2_E) * one * one)
            highest = functools.reduce(jnp.maximum, energies)
            total = functools.reduce(jnp.add, [jnp.exp2(energy - highest) for energy in energies])
            tile, row = first_tile + first_row // chan_rows, first_row % chan_rows
            result[row : row + PACKED, tile * LANES : (tile + 1) * LANES] = (
                jnp.log2(total) + highest
            ) * (1.0 / LOG2_E)
        if plan.given:
            continue
        columns_now = pl.ds(first_tile * LANES, some * LANES)
        place = out.at[:, pl.ds((plan.out_first + first_tile) * LANES, some * LANES)]
        copies.append(pltpu.make_async_copy(result.at[:, columns_now], place, arrived.at[turn]))
        copies[-1].start()
    for copy in copies:
        copy.wait()


class Plan:
    def __init__(self, main_tiles, halos, empty_tiles, out_first, out_tiles, taken, given, levels, tap_tiles):
        self.main_tiles, self.halos, self.empty_tiles = main_tiles, halos, empty_tiles
        self.out_first, self.out_tiles = out_first, out_tiles
        self.taken, self.given = taken, given
        self.made = out_tiles if taken else out_tiles + tap_tiles
        self.first = out_first + tap_tiles if taken else 0
        self.lengths = lengths_of(self.made, levels)
        turns = -(-out_tiles // 6)
        ends = [out_tiles * turn // turns for turn in range(turns + 1)]
        self.chunks = [(start, end - start) for start, end in zip(ends, ends[1:])]
        self.state_tiles = main_tiles + sum(halos) + empty_tiles - self.first + max(2 ** levels[-1] // LANES, 1) + 1


def local(filterbank, delay_shifts, pulse_filters):
    chan_rows, time_len = filterbank.shape
    group_count = lax.axis_size("freq")
    assert lax.axis_size("sub") == 2 and 2 * chan_rows == LANES
    level_count = delay_shifts.shape[0]
    width_count, tap_count = pulse_filters.shape
    tap_tiles = tap_count // LANES
    time_tiles = time_len // LANES
    far_levels = range(level_count - bits_of(group_count), level_count)
    near_reach = 2 ** far_levels[0] - 1
    near_len = rounded_up(near_reach, LANES)
    far_tiles = -(-(2**level_count - 1 - near_reach + tap_count) // LANES)

    in_vmem = pl.BlockSpec(memory_space=pltpu.VMEM)
    in_any = pl.BlockSpec(memory_space=pl.ANY)
    params = pltpu.CompilerParams(vmem_limit_bytes=VMEM_LIMIT)
    block_rows = chan_rows // group_count
    table = pltpu.VMEM((LANES, LANES), jnp.float32)

    def within_chip(operands, spans, raw_tiles, out_tiles, sending):
        state = pltpu.VMEM((raw_tiles + 1, chan_rows, LANES), jnp.float32)
        if sending:
            block = jax.ShapeDtypeStruct((time_tiles, block_rows, LANES), jnp.bfloat16)
            out_shape = [block] * group_count
        else:
            out_shape = [
                jax.ShapeDtypeStruct((out_tiles, chan_rows, LANES), jnp.float32),
                jax.ShapeDtypeStruct((LANES, LANES), jnp.float32),
            ]
        return pl.pallas_call(
            functools.partial(chip_kernel, spans, out_tiles, group_count if sending else 0),
            out_shape=out_shape,
            in_specs=[in_vmem] * len(operands),
            out_specs=[in_vmem] * len(out_shape),
            scratch_shapes=[pltpu.VMEM((raw_tiles + 1, 2 * chan_rows, LANES), jnp.float32), state, state]
            + ([] if sending else [table]),
            compiler_params=params,
        )(*operands)

    def between_chips(plan, blocks, halos, carried=()):
        state = pltpu.VMEM((plan.state_tiles, chan_rows, LANES), jnp.float32)
        operands = [columns, taps, *blocks, *halos, *carried]
        result = (chan_rows, plan.out_tiles * LANES)
        if plan.given:
            out_shape = [
                jax.ShapeDtypeStruct(result, jnp.float32),
                jax.ShapeDtypeStruct((tap_tiles, chan_rows, LANES), jnp.bfloat16),
            ]
            out_specs, scratch = [in_vmem] * 2, []
        else:
            out_shape, out_specs = [jax.ShapeDtypeStruct((chan_rows, time_len), jnp.float32)], [in_any]
            scratch = [pltpu.VMEM(result, jnp.float32), pltpu.SemaphoreType.DMA((len(plan.chunks) + 1,))]
        most = max(some for _, some in plan.chunks)
        scale = 1.0 / math.sqrt(delay_shifts.shape[1])
        return pl.pallas_call(
            functools.partial(trial_kernel, plan, group_count, level_count, scale),
            out_shape=out_shape,
            in_specs=[in_vmem] * len(operands),
            out_specs=out_specs,
            scratch_shapes=[
                state,
                state,
                pltpu.VMEM((plan.out_tiles + tap_tiles, chan_rows, LANES), jnp.bfloat16),
                pltpu.VMEM((most * chan_rows, width_count * LANES), jnp.float32),
            ]
            + scratch,
            compiler_params=params,
        )(*operands)

    other_core = from_partner(filterbank, "sub", 1)
    own, ahead = pl.pallas_call(
        load_kernel,
        out_shape=[
            jax.ShapeDtypeStruct(filterbank.shape, filterbank.dtype),
            jax.ShapeDtypeStruct((chan_rows, near_len), filterbank.dtype),
        ],
        in_specs=[in_vmem],
        out_specs=[in_vmem] * 2,
        compiler_params=params,
    )(filterbank)
    near_tiles = near_len // LANES
    early = time_tiles - near_tiles
    rows, delays = within_chip(
        [own, other_core, delay_shifts], [(0, time_len, 0)], time_tiles, early, False
    )
    both, spans = ([own], [other_core]), [(early * LANES, near_len, 0)]
    if lax.axis_size("tm") > 1:
        for crossed in range(2):
            both[crossed].append(from_ahead(ahead, 1, crossed))
        spans.append((0, near_len, 1))
    main = list(within_chip([*both[0], *both[1], rows, delays], spans, 2 * near_tiles, near_tiles, True))
    late_shifts, late_filters, main[0] = lax.optimization_barrier((delay_shifts, pulse_filters, main[0]))
    columns, taps = pl.pallas_call(
        functools.partial(table_kernel, group_count, block_rows),
        out_shape=[
            jax.ShapeDtypeStruct((LANES, LANES), jnp.float32),
            jax.ShapeDtypeStruct((width_count * LANES, tap_count + LANES), jnp.bfloat16),
        ],
        in_specs=[in_vmem] * 2,
        out_specs=[in_vmem] * 2,
        scratch_shapes=[table],
        compiler_params=params,
    )(late_shifts, late_filters)
    *main, last = exchanged(main)
    columns, taps, last = lax.optimization_barrier((columns, taps, last))
    main.append(last)

    halos, takes = [], []
    rest = far_tiles
    if lax.axis_size("tm") > 1:
        first_tiles = min(time_tiles, far_tiles)
        joined = pl.pallas_call(
            join_kernel,
            out_shape=jax.ShapeDtypeStruct(
                (first_tiles, chan_rows - block_rows, LANES), jnp.bfloat16
            ),
            in_specs=[in_vmem] * (group_count - 1),
            out_specs=in_vmem,
            scratch_shapes=[pltpu.VMEM((first_tiles, chan_rows - block_rows, LANES), jnp.float32)],
            compiler_params=params,
        )(*main[:-1])
        for hop in range(1, lax.axis_size("tm")):
            if rest > 0:
                takes.append(min(time_tiles, rest))
                halos.append(from_ahead(joined[: takes[-1]], hop, 0))
                halos.append(from_ahead(main[-1][: takes[-1]], hop, 0))
                rest -= takes[-1]
    lost = -(-sum(2**level for level in far_levels) // LANES) + tap_tiles
    early_tiles = time_tiles - lost
    if early_tiles <= 0:
        plan = Plan(time_tiles, takes, rest, 0, time_tiles, False, False, far_levels, tap_tiles)
        return between_chips(plan, main, halos)[0]
    plan = Plan(time_tiles, [], 0, 0, early_tiles, False, True, far_levels, tap_tiles)
    out, *carried = between_chips(plan, main, [])
    late_tiles = time_tiles - early_tiles
    plan = Plan(time_tiles, takes, rest, early_tiles, late_tiles, True, False, far_levels, tap_tiles)
    return between_chips(plan, main, halos, [*carried, out])[0]


def solution(mesh):
    in_specs = (P(("beams", "freq", "sub"), "tm"), P(), P())
    out_specs = P(("beams", "freq", "sub"), "tm")
    return jax.shard_map(local, mesh=mesh, in_specs=in_specs, out_specs=out_specs, check_vma=False)
```

```python
import functools
import math

import jax
import jax.numpy as jnp
from jax import lax
from jax.experimental import pallas as pl
from jax.experimental.pallas import tpu as pltpu
from jax.sharding import PartitionSpec as P

LANES = 128
SUBLANES = 8
PACKED = 16
SHORT = 4
LOG2_E = 1.4426950408889634
VMEM_LIMIT = 48 * 2**20


def rounded_up(value, unit):
    return -(-value // unit) * unit


def reversed_bits(value, bit_count):
    result = 0
    for bit_num in range(bit_count):
        result = result | (value >> bit_num & 1) << bit_count - 1 - bit_num
    return result


def bits_of(count):
    return count.bit_length() - 1


def from_ahead(value, steps):
    count = lax.axis_size("tm")
    return lax.ppermute(value, "tm", [((block + steps) % count, block) for block in range(count)])


def from_partner(value, axis, mask):
    count = lax.axis_size(axis)
    return lax.ppermute(value, axis, [(source, source ^ mask) for source in range(count)])


def mask_orders(group_count):
    far = list(range(group_count - 1, 1, -1))
    return [1, *far], far[-1:] + far[:-1] + [1]


def step_masks(group_count, core):
    orders = mask_orders(group_count)
    return [0] + [jnp.where(core == 0, first, second) for first, second in zip(*orders)]


def exchanged(blocks):
    count = lax.axis_size("freq")
    received = [blocks[0]]
    for block, masks in zip(blocks[1:], zip(*mask_orders(count))):
        route = [
            (chip * 2 + core, (chip ^ masks[core]) * 2 + core) for chip in range(count) for core in range(2)
        ]
        received.append(lax.ppermute(block, ("freq", "sub"), route))
    return received


def lanes():
    return lax.broadcasted_iota(jnp.int32, (SUBLANES, LANES), 1)


def gathered(value, index):
    return jnp.take_along_axis(value, index, axis=1, mode="promise_in_bounds")


def transposed_table(rows, table, columns):
    for index, row in enumerate(rows):
        table[index : index + 1, :] = row.astype(jnp.float32)
    columns[...] = table[...].T


def merge_short(source, target, low, high, outs, tiles, most):
    inside = [lanes() < LANES - delay for delay in range(1, most + 1)]
    chosen = [([amount == delay for delay in range(1, most + 1)], place) for amount, place in outs]

    def rolled(tile):
        value = source[tile, high, :]
        return value, [pltpu.roll(value, LANES - delay, 1) for delay in range(1, most + 1)]

    now = rolled(0)
    for tile in range(tiles):
        later = rolled(tile + 1)
        copies = [jnp.where(*parts) for parts in zip(inside, now[1], later[1])]
        lower = source[tile, low, :]
        for masks, place in chosen:
            moved = now[0]
            for mask, copy in zip(masks, copies):
                moved = jnp.where(mask, copy, moved)
            target[tile, place, :] = lower + moved
        now = later


def merge(source, target, low, high, outs, tiles, most):
    if most <= SHORT:
        return merge_short(source, target, low, high, outs, tiles, most)
    lane = lanes()
    apart = max(most // LANES, 1)
    chosen = []
    for amount, place in outs:
        part = amount if most < LANES else amount & LANES - 1
        moved = (lane < part).astype(jnp.int32)
        if most >= LANES:
            moved = moved + (amount >> bits_of(LANES))
        masks = [moved == offset for offset in range(1, apart + 1)]
        chosen.append((masks, lane + part & LANES - 1, place))
    for masks, index, place in chosen:
        upper = [source[offset, high, :] for offset in range(apart)]
        for tile in range(tiles):
            upper.append(source[tile + apart, high, :])
            mixed = upper[0]
            for mask, other in zip(masks, upper[1:]):
                mixed = jnp.where(mask, other, mixed)
            target[tile, place, :] = source[tile, low, :] + gathered(mixed, index)
            upper = upper[1:]


def tree_levels(state, other, columns, first, levels, held, lengths, packed=False):
    rows = columns.shape[0] // 2
    source, target = state, other
    done = 0
    while done < len(levels):
        narrow = held < SUBLANES
        bits = min(bits_of(SUBLANES // held), len(levels) - done) if narrow else len(levels) - done
        for turn in range(bits):
            level = levels[done + turn]
            inner = turn + 1 < bits
            natural = turn == 0 and not (packed and done == 0)

            def rows_in(vector, start, stride):
                return pl.ds(start, SUBLANES, stride=stride) if natural else pl.ds(vector * SUBLANES, SUBLANES)

            def rows_out(vector, start, stride):
                return pl.ds(vector * SUBLANES, SUBLANES) if inner else pl.ds(start, SUBLANES, stride=stride)

            def amounts(start, stride):
                column = columns[pl.ds(start, SUBLANES, stride=stride), :]
                one = column[:, first + done + turn : first + done + turn + 1]
                return jnp.broadcast_to(one, (SUBLANES, LANES)).astype(jnp.int32)

            if narrow:
                now = held << turn
                for band in range(SUBLANES // (2 * now)):
                    for trial in range(now):
                        low, high = 2 * band * now + trial, (2 * band + 1) * now + trial
                        outs = [band * 2 * now + 2 * trial + odd for odd in range(2)]
                        merge(
                            source,
                            target,
                            rows_in(low, low, SUBLANES),
                            rows_in(high, high, SUBLANES),
                            [(amounts(out, SUBLANES), rows_out(out, out, SUBLANES)) for out in outs],
                            lengths[done + turn],
                            2**level,
                        )
            else:
                groups, split = held // SUBLANES, 2**turn
                for band in range(rows // (2 * held * split)):
                    for group in range(groups):
                        for place in range(split):
                            low, high = [
                                ((2 * band + upper) * groups + group) * split + place for upper in range(2)
                            ]
                            outs = []
                            for odd in range(2):
                                vector = (band * groups + group) * 2 * split + 2 * place + odd
                                start = (band * groups + group) * SUBLANES * 2 * split + 2 * place + odd
                                outs.append((amounts(start, 2 * split), rows_out(vector, start, 2 * split)))
                            merge(
                                source,
                                target,
                                rows_in(low, low * SUBLANES, 1),
                                rows_in(high, high * SUBLANES, 1),
                                outs,
                                lengths[done + turn],
                                2**level,
                            )
            source, target = target, source
        held <<= bits
        done += bits
    return source


def lengths_of(made, levels):
    return [made + -(-sum(2**later for later in levels if later > level) // LANES) for level in levels]


def load_kernel(whole, copied):
    copied[...] = whole[...]


def start_kernel(whole, other, ahead):
    rows, length = whole.shape[0], ahead.shape[1]
    ahead[:rows, :] = whole[:, :length]
    ahead[rows:, :] = other[:, :length]


def placed(target, blocks, tiles, skip):
    chip, core = lax.axis_index("freq"), lax.axis_index("sub")
    rows = blocks[0].shape[1]
    for mask, block in zip(step_masks(len(blocks), core), blocks):
        start = pl.multiple_of((chip ^ mask) * rows, rows)
        for tile in range(skip, tiles):
            target[tile - skip, pl.ds(start, rows), :] = block[tile, :, :].astype(jnp.float32)


def join_kernel(*refs):
    *blocks, out, state = refs
    rows = blocks[0].shape[1]
    for tile in range(out.shape[0]):
        for index, block in enumerate(blocks):
            state[tile, index * rows : (index + 1) * rows, :] = block[tile, :, :].astype(jnp.float32)
        out[tile, :, :] = state[tile, :, :].astype(jnp.bfloat16)


def chip_kernel(spans, out_tiles, group_count, *refs):
    chan_rows = refs[0].shape[0]
    pieces = [[(refs[side], 0)] + [(ref, side * chan_rows) for ref in refs[2 : len(spans) + 1]] for side in range(2)]
    refs = refs[len(spans) + 1 :]
    local_count = bits_of(chan_rows)
    chip, core = lax.axis_index("freq"), lax.axis_index("sub")
    if group_count:
        (earlier, columns), blocks, (raw, ping, pong) = refs[:2], refs[2:-3], refs[-3:]
    else:
        shifts, rows, columns, raw, ping, pong, table = refs
        chunk = shifts[0:SUBLANES, pl.ds(pl.multiple_of(chip * LANES, LANES), LANES)]
        lane, level = lanes(), lax.broadcasted_iota(jnp.int32, (SUBLANES, LANES), 0)
        kept = lane & (1 << level) - 1
        picked = gathered(chunk, (2 * (lane - kept) + (core << level) + kept) & LANES - 1)
        transposed_table([picked[at : at + 1, :] for at in range(local_count + 1)], table, columns)
    for side in range(2):
        place = pl.multiple_of((core ^ side) * chan_rows, chan_rows)
        tile = 0
        for (piece, row), (column, length, ahead) in zip(pieces[side], spans):
            there = lax.axis_index("tm") + ahead < lax.axis_size("tm")
            for start in range(column, column + length, LANES):
                part = piece[row : row + chan_rows, start : start + LANES].astype(jnp.float32)
                if ahead:
                    part = jnp.where(there, part, 0.0)
                raw[tile, pl.ds(place, chan_rows), :] = part
                tile += 1
        for later in range(tile, raw.shape[0] - 1):
            raw[later, pl.ds(place, chan_rows), :] = jnp.zeros((chan_rows, LANES), jnp.float32)
    levels = list(range(local_count + 1))
    lengths = lengths_of(out_tiles, levels)
    mask = lanes() >= core
    for vector in range(SUBLANES):
        low, high = [pl.ds(2 * vector + odd, SUBLANES, stride=2 * SUBLANES) for odd in range(2)]
        upper = raw[0, high, :]
        for tile in range(lengths[0]):
            later = raw[tile + 1, high, :]
            moved = pltpu.roll(jnp.where(mask, upper, later), LANES - core & LANES - 1, 1)
            ping[tile, pl.ds(vector * SUBLANES, SUBLANES), :] = raw[tile, low, :] + moved
            upper = later
    last = tree_levels(ping, pong, columns, 1, levels[1:], 1, lengths[1:], packed=True)
    if not group_count:
        for tile in range(out_tiles):
            rows[tile, :, :] = last[tile, :, :]
        return
    size = chan_rows // group_count
    own = reversed_bits(chip, bits_of(group_count))
    first = earlier.shape[0]
    for mask, block in zip(step_masks(group_count, core), blocks):
        start = pl.multiple_of((own ^ reversed_bits(mask, bits_of(group_count))) * size, size)
        for tile in range(first):
            block[tile, :, :] = earlier[tile, pl.ds(start, size), :].astype(jnp.bfloat16)
        for tile in range(out_tiles):
            block[first + tile, :, :] = last[tile, pl.ds(start, size), :].astype(jnp.bfloat16)


def toeplitz(filters, target):
    width_count, tap_count = filters.shape
    lane = lax.broadcasted_iota(jnp.int32, (LANES, LANES), 1)
    row = lax.broadcasted_iota(jnp.int32, (LANES, LANES), 0)
    taps = filters[...].astype(jnp.float32)
    zeros = jnp.zeros((LANES, LANES), jnp.float32)
    for width in range(width_count):
        before = zeros
        for start in range(0, tap_count + LANES, LANES):
            if start < tap_count:
                spread = jnp.broadcast_to(taps[width : width + 1, start : start + LANES], (LANES, LANES))
                rolled = pltpu.roll(spread, 0, 1, stride=1, stride_axis=0)
            else:
                rolled = zeros
            part = jnp.where(lane >= row, rolled, before)
            target[width * LANES : (width + 1) * LANES, start : start + LANES] = part.astype(jnp.bfloat16)
            before = rolled


def table_kernel(group_count, block_rows, shifts, filters, columns, taps, table):
    level_count = shifts.shape[0]
    chip, core = lax.axis_index("freq"), lax.axis_index("sub")
    own = reversed_bits(chip * 2 + core, bits_of(group_count) + 1)
    lane = lax.broadcasted_iota(jnp.int32, (1, LANES), 1)
    rows = []
    for section in range(bits_of(group_count)):
        level = level_count - bits_of(group_count) + section
        wide = block_rows * 2 ** (section + 1)
        row = jnp.zeros((1, LANES), jnp.int32)
        for subband in range(block_rows * group_count // wide):
            start = subband * 2 ** (level + 1) + own * wide
            tile = pl.multiple_of(start >> bits_of(LANES) << bits_of(LANES), LANES)
            chunk = shifts[level : level + 1, pl.ds(tile, LANES)]
            moved = pltpu.roll(chunk, subband * wide - (start & LANES - 1) & LANES - 1, 1)
            row = jnp.where(lane >= subband * wide, moved, row)
        rows.append(row)
    transposed_table(rows, table, columns)
    toeplitz(filters, taps)


def trial_kernel(plan, group_count, level_count, scale, columns, taps, *refs):
    blocks, refs = refs[:group_count], refs[group_count:]
    halos, refs = refs[: 2 * len(plan.halos)], refs[2 * len(plan.halos) :]
    if plan.taken:
        carried, so_far, refs = refs[0], refs[1], refs[2:]
    out, refs = refs[0], refs[1:]
    if plan.given:
        handed, refs = refs[0], refs[1:]
    state, other, normal, responses, *refs = refs
    if plan.given:
        result = out
    else:
        result, arrived = refs
    chan_rows = result.shape[0]
    block_rows = chan_rows // group_count
    width_count, kept = taps.shape[0] // LANES, taps.shape[1] // LANES - 1
    levels = list(range(level_count - bits_of(group_count), level_count))
    copies = []
    if plan.taken:
        place = out.at[:, pl.ds(0, plan.out_first * LANES)]
        copies.append(pltpu.make_async_copy(so_far, place, arrived.at[len(plan.chunks)]))
        copies[0].start()
    placed(state, blocks, plan.main_tiles, plan.first)
    at = plan.main_tiles - plan.first
    chip, core = lax.axis_index("freq"), lax.axis_index("sub")
    for hop, tiles in enumerate(plan.halos, 1):
        there = lax.axis_index("tm") + hop < lax.axis_size("tm")
        for tile in range(tiles):
            joined, single = [
                jnp.where(there, halo[tile, :, :].astype(jnp.float32), 0.0)
                for halo in halos[2 * hop - 2 : 2 * hop]
            ]
            for index, mask in enumerate(step_masks(group_count, core)):
                start = pl.multiple_of((chip ^ mask) * block_rows, block_rows)
                if index + 1 < group_count:
                    part = joined[index * block_rows : (index + 1) * block_rows]
                else:
                    part = single
                state[at, pl.ds(start, block_rows), :] = part
            at += 1
    for tile in range(at, at + plan.empty_tiles):
        state[tile, :, :] = jnp.zeros((chan_rows, LANES), jnp.float32)
    last = tree_levels(state, other, columns, 0, levels, block_rows, plan.lengths)
    head = kept if plan.taken else 0
    for tile in range(head):
        normal[tile, :, :] = carried[tile, :, :]
    for tile in range(plan.made):
        normal[head + tile, :, :] = (last[tile, :, :] * scale).astype(jnp.bfloat16)
    count = plan.out_tiles
    if plan.given:
        for tile in range(kept):
            handed[tile, :, :] = normal[count + tile, :, :]
    for turn, (first_tile, some) in enumerate(plan.chunks):
        size = some * chan_rows
        windows = [
            normal[first_tile + offset : first_tile + offset + some, :, :].reshape(size, LANES)
            for offset in range(kept + 1)
        ]
        responses[0:size, :] = lax.dot_general(
            jnp.concatenate(windows, axis=1),
            taps[...],
            (((1,), (1,)), ((), ())),
            preferred_element_type=jnp.float32,
        )
        for first_row in range(0, size, PACKED):
            energies = []
            for width in range(width_count):
                one = responses[first_row : first_row + PACKED, width * LANES : (width + 1) * LANES]
                energies.append((0.5 * LOG2_E) * one * one)
            highest = functools.reduce(jnp.maximum, energies)
            total = functools.reduce(jnp.add, [jnp.exp2(energy - highest) for energy in energies])
            tile, row = first_tile + first_row // chan_rows, first_row % chan_rows
            result[row : row + PACKED, tile * LANES : (tile + 1) * LANES] = (
                jnp.log2(total) + highest
            ) * (1.0 / LOG2_E)
        if plan.given:
            continue
        columns_now = pl.ds(first_tile * LANES, some * LANES)
        place = out.at[:, pl.ds((plan.out_first + first_tile) * LANES, some * LANES)]
        copies.append(pltpu.make_async_copy(result.at[:, columns_now], place, arrived.at[turn]))
        copies[-1].start()
    for copy in copies:
        copy.wait()


class Plan:
    def __init__(self, main_tiles, halos, empty_tiles, out_first, out_tiles, taken, given, levels, tap_tiles):
        self.main_tiles, self.halos, self.empty_tiles = main_tiles, halos, empty_tiles
        self.out_first, self.out_tiles = out_first, out_tiles
        self.taken, self.given = taken, given
        self.made = out_tiles if taken else out_tiles + tap_tiles
        self.first = out_first + tap_tiles if taken else 0
        self.lengths = lengths_of(self.made, levels)
        turns = -(-out_tiles // 6)
        ends = [out_tiles * turn // turns for turn in range(turns + 1)]
        self.chunks = [(start, end - start) for start, end in zip(ends, ends[1:])]
        self.state_tiles = main_tiles + sum(halos) + empty_tiles - self.first + max(2 ** levels[-1] // LANES, 1) + 1


def local(filterbank, delay_shifts, pulse_filters):
    chan_rows, time_len = filterbank.shape
    group_count = lax.axis_size("freq")
    assert lax.axis_size("sub") == 2 and 2 * chan_rows == LANES
    level_count = delay_shifts.shape[0]
    width_count, tap_count = pulse_filters.shape
    tap_tiles = tap_count // LANES
    time_tiles = time_len // LANES
    far_levels = range(level_count - bits_of(group_count), level_count)
    near_reach = 2 ** far_levels[0] - 1
    near_len = rounded_up(near_reach, LANES)
    far_tiles = -(-(2**level_count - 1 - near_reach + tap_count) // LANES)

    in_vmem = pl.BlockSpec(memory_space=pltpu.VMEM)
    in_any = pl.BlockSpec(memory_space=pl.ANY)
    params = pltpu.CompilerParams(vmem_limit_bytes=VMEM_LIMIT)
    block_rows = chan_rows // group_count
    table = pltpu.VMEM((LANES, LANES), jnp.float32)

    def within_chip(operands, spans, raw_tiles, out_tiles, sending):
        state = pltpu.VMEM((raw_tiles + 1, chan_rows, LANES), jnp.float32)
        if sending:
            block = jax.ShapeDtypeStruct((time_tiles, block_rows, LANES), jnp.bfloat16)
            out_shape = [block] * group_count
        else:
            out_shape = [
                jax.ShapeDtypeStruct((out_tiles, chan_rows, LANES), jnp.float32),
                jax.ShapeDtypeStruct((LANES, LANES), jnp.float32),
            ]
        return pl.pallas_call(
            functools.partial(chip_kernel, spans, out_tiles, group_count if sending else 0),
            out_shape=out_shape,
            in_specs=[in_vmem] * len(operands),
            out_specs=[in_vmem] * len(out_shape),
            scratch_shapes=[pltpu.VMEM((raw_tiles + 1, 2 * chan_rows, LANES), jnp.float32), state, state]
            + ([] if sending else [table]),
            compiler_params=params,
        )(*operands)

    def between_chips(plan, blocks, halos, carried=()):
        state = pltpu.VMEM((plan.state_tiles, chan_rows, LANES), jnp.float32)
        operands = [columns, taps, *blocks, *halos, *carried]
        result = (chan_rows, plan.out_tiles * LANES)
        if plan.given:
            out_shape = [
                jax.ShapeDtypeStruct(result, jnp.float32),
                jax.ShapeDtypeStruct((tap_tiles, chan_rows, LANES), jnp.bfloat16),
            ]
            out_specs, scratch = [in_vmem] * 2, []
        else:
            out_shape, out_specs = [jax.ShapeDtypeStruct((chan_rows, time_len), jnp.float32)], [in_any]
            scratch = [pltpu.VMEM(result, jnp.float32), pltpu.SemaphoreType.DMA((len(plan.chunks) + 1,))]
        most = max(some for _, some in plan.chunks)
        scale = 1.0 / math.sqrt(delay_shifts.shape[1])
        return pl.pallas_call(
            functools.partial(trial_kernel, plan, group_count, level_count, scale),
            out_shape=out_shape,
            in_specs=[in_vmem] * len(operands),
            out_specs=out_specs,
            scratch_shapes=[
                state,
                state,
                pltpu.VMEM((plan.out_tiles + tap_tiles, chan_rows, LANES), jnp.bfloat16),
                pltpu.VMEM((most * chan_rows, width_count * LANES), jnp.float32),
            ]
            + scratch,
            compiler_params=params,
        )(*operands)

    other_core = from_partner(filterbank, "sub", 1)
    own = pl.pallas_call(
        load_kernel,
        out_shape=jax.ShapeDtypeStruct(filterbank.shape, filterbank.dtype),
        in_specs=[in_vmem],
        out_specs=in_vmem,
        compiler_params=params,
    )(filterbank)
    ahead = pl.pallas_call(
        start_kernel,
        out_shape=jax.ShapeDtypeStruct((2 * chan_rows, near_len), filterbank.dtype),
        in_specs=[in_vmem] * 2,
        out_specs=in_vmem,
        compiler_params=params,
    )(own, other_core)
    near_tiles = near_len // LANES
    early = time_tiles - near_tiles
    rows, delays = within_chip(
        [own, other_core, delay_shifts], [(0, time_len, 0)], time_tiles, early, False
    )
    operands, spans = [own, other_core], [(early * LANES, near_len, 0)]
    if lax.axis_size("tm") > 1:
        operands.append(from_ahead(ahead, 1))
        spans.append((0, near_len, 1))
    main = list(within_chip([*operands, rows, delays], spans, 2 * near_tiles, near_tiles, True))
    late_shifts, late_filters, main[0] = lax.optimization_barrier((delay_shifts, pulse_filters, main[0]))
    columns, taps = pl.pallas_call(
        functools.partial(table_kernel, group_count, block_rows),
        out_shape=[
            jax.ShapeDtypeStruct((LANES, LANES), jnp.float32),
            jax.ShapeDtypeStruct((width_count * LANES, tap_count + LANES), jnp.bfloat16),
        ],
        in_specs=[in_vmem] * 2,
        out_specs=[in_vmem] * 2,
        scratch_shapes=[table],
        compiler_params=params,
    )(late_shifts, late_filters)
    *main, last = exchanged(main)
    columns, taps, last = lax.optimization_barrier((columns, taps, last))
    main.append(last)

    halos, takes = [], []
    rest = far_tiles
    if lax.axis_size("tm") > 1:
        first_tiles = min(time_tiles, far_tiles)
        joined = pl.pallas_call(
            join_kernel,
            out_shape=jax.ShapeDtypeStruct(
                (first_tiles, chan_rows - block_rows, LANES), jnp.bfloat16
            ),
            in_specs=[in_vmem] * (group_count - 1),
            out_specs=in_vmem,
            scratch_shapes=[pltpu.VMEM((first_tiles, chan_rows - block_rows, LANES), jnp.float32)],
            compiler_params=params,
        )(*main[:-1])
        for hop in range(1, lax.axis_size("tm")):
            if rest > 0:
                takes.append(min(time_tiles, rest))
                halos.append(from_ahead(joined[: takes[-1]], hop))
                halos.append(from_ahead(main[-1][: takes[-1]], hop))
                rest -= takes[-1]
    lost = -(-sum(2**level for level in far_levels) // LANES) + tap_tiles
    early_tiles = time_tiles - lost
    if early_tiles <= 0:
        plan = Plan(time_tiles, takes, rest, 0, time_tiles, False, False, far_levels, tap_tiles)
        return between_chips(plan, main, halos)[0]
    plan = Plan(time_tiles, [], 0, 0, early_tiles, False, True, far_levels, tap_tiles)
    out, *carried = between_chips(plan, main, [])
    late_tiles = time_tiles - early_tiles
    plan = Plan(time_tiles, takes, rest, early_tiles, late_tiles, True, False, far_levels, tap_tiles)
    return between_chips(plan, main, halos, [*carried, out])[0]


def solution(mesh):
    in_specs = (P(("beams", "freq", "sub"), "tm"), P(), P())
    out_specs = P(("beams", "freq", "sub"), "tm")
    return jax.shard_map(local, mesh=mesh, in_specs=in_specs, out_specs=out_specs, check_vma=False)
```

```python
import functools
import math

import jax
import jax.numpy as jnp
from jax import lax
from jax.experimental import pallas as pl
from jax.experimental.pallas import tpu as pltpu
from jax.sharding import PartitionSpec as P

LANES = 128
SUBLANES = 8
PACKED = 16
SHORT = 4
LOG2_E = 1.4426950408889634
VMEM_LIMIT = 48 * 2**20


def rounded_up(value, unit):
    return -(-value // unit) * unit


def reversed_bits(value, bit_count):
    result = 0
    for bit_num in range(bit_count):
        result = result | (value >> bit_num & 1) << bit_count - 1 - bit_num
    return result


def bits_of(count):
    return count.bit_length() - 1


def from_ahead(value, steps):
    count = lax.axis_size("tm")
    return lax.ppermute(value, "tm", [((block + steps) % count, block) for block in range(count)])


def from_partner(value, axis, mask):
    count = lax.axis_size(axis)
    return lax.ppermute(value, axis, [(source, source ^ mask) for source in range(count)])


def mask_orders(group_count):
    far = list(range(group_count - 1, 1, -1))
    return [1, *far], far[-1:] + far[:-1] + [1]


def step_masks(group_count, core):
    orders = mask_orders(group_count)
    return [0] + [jnp.where(core == 0, first, second) for first, second in zip(*orders)]


def exchanged(blocks, cut):
    count = lax.axis_size("freq")
    received = [(0, 0, blocks[0])]
    for step, masks in enumerate(zip(*mask_orders(count)), 1):
        route = [
            (chip * 2 + core, (chip ^ masks[core]) * 2 + core) for chip in range(count) for core in range(2)
        ]
        tiles = blocks[step].shape[0]
        ends = [0, cut, tiles] if step + 1 == count and 0 < cut < tiles else [0, tiles]
        for first, end in zip(ends, ends[1:]):
            received.append((step, first, lax.ppermute(blocks[step][first:end], ("freq", "sub"), route)))
    return received


def lanes():
    return lax.broadcasted_iota(jnp.int32, (SUBLANES, LANES), 1)


def gathered(value, index):
    return jnp.take_along_axis(value, index, axis=1, mode="promise_in_bounds")


def transposed_table(rows, table, columns):
    for index, row in enumerate(rows):
        table[index : index + 1, :] = row.astype(jnp.float32)
    columns[...] = table[...].T


def merge_short(source, target, low, high, outs, tiles, most):
    inside = [lanes() < LANES - delay for delay in range(1, most + 1)]
    chosen = [([amount == delay for delay in range(1, most + 1)], place) for amount, place in outs]

    def rolled(tile):
        value = source[tile, high, :]
        return value, [pltpu.roll(value, LANES - delay, 1) for delay in range(1, most + 1)]

    now = rolled(0)
    for tile in range(tiles):
        later = rolled(tile + 1)
        copies = [jnp.where(*parts) for parts in zip(inside, now[1], later[1])]
        lower = source[tile, low, :]
        for masks, place in chosen:
            moved = now[0]
            for mask, copy in zip(masks, copies):
                moved = jnp.where(mask, copy, moved)
            target[tile, place, :] = lower + moved
        now = later


def merge(source, target, low, high, outs, tiles, most):
    if most <= SHORT:
        return merge_short(source, target, low, high, outs, tiles, most)
    lane = lanes()
    apart = max(most // LANES, 1)
    chosen = []
    for amount, place in outs:
        part = amount if most < LANES else amount & LANES - 1
        moved = (lane < part).astype(jnp.int32)
        if most >= LANES:
            moved = moved + (amount >> bits_of(LANES))
        masks = [moved == offset for offset in range(1, apart + 1)]
        chosen.append((masks, lane + part & LANES - 1, place))
    for masks, index, place in chosen:
        upper = [source[offset, high, :] for offset in range(apart)]
        for tile in range(tiles):
            upper.append(source[tile + apart, high, :])
            mixed = upper[0]
            for mask, other in zip(masks, upper[1:]):
                mixed = jnp.where(mask, other, mixed)
            target[tile, place, :] = source[tile, low, :] + gathered(mixed, index)
            upper = upper[1:]


def tree_levels(state, other, columns, first, levels, held, lengths, packed=False):
    rows = columns.shape[0] // 2
    source, target = state, other
    done = 0
    while done < len(levels):
        narrow = held < SUBLANES
        bits = min(bits_of(SUBLANES // held), len(levels) - done) if narrow else len(levels) - done
        for turn in range(bits):
            level = levels[done + turn]
            inner = turn + 1 < bits
            natural = turn == 0 and not (packed and done == 0)

            def rows_in(vector, start, stride):
                return pl.ds(start, SUBLANES, stride=stride) if natural else pl.ds(vector * SUBLANES, SUBLANES)

            def rows_out(vector, start, stride):
                return pl.ds(vector * SUBLANES, SUBLANES) if inner else pl.ds(start, SUBLANES, stride=stride)

            def amounts(start, stride):
                column = columns[pl.ds(start, SUBLANES, stride=stride), :]
                one = column[:, first + done + turn : first + done + turn + 1]
                return jnp.broadcast_to(one, (SUBLANES, LANES)).astype(jnp.int32)

            if narrow:
                now = held << turn
                for band in range(SUBLANES // (2 * now)):
                    for trial in range(now):
                        low, high = 2 * band * now + trial, (2 * band + 1) * now + trial
                        outs = [band * 2 * now + 2 * trial + odd for odd in range(2)]
                        merge(
                            source,
                            target,
                            rows_in(low, low, SUBLANES),
                            rows_in(high, high, SUBLANES),
                            [(amounts(out, SUBLANES), rows_out(out, out, SUBLANES)) for out in outs],
                            lengths[done + turn],
                            2**level,
                        )
            else:
                groups, split = held // SUBLANES, 2**turn
                for band in range(rows // (2 * held * split)):
                    for group in range(groups):
                        for place in range(split):
                            low, high = [
                                ((2 * band + upper) * groups + group) * split + place for upper in range(2)
                            ]
                            outs = []
                            for odd in range(2):
                                vector = (band * groups + group) * 2 * split + 2 * place + odd
                                start = (band * groups + group) * SUBLANES * 2 * split + 2 * place + odd
                                outs.append((amounts(start, 2 * split), rows_out(vector, start, 2 * split)))
                            merge(
                                source,
                                target,
                                rows_in(low, low * SUBLANES, 1),
                                rows_in(high, high * SUBLANES, 1),
                                outs,
                                lengths[done + turn],
                                2**level,
                            )
            source, target = target, source
        held <<= bits
        done += bits
    return source


def lengths_of(made, levels):
    return [made + -(-sum(2**later for later in levels if later > level) // LANES) for level in levels]


def load_kernel(whole, copied):
    copied[...] = whole[...]


def start_kernel(whole, other, ahead):
    rows, length = whole.shape[0], ahead.shape[1]
    ahead[:rows, :] = whole[:, :length]
    ahead[rows:, :] = other[:, :length]


def placed(target, blocks, group_count, skip):
    chip, core = lax.axis_index("freq"), lax.axis_index("sub")
    masks = step_masks(group_count, core)
    for step, first, block in blocks:
        tiles, rows = block.shape[:2]
        start = pl.multiple_of((chip ^ masks[step]) * rows, rows)
        for tile in range(max(skip - first, 0), tiles):
            target[first + tile - skip, pl.ds(start, rows), :] = block[tile, :, :].astype(jnp.float32)


def join_kernel(*refs):
    *blocks, out, state = refs
    rows = blocks[0].shape[1]
    for tile in range(out.shape[0]):
        for index, block in enumerate(blocks):
            state[tile, index * rows : (index + 1) * rows, :] = block[tile, :, :].astype(jnp.float32)
        out[tile, :, :] = state[tile, :, :].astype(jnp.bfloat16)


def chip_kernel(spans, out_tiles, group_count, *refs):
    chan_rows = refs[0].shape[0]
    pieces = [[(refs[side], 0)] + [(ref, side * chan_rows) for ref in refs[2 : len(spans) + 1]] for side in range(2)]
    refs = refs[len(spans) + 1 :]
    local_count = bits_of(chan_rows)
    chip, core = lax.axis_index("freq"), lax.axis_index("sub")
    if group_count:
        (earlier, columns), blocks, (raw, ping, pong) = refs[:2], refs[2:-3], refs[-3:]
    else:
        shifts, rows, columns, raw, ping, pong, table = refs
        chunk = shifts[0:SUBLANES, pl.ds(pl.multiple_of(chip * LANES, LANES), LANES)]
        lane, level = lanes(), lax.broadcasted_iota(jnp.int32, (SUBLANES, LANES), 0)
        kept = lane & (1 << level) - 1
        picked = gathered(chunk, (2 * (lane - kept) + (core << level) + kept) & LANES - 1)
        transposed_table([picked[at : at + 1, :] for at in range(local_count + 1)], table, columns)
    for side in range(2):
        place = pl.multiple_of((core ^ side) * chan_rows, chan_rows)
        tile = 0
        for (piece, row), (column, length, ahead) in zip(pieces[side], spans):
            there = lax.axis_index("tm") + ahead < lax.axis_size("tm")
            for start in range(column, column + length, LANES):
                part = piece[row : row + chan_rows, start : start + LANES].astype(jnp.float32)
                if ahead:
                    part = jnp.where(there, part, 0.0)
                raw[tile, pl.ds(place, chan_rows), :] = part
                tile += 1
        for later in range(tile, raw.shape[0] - 1):
            raw[later, pl.ds(place, chan_rows), :] = jnp.zeros((chan_rows, LANES), jnp.float32)
    levels = list(range(local_count + 1))
    lengths = lengths_of(out_tiles, levels)
    mask = lanes() >= core
    for vector in range(SUBLANES):
        low, high = [pl.ds(2 * vector + odd, SUBLANES, stride=2 * SUBLANES) for odd in range(2)]
        upper = raw[0, high, :]
        for tile in range(lengths[0]):
            later = raw[tile + 1, high, :]
            moved = pltpu.roll(jnp.where(mask, upper, later), LANES - core & LANES - 1, 1)
            ping[tile, pl.ds(vector * SUBLANES, SUBLANES), :] = raw[tile, low, :] + moved
            upper = later
    last = tree_levels(ping, pong, columns, 1, levels[1:], 1, lengths[1:], packed=True)
    if not group_count:
        for tile in range(out_tiles):
            rows[tile, :, :] = last[tile, :, :]
        return
    size = chan_rows // group_count
    own = reversed_bits(chip, bits_of(group_count))
    first = earlier.shape[0]
    for mask, block in zip(step_masks(group_count, core), blocks):
        start = pl.multiple_of((own ^ reversed_bits(mask, bits_of(group_count))) * size, size)
        for tile in range(first):
            block[tile, :, :] = earlier[tile, pl.ds(start, size), :].astype(jnp.bfloat16)
        for tile in range(out_tiles):
            block[first + tile, :, :] = last[tile, pl.ds(start, size), :].astype(jnp.bfloat16)


def toeplitz(filters, target):
    width_count, tap_count = filters.shape
    lane = lax.broadcasted_iota(jnp.int32, (LANES, LANES), 1)
    row = lax.broadcasted_iota(jnp.int32, (LANES, LANES), 0)
    taps = filters[...].astype(jnp.float32)
    zeros = jnp.zeros((LANES, LANES), jnp.float32)
    for width in range(width_count):
        before = zeros
        for start in range(0, tap_count + LANES, LANES):
            if start < tap_count:
                spread = jnp.broadcast_to(taps[width : width + 1, start : start + LANES], (LANES, LANES))
                rolled = pltpu.roll(spread, 0, 1, stride=1, stride_axis=0)
            else:
                rolled = zeros
            part = jnp.where(lane >= row, rolled, before)
            target[width * LANES : (width + 1) * LANES, start : start + LANES] = part.astype(jnp.bfloat16)
            before = rolled


def table_kernel(group_count, block_rows, shifts, filters, columns, taps, table):
    level_count = shifts.shape[0]
    chip, core = lax.axis_index("freq"), lax.axis_index("sub")
    own = reversed_bits(chip * 2 + core, bits_of(group_count) + 1)
    lane = lax.broadcasted_iota(jnp.int32, (1, LANES), 1)
    rows = []
    for section in range(bits_of(group_count)):
        level = level_count - bits_of(group_count) + section
        wide = block_rows * 2 ** (section + 1)
        row = jnp.zeros((1, LANES), jnp.int32)
        for subband in range(block_rows * group_count // wide):
            start = subband * 2 ** (level + 1) + own * wide
            tile = pl.multiple_of(start >> bits_of(LANES) << bits_of(LANES), LANES)
            chunk = shifts[level : level + 1, pl.ds(tile, LANES)]
            moved = pltpu.roll(chunk, subband * wide - (start & LANES - 1) & LANES - 1, 1)
            row = jnp.where(lane >= subband * wide, moved, row)
        rows.append(row)
    transposed_table(rows, table, columns)
    toeplitz(filters, taps)


def trial_kernel(plan, group_count, level_count, scale, columns, taps, *refs):
    blocks, refs = refs[: len(plan.pieces)], refs[len(plan.pieces) :]
    halos, refs = refs[: len(plan.halos)], refs[len(plan.halos) :]
    if plan.taken:
        carried, so_far, refs = refs[0], refs[1], refs[2:]
    out, refs = refs[0], refs[1:]
    if plan.given:
        handed, refs = refs[0], refs[1:]
    state, other, normal, responses, *refs = refs
    if plan.given:
        result = out
    else:
        result, arrived = refs
    chan_rows = result.shape[0]
    block_rows = chan_rows // group_count
    width_count, kept = taps.shape[0] // LANES, taps.shape[1] // LANES - 1
    levels = list(range(level_count - bits_of(group_count), level_count))
    copies = []
    if plan.taken:
        place = out.at[:, pl.ds(0, plan.out_first * LANES)]
        copies.append(pltpu.make_async_copy(so_far, place, arrived.at[len(plan.chunks)]))
        copies[0].start()
    pieces = [(step, first, block) for (step, first), block in zip(plan.pieces, blocks)]
    placed(state, pieces, group_count, plan.first)
    at = plan.main_tiles - plan.first
    chip, core = lax.axis_index("freq"), lax.axis_index("sub")
    for hop, tiles in enumerate(plan.halos, 1):
        there = lax.axis_index("tm") + hop < lax.axis_size("tm")
        for tile in range(tiles):
            joined = jnp.where(there, halos[hop - 1][tile, :, :].astype(jnp.float32), 0.0)
            for index, mask in enumerate(step_masks(group_count, core)):
                start = pl.multiple_of((chip ^ mask) * block_rows, block_rows)
                part = joined[index * block_rows : (index + 1) * block_rows]
                state[at, pl.ds(start, block_rows), :] = part
            at += 1
    for tile in range(at, at + plan.empty_tiles):
        state[tile, :, :] = jnp.zeros((chan_rows, LANES), jnp.float32)
    last = tree_levels(state, other, columns, 0, levels, block_rows, plan.lengths)
    head = kept if plan.taken else 0
    for tile in range(head):
        normal[tile, :, :] = carried[tile, :, :]
    for tile in range(plan.made):
        normal[head + tile, :, :] = (last[tile, :, :] * scale).astype(jnp.bfloat16)
    count = plan.out_tiles
    if plan.given:
        for tile in range(kept):
            handed[tile, :, :] = normal[count + tile, :, :]
    for turn, (first_tile, some) in enumerate(plan.chunks):
        size = some * chan_rows
        windows = [
            normal[first_tile + offset : first_tile + offset + some, :, :].reshape(size, LANES)
            for offset in range(kept + 1)
        ]
        responses[0:size, :] = lax.dot_general(
            jnp.concatenate(windows, axis=1),
            taps[...],
            (((1,), (1,)), ((), ())),
            preferred_element_type=jnp.float32,
        )
        for first_row in range(0, size, PACKED):
            energies = []
            for width in range(width_count):
                one = responses[first_row : first_row + PACKED, width * LANES : (width + 1) * LANES]
                energies.append((0.5 * LOG2_E) * one * one)
            highest = functools.reduce(jnp.maximum, energies)
            total = functools.reduce(jnp.add, [jnp.exp2(energy - highest) for energy in energies])
            tile, row = first_tile + first_row // chan_rows, first_row % chan_rows
            result[row : row + PACKED, tile * LANES : (tile + 1) * LANES] = (
                jnp.log2(total) + highest
            ) * (1.0 / LOG2_E)
        if plan.given:
            continue
        columns_now = pl.ds(first_tile * LANES, some * LANES)
        place = out.at[:, pl.ds((plan.out_first + first_tile) * LANES, some * LANES)]
        copies.append(pltpu.make_async_copy(result.at[:, columns_now], place, arrived.at[turn]))
        copies[-1].start()
    for copy in copies:
        copy.wait()


class Plan:
    def __init__(self, pieces, main_tiles, halos, empty_tiles, out_first, out_tiles, taken, given, levels, tap_tiles):
        self.pieces = pieces
        self.main_tiles, self.halos, self.empty_tiles = main_tiles, halos, empty_tiles
        self.out_first, self.out_tiles = out_first, out_tiles
        self.taken, self.given = taken, given
        self.made = out_tiles if taken else out_tiles + tap_tiles
        self.first = out_first + tap_tiles if taken else 0
        self.lengths = lengths_of(self.made, levels)
        turns = -(-out_tiles // 6)
        ends = [out_tiles * turn // turns for turn in range(turns + 1)]
        self.chunks = [(start, end - start) for start, end in zip(ends, ends[1:])]
        self.state_tiles = main_tiles + sum(halos) + empty_tiles - self.first + max(2 ** levels[-1] // LANES, 1) + 1


def local(filterbank, delay_shifts, pulse_filters):
    chan_rows, time_len = filterbank.shape
    group_count = lax.axis_size("freq")
    assert lax.axis_size("sub") == 2 and 2 * chan_rows == LANES
    level_count = delay_shifts.shape[0]
    width_count, tap_count = pulse_filters.shape
    tap_tiles = tap_count // LANES
    time_tiles = time_len // LANES
    far_levels = range(level_count - bits_of(group_count), level_count)
    near_reach = 2 ** far_levels[0] - 1
    near_len = rounded_up(near_reach, LANES)
    far_tiles = -(-(2**level_count - 1 - near_reach + tap_count) // LANES)

    in_vmem = pl.BlockSpec(memory_space=pltpu.VMEM)
    in_any = pl.BlockSpec(memory_space=pl.ANY)
    params = pltpu.CompilerParams(vmem_limit_bytes=VMEM_LIMIT)
    block_rows = chan_rows // group_count
    table = pltpu.VMEM((LANES, LANES), jnp.float32)

    def within_chip(operands, spans, raw_tiles, out_tiles, sending):
        state = pltpu.VMEM((raw_tiles + 1, chan_rows, LANES), jnp.float32)
        if sending:
            block = jax.ShapeDtypeStruct((time_tiles, block_rows, LANES), jnp.bfloat16)
            out_shape = [block] * group_count
        else:
            out_shape = [
                jax.ShapeDtypeStruct((out_tiles, chan_rows, LANES), jnp.float32),
                jax.ShapeDtypeStruct((LANES, LANES), jnp.float32),
            ]
        return pl.pallas_call(
            functools.partial(chip_kernel, spans, out_tiles, group_count if sending else 0),
            out_shape=out_shape,
            in_specs=[in_vmem] * len(operands),
            out_specs=[in_vmem] * len(out_shape),
            scratch_shapes=[pltpu.VMEM((raw_tiles + 1, 2 * chan_rows, LANES), jnp.float32), state, state]
            + ([] if sending else [table]),
            compiler_params=params,
        )(*operands)

    def between_chips(plan, blocks, halos, carried=()):
        state = pltpu.VMEM((plan.state_tiles, chan_rows, LANES), jnp.float32)
        operands = [columns, taps, *blocks, *halos, *carried]
        result = (chan_rows, plan.out_tiles * LANES)
        if plan.given:
            out_shape = [
                jax.ShapeDtypeStruct(result, jnp.float32),
                jax.ShapeDtypeStruct((tap_tiles, chan_rows, LANES), jnp.bfloat16),
            ]
            out_specs, scratch = [in_vmem] * 2, []
        else:
            out_shape, out_specs = [jax.ShapeDtypeStruct((chan_rows, time_len), jnp.float32)], [in_any]
            scratch = [pltpu.VMEM(result, jnp.float32), pltpu.SemaphoreType.DMA((len(plan.chunks) + 1,))]
        most = max(some for _, some in plan.chunks)
        scale = 1.0 / math.sqrt(delay_shifts.shape[1])
        return pl.pallas_call(
            functools.partial(trial_kernel, plan, group_count, level_count, scale),
            out_shape=out_shape,
            in_specs=[in_vmem] * len(operands),
            out_specs=out_specs,
            scratch_shapes=[
                state,
                state,
                pltpu.VMEM((plan.out_tiles + tap_tiles, chan_rows, LANES), jnp.bfloat16),
                pltpu.VMEM((most * chan_rows, width_count * LANES), jnp.float32),
            ]
            + scratch,
            compiler_params=params,
            cost_estimate=pl.CostEstimate(
                flops=2 * plan.out_tiles * LANES * chan_rows * width_count * (tap_count + LANES),
                bytes_accessed=40 * plan.out_tiles * LANES * chan_rows * width_count,
                transcendentals=plan.out_tiles * LANES * chan_rows * (width_count + 1),
            ),
        )(*operands)

    other_core = from_partner(filterbank, "sub", 1)
    own = pl.pallas_call(
        load_kernel,
        out_shape=jax.ShapeDtypeStruct(filterbank.shape, filterbank.dtype),
        in_specs=[in_vmem],
        out_specs=in_vmem,
        compiler_params=params,
    )(filterbank)
    ahead = pl.pallas_call(
        start_kernel,
        out_shape=jax.ShapeDtypeStruct((2 * chan_rows, near_len), filterbank.dtype),
        in_specs=[in_vmem] * 2,
        out_specs=in_vmem,
        compiler_params=params,
    )(own, other_core)
    near_tiles = near_len // LANES
    early = time_tiles - near_tiles
    rows, delays = within_chip(
        [own, other_core, delay_shifts], [(0, time_len, 0)], time_tiles, early, False
    )
    operands, spans = [own, other_core], [(early * LANES, near_len, 0)]
    if lax.axis_size("tm") > 1:
        operands.append(from_ahead(ahead, 1))
        spans.append((0, near_len, 1))
    main = list(within_chip([*operands, rows, delays], spans, 2 * near_tiles, near_tiles, True))
    late_shifts, late_filters, main[0] = lax.optimization_barrier((delay_shifts, pulse_filters, main[0]))
    columns, taps = pl.pallas_call(
        functools.partial(table_kernel, group_count, block_rows),
        out_shape=[
            jax.ShapeDtypeStruct((LANES, LANES), jnp.float32),
            jax.ShapeDtypeStruct((width_count * LANES, tap_count + LANES), jnp.bfloat16),
        ],
        in_specs=[in_vmem] * 2,
        out_specs=[in_vmem] * 2,
        scratch_shapes=[table],
        compiler_params=params,
    )(late_shifts, late_filters)
    first_tiles = min(time_tiles, far_tiles) if lax.axis_size("tm") > 1 else 0
    *arrived, (step, first, last) = exchanged(main, first_tiles)
    columns, taps, last = lax.optimization_barrier((columns, taps, last))
    arrived.append((step, first, last))
    pieces = [(step, first) for step, first, _ in arrived]
    main = [block for _, _, block in arrived]

    halos, takes = [], []
    rest = far_tiles
    if lax.axis_size("tm") > 1:
        heads = [block for _, first, block in arrived if first == 0]
        joined = pl.pallas_call(
            join_kernel,
            out_shape=jax.ShapeDtypeStruct((first_tiles, chan_rows, LANES), jnp.bfloat16),
            in_specs=[in_vmem] * len(heads),
            out_specs=in_vmem,
            scratch_shapes=[pltpu.VMEM((first_tiles, chan_rows, LANES), jnp.float32)],
            compiler_params=params,
        )(*heads)
        for hop in range(1, lax.axis_size("tm")):
            if rest > 0:
                takes.append(min(time_tiles, rest))
                halos.append(from_ahead(joined[: takes[-1]], hop))
                rest -= takes[-1]
    lost = -(-sum(2**level for level in far_levels) // LANES) + tap_tiles
    early_tiles = time_tiles - lost
    if early_tiles <= 0:
        plan = Plan(pieces, time_tiles, takes, rest, 0, time_tiles, False, False, far_levels, tap_tiles)
        return between_chips(plan, main, halos)[0]
    plan = Plan(pieces, time_tiles, [], 0, 0, early_tiles, False, True, far_levels, tap_tiles)
    out, *carried = between_chips(plan, main, [])
    late_tiles = time_tiles - early_tiles
    plan = Plan(pieces, time_tiles, takes, rest, early_tiles, late_tiles, True, False, far_levels, tap_tiles)
    return between_chips(plan, main, halos, [*carried, out])[0]


def solution(mesh):
    in_specs = (P(("beams", "freq", "sub"), "tm"), P(), P())
    out_specs = P(("beams", "freq", "sub"), "tm")
    return jax.shard_map(local, mesh=mesh, in_specs=in_specs, out_specs=out_specs, check_vma=False)
```

```python
import functools
import math

import jax
import jax.numpy as jnp
from jax import lax
from jax.experimental import pallas as pl
from jax.experimental.pallas import tpu as pltpu
from jax.sharding import PartitionSpec as P

LANES = 128
SUBLANES = 8
PACKED = 16
SHORT = 4
LOG2_E = 1.4426950408889634
VMEM_LIMIT = 48 * 2**20


def rounded_up(value, unit):
    return -(-value // unit) * unit


def reversed_bits(value, bit_count):
    result = 0
    for bit_num in range(bit_count):
        result = result | (value >> bit_num & 1) << bit_count - 1 - bit_num
    return result


def bits_of(count):
    return count.bit_length() - 1


def from_ahead(value, steps):
    count = lax.axis_size("tm")
    return lax.ppermute(value, "tm", [((block + steps) % count, block) for block in range(count)])


def from_partner(value, axis, mask):
    count = lax.axis_size(axis)
    return lax.ppermute(value, axis, [(source, source ^ mask) for source in range(count)])


def mask_orders(group_count):
    far = list(range(group_count - 1, 1, -1))
    return [1, *far], far[-1:] + far[:-1] + [1]


def step_masks(group_count, core):
    orders = mask_orders(group_count)
    return [0] + [jnp.where(core == 0, first, second) for first, second in zip(*orders)]


def exchanged(blocks):
    count = lax.axis_size("freq")
    received = [blocks[0]]
    for block, masks in zip(blocks[1:], zip(*mask_orders(count))):
        route = [
            (chip * 2 + core, (chip ^ masks[core]) * 2 + core) for chip in range(count) for core in range(2)
        ]
        received.append(lax.ppermute(block, ("freq", "sub"), route))
    return received


def lanes():
    return lax.broadcasted_iota(jnp.int32, (SUBLANES, LANES), 1)


def gathered(value, index):
    return jnp.take_along_axis(value, index, axis=1, mode="promise_in_bounds")


def transposed_table(rows, table, columns):
    for index, row in enumerate(rows):
        table[index : index + 1, :] = row.astype(jnp.float32)
    columns[...] = table[...].T


def merge_short(source, target, low, high, outs, tiles, most):
    inside = [lanes() < LANES - delay for delay in range(1, most + 1)]
    chosen = [([amount == delay for delay in range(1, most + 1)], place) for amount, place in outs]

    def rolled(tile):
        value = source[tile, high, :]
        return value, [pltpu.roll(value, LANES - delay, 1) for delay in range(1, most + 1)]

    now = rolled(0)
    for tile in range(tiles):
        later = rolled(tile + 1)
        copies = [jnp.where(*parts) for parts in zip(inside, now[1], later[1])]
        lower = source[tile, low, :]
        for masks, place in chosen:
            moved = now[0]
            for mask, copy in zip(masks, copies):
                moved = jnp.where(mask, copy, moved)
            target[tile, place, :] = lower + moved
        now = later


def merge(source, target, low, high, outs, tiles, most):
    if most <= SHORT:
        return merge_short(source, target, low, high, outs, tiles, most)
    lane = lanes()
    apart = max(most // LANES, 1)
    chosen = []
    for amount, place in outs:
        part = amount if most < LANES else amount & LANES - 1
        moved = (lane < part).astype(jnp.int32)
        if most >= LANES:
            moved = moved + (amount >> bits_of(LANES))
        masks = [moved == offset for offset in range(1, apart + 1)]
        chosen.append((masks, lane + part & LANES - 1, place))
    for masks, index, place in chosen:
        upper = [source[offset, high, :] for offset in range(apart)]
        for tile in range(tiles):
            upper.append(source[tile + apart, high, :])
            mixed = upper[0]
            for mask, other in zip(masks, upper[1:]):
                mixed = jnp.where(mask, other, mixed)
            target[tile, place, :] = source[tile, low, :] + gathered(mixed, index)
            upper = upper[1:]


def tree_levels(state, other, columns, first, levels, held, lengths, packed=False):
    rows = columns.shape[0] // 2
    source, target = state, other
    done = 0
    while done < len(levels):
        narrow = held < SUBLANES
        bits = min(bits_of(SUBLANES // held), len(levels) - done) if narrow else len(levels) - done
        for turn in range(bits):
            level = levels[done + turn]
            inner = turn + 1 < bits
            natural = turn == 0 and not (packed and done == 0)

            def rows_in(vector, start, stride):
                return pl.ds(start, SUBLANES, stride=stride) if natural else pl.ds(vector * SUBLANES, SUBLANES)

            def rows_out(vector, start, stride):
                return pl.ds(vector * SUBLANES, SUBLANES) if inner else pl.ds(start, SUBLANES, stride=stride)

            def amounts(start, stride):
                column = columns[pl.ds(start, SUBLANES, stride=stride), :]
                one = column[:, first + done + turn : first + done + turn + 1]
                return jnp.broadcast_to(one, (SUBLANES, LANES)).astype(jnp.int32)

            if narrow:
                now = held << turn
                for band in range(SUBLANES // (2 * now)):
                    for trial in range(now):
                        low, high = 2 * band * now + trial, (2 * band + 1) * now + trial
                        outs = [band * 2 * now + 2 * trial + odd for odd in range(2)]
                        merge(
                            source,
                            target,
                            rows_in(low, low, SUBLANES),
                            rows_in(high, high, SUBLANES),
                            [(amounts(out, SUBLANES), rows_out(out, out, SUBLANES)) for out in outs],
                            lengths[done + turn],
                            2**level,
                        )
            else:
                groups, split = held // SUBLANES, 2**turn
                for band in range(rows // (2 * held * split)):
                    for group in range(groups):
                        for place in range(split):
                            low, high = [
                                ((2 * band + upper) * groups + group) * split + place for upper in range(2)
                            ]
                            outs = []
                            for odd in range(2):
                                vector = (band * groups + group) * 2 * split + 2 * place + odd
                                start = (band * groups + group) * SUBLANES * 2 * split + 2 * place + odd
                                outs.append((amounts(start, 2 * split), rows_out(vector, start, 2 * split)))
                            merge(
                                source,
                                target,
                                rows_in(low, low * SUBLANES, 1),
                                rows_in(high, high * SUBLANES, 1),
                                outs,
                                lengths[done + turn],
                                2**level,
                            )
            source, target = target, source
        held <<= bits
        done += bits
    return source


def lengths_of(made, levels):
    return [made + -(-sum(2**later for later in levels if later > level) // LANES) for level in levels]


def load_kernel(whole, copied):
    copied[...] = whole[...]


def start_kernel(whole, other, ahead):
    rows, length = whole.shape[0], ahead.shape[1]
    ahead[:rows, :] = whole[:, :length]
    ahead[rows:, :] = other[:, :length]


def placed(target, blocks, tiles, skip):
    chip, core = lax.axis_index("freq"), lax.axis_index("sub")
    rows = blocks[0].shape[1]
    for mask, block in zip(step_masks(len(blocks), core), blocks):
        start = pl.multiple_of((chip ^ mask) * rows, rows)
        for tile in range(skip, tiles):
            target[tile - skip, pl.ds(start, rows), :] = block[tile, :, :].astype(jnp.float32)


def join_kernel(*refs):
    *blocks, out, state = refs
    rows = blocks[0].shape[1]
    for tile in range(out.shape[0]):
        for index, block in enumerate(blocks):
            state[tile, index * rows : (index + 1) * rows, :] = block[tile, :, :].astype(jnp.float32)
        out[tile, :, :] = state[tile, :, :].astype(jnp.bfloat16)


def chip_kernel(spans, out_tiles, group_count, *refs):
    chan_rows = refs[0].shape[0]
    pieces = [[(refs[side], 0)] + [(ref, side * chan_rows) for ref in refs[2 : len(spans) + 1]] for side in range(2)]
    refs = refs[len(spans) + 1 :]
    local_count = bits_of(chan_rows)
    chip, core = lax.axis_index("freq"), lax.axis_index("sub")
    if group_count:
        (earlier, columns), blocks, (raw, ping, pong) = refs[:2], refs[2:-3], refs[-3:]
    else:
        shifts, rows, columns, raw, ping, pong, table = refs
        chunk = shifts[0:SUBLANES, pl.ds(pl.multiple_of(chip * LANES, LANES), LANES)]
        lane, level = lanes(), lax.broadcasted_iota(jnp.int32, (SUBLANES, LANES), 0)
        kept = lane & (1 << level) - 1
        picked = gathered(chunk, (2 * (lane - kept) + (core << level) + kept) & LANES - 1)
        transposed_table([picked[at : at + 1, :] for at in range(local_count + 1)], table, columns)
    for side in range(2):
        place = pl.multiple_of((core ^ side) * chan_rows, chan_rows)
        tile = 0
        for (piece, row), (column, length, ahead) in zip(pieces[side], spans):
            there = lax.axis_index("tm") + ahead < lax.axis_size("tm")
            for start in range(column, column + length, LANES):
                part = piece[row : row + chan_rows, start : start + LANES].astype(jnp.float32)
                if ahead:
                    part = jnp.where(there, part, 0.0)
                raw[tile, pl.ds(place, chan_rows), :] = part
                tile += 1
        for later in range(tile, raw.shape[0] - 1):
            raw[later, pl.ds(place, chan_rows), :] = jnp.zeros((chan_rows, LANES), jnp.float32)
    levels = list(range(local_count + 1))
    lengths = lengths_of(out_tiles, levels)
    mask = lanes() >= core
    for vector in range(SUBLANES):
        low, high = [pl.ds(2 * vector + odd, SUBLANES, stride=2 * SUBLANES) for odd in range(2)]
        upper = raw[0, high, :]
        for tile in range(lengths[0]):
            later = raw[tile + 1, high, :]
            moved = pltpu.roll(jnp.where(mask, upper, later), LANES - core & LANES - 1, 1)
            ping[tile, pl.ds(vector * SUBLANES, SUBLANES), :] = raw[tile, low, :] + moved
            upper = later
    last = tree_levels(ping, pong, columns, 1, levels[1:], 1, lengths[1:], packed=True)
    if not group_count:
        for tile in range(out_tiles):
            rows[tile, :, :] = last[tile, :, :]
        return
    size = chan_rows // group_count
    own = reversed_bits(chip, bits_of(group_count))
    first = earlier.shape[0]
    for mask, block in zip(step_masks(group_count, core), blocks):
        start = pl.multiple_of((own ^ reversed_bits(mask, bits_of(group_count))) * size, size)
        for tile in range(first):
            block[tile, :, :] = earlier[tile, pl.ds(start, size), :].astype(jnp.bfloat16)
        for tile in range(out_tiles):
            block[first + tile, :, :] = last[tile, pl.ds(start, size), :].astype(jnp.bfloat16)


def toeplitz(filters, target):
    width_count, tap_count = filters.shape
    lane = lax.broadcasted_iota(jnp.int32, (LANES, LANES), 1)
    row = lax.broadcasted_iota(jnp.int32, (LANES, LANES), 0)
    taps = filters[...].astype(jnp.float32)
    zeros = jnp.zeros((LANES, LANES), jnp.float32)
    for width in range(width_count):
        before = zeros
        for start in range(0, tap_count + LANES, LANES):
            if start < tap_count:
                spread = jnp.broadcast_to(taps[width : width + 1, start : start + LANES], (LANES, LANES))
                rolled = pltpu.roll(spread, 0, 1, stride=1, stride_axis=0)
            else:
                rolled = zeros
            part = jnp.where(lane >= row, rolled, before)
            target[width * LANES : (width + 1) * LANES, start : start + LANES] = part.astype(jnp.bfloat16)
            before = rolled


def table_kernel(group_count, block_rows, shifts, filters, columns, taps, table):
    level_count = shifts.shape[0]
    chip, core = lax.axis_index("freq"), lax.axis_index("sub")
    own = reversed_bits(chip * 2 + core, bits_of(group_count) + 1)
    lane = lax.broadcasted_iota(jnp.int32, (1, LANES), 1)
    rows = []
    for section in range(bits_of(group_count)):
        level = level_count - bits_of(group_count) + section
        wide = block_rows * 2 ** (section + 1)
        row = jnp.zeros((1, LANES), jnp.int32)
        for subband in range(block_rows * group_count // wide):
            start = subband * 2 ** (level + 1) + own * wide
            tile = pl.multiple_of(start >> bits_of(LANES) << bits_of(LANES), LANES)
            chunk = shifts[level : level + 1, pl.ds(tile, LANES)]
            moved = pltpu.roll(chunk, subband * wide - (start & LANES - 1) & LANES - 1, 1)
            row = jnp.where(lane >= subband * wide, moved, row)
        rows.append(row)
    transposed_table(rows, table, columns)
    toeplitz(filters, taps)


def trial_kernel(plan, group_count, level_count, scale, columns, taps, *refs):
    blocks, refs = refs[:group_count], refs[group_count:]
    halos, refs = refs[: 3 * len(plan.halos)], refs[3 * len(plan.halos) :]
    if plan.taken:
        carried, so_far, refs = refs[0], refs[1], refs[2:]
    out, refs = refs[0], refs[1:]
    if plan.given:
        handed, refs = refs[0], refs[1:]
    state, other, normal, responses, *refs = refs
    if plan.given:
        result = out
    else:
        result, arrived = refs
    chan_rows = result.shape[0]
    block_rows = chan_rows // group_count
    width_count, kept = taps.shape[0] // LANES, taps.shape[1] // LANES - 1
    levels = list(range(level_count - bits_of(group_count), level_count))
    copies = []
    if plan.taken:
        place = out.at[:, pl.ds(0, plan.out_first * LANES)]
        copies.append(pltpu.make_async_copy(so_far, place, arrived.at[len(plan.chunks)]))
        copies[0].start()
    placed(state, blocks, plan.main_tiles, plan.first)
    at = plan.main_tiles - plan.first
    chip, core = lax.axis_index("freq"), lax.axis_index("sub")
    for hop, tiles in enumerate(plan.halos, 1):
        there = lax.axis_index("tm") + hop < lax.axis_size("tm")
        for tile in range(tiles):
            joined, *single = [
                jnp.where(there, halo[tile, :, :].astype(jnp.float32), 0.0)
                for halo in halos[3 * hop - 3 : 3 * hop]
            ]
            for index, mask in enumerate(step_masks(group_count, core)):
                start = pl.multiple_of((chip ^ mask) * block_rows, block_rows)
                if index + 2 < group_count:
                    part = joined[index * block_rows : (index + 1) * block_rows]
                else:
                    part = single[index + 2 - group_count]
                state[at, pl.ds(start, block_rows), :] = part
            at += 1
    for tile in range(at, at + plan.empty_tiles):
        state[tile, :, :] = jnp.zeros((chan_rows, LANES), jnp.float32)
    last = tree_levels(state, other, columns, 0, levels, block_rows, plan.lengths)
    head = kept if plan.taken else 0
    for tile in range(head):
        normal[tile, :, :] = carried[tile, :, :]
    for tile in range(plan.made):
        normal[head + tile, :, :] = (last[tile, :, :] * scale).astype(jnp.bfloat16)
    count = plan.out_tiles
    if plan.given:
        for tile in range(kept):
            handed[tile, :, :] = normal[count + tile, :, :]
    for turn, (first_tile, some) in enumerate(plan.chunks):
        size = some * chan_rows
        windows = [
            normal[first_tile + offset : first_tile + offset + some, :, :].reshape(size, LANES)
            for offset in range(kept + 1)
        ]
        responses[0:size, :] = lax.dot_general(
            jnp.concatenate(windows, axis=1),
            taps[...],
            (((1,), (1,)), ((), ())),
            preferred_element_type=jnp.float32,
        )
        for first_row in range(0, size, PACKED):
            energies = []
            for width in range(width_count):
                one = responses[first_row : first_row + PACKED, width * LANES : (width + 1) * LANES]
                energies.append((0.5 * LOG2_E) * one * one)
            highest = functools.reduce(jnp.maximum, energies)
            total = functools.reduce(jnp.add, [jnp.exp2(energy - highest) for energy in energies])
            tile, row = first_tile + first_row // chan_rows, first_row % chan_rows
            result[row : row + PACKED, tile * LANES : (tile + 1) * LANES] = (
                jnp.log2(total) + highest
            ) * (1.0 / LOG2_E)
        if plan.given:
            continue
        columns_now = pl.ds(first_tile * LANES, some * LANES)
        place = out.at[:, pl.ds((plan.out_first + first_tile) * LANES, some * LANES)]
        copies.append(pltpu.make_async_copy(result.at[:, columns_now], place, arrived.at[turn]))
        copies[-1].start()
    for copy in copies:
        copy.wait()


class Plan:
    def __init__(self, main_tiles, halos, empty_tiles, out_first, out_tiles, taken, given, levels, tap_tiles):
        self.main_tiles, self.halos, self.empty_tiles = main_tiles, halos, empty_tiles
        self.out_first, self.out_tiles = out_first, out_tiles
        self.taken, self.given = taken, given
        self.made = out_tiles if taken else out_tiles + tap_tiles
        self.first = out_first + tap_tiles if taken else 0
        self.lengths = lengths_of(self.made, levels)
        turns = -(-out_tiles // 6)
        ends = [out_tiles * turn // turns for turn in range(turns + 1)]
        self.chunks = [(start, end - start) for start, end in zip(ends, ends[1:])]
        self.state_tiles = main_tiles + sum(halos) + empty_tiles - self.first + max(2 ** levels[-1] // LANES, 1) + 1


def local(filterbank, delay_shifts, pulse_filters):
    chan_rows, time_len = filterbank.shape
    group_count = lax.axis_size("freq")
    assert lax.axis_size("sub") == 2 and 2 * chan_rows == LANES
    level_count = delay_shifts.shape[0]
    width_count, tap_count = pulse_filters.shape
    tap_tiles = tap_count // LANES
    time_tiles = time_len // LANES
    far_levels = range(level_count - bits_of(group_count), level_count)
    near_reach = 2 ** far_levels[0] - 1
    near_len = rounded_up(near_reach, LANES)
    far_tiles = -(-(2**level_count - 1 - near_reach + tap_count) // LANES)

    in_vmem = pl.BlockSpec(memory_space=pltpu.VMEM)
    in_any = pl.BlockSpec(memory_space=pl.ANY)
    params = pltpu.CompilerParams(vmem_limit_bytes=VMEM_LIMIT)
    block_rows = chan_rows // group_count
    table = pltpu.VMEM((LANES, LANES), jnp.float32)

    def within_chip(operands, spans, raw_tiles, out_tiles, sending):
        state = pltpu.VMEM((raw_tiles + 1, chan_rows, LANES), jnp.float32)
        if sending:
            block = jax.ShapeDtypeStruct((time_tiles, block_rows, LANES), jnp.bfloat16)
            out_shape = [block] * group_count
        else:
            out_shape = [
                jax.ShapeDtypeStruct((out_tiles, chan_rows, LANES), jnp.float32),
                jax.ShapeDtypeStruct((LANES, LANES), jnp.float32),
            ]
        return pl.pallas_call(
            functools.partial(chip_kernel, spans, out_tiles, group_count if sending else 0),
            out_shape=out_shape,
            in_specs=[in_vmem] * len(operands),
            out_specs=[in_vmem] * len(out_shape),
            scratch_shapes=[pltpu.VMEM((raw_tiles + 1, 2 * chan_rows, LANES), jnp.float32), state, state]
            + ([] if sending else [table]),
            compiler_params=params,
        )(*operands)

    def between_chips(plan, blocks, halos, carried=()):
        state = pltpu.VMEM((plan.state_tiles, chan_rows, LANES), jnp.float32)
        operands = [columns, taps, *blocks, *halos, *carried]
        result = (chan_rows, plan.out_tiles * LANES)
        if plan.given:
            out_shape = [
                jax.ShapeDtypeStruct(result, jnp.float32),
                jax.ShapeDtypeStruct((tap_tiles, chan_rows, LANES), jnp.bfloat16),
            ]
            out_specs, scratch = [in_vmem] * 2, []
        else:
            out_shape, out_specs = [jax.ShapeDtypeStruct((chan_rows, time_len), jnp.float32)], [in_any]
            scratch = [pltpu.VMEM(result, jnp.float32), pltpu.SemaphoreType.DMA((len(plan.chunks) + 1,))]
        most = max(some for _, some in plan.chunks)
        scale = 1.0 / math.sqrt(delay_shifts.shape[1])
        return pl.pallas_call(
            functools.partial(trial_kernel, plan, group_count, level_count, scale),
            out_shape=out_shape,
            in_specs=[in_vmem] * len(operands),
            out_specs=out_specs,
            scratch_shapes=[
                state,
                state,
                pltpu.VMEM((plan.out_tiles + tap_tiles, chan_rows, LANES), jnp.bfloat16),
                pltpu.VMEM((most * chan_rows, width_count * LANES), jnp.float32),
            ]
            + scratch,
            compiler_params=params,
        )(*operands)

    other_core = from_partner(filterbank, "sub", 1)
    own = pl.pallas_call(
        load_kernel,
        out_shape=jax.ShapeDtypeStruct(filterbank.shape, filterbank.dtype),
        in_specs=[in_vmem],
        out_specs=in_vmem,
        compiler_params=params,
    )(filterbank)
    ahead = pl.pallas_call(
        start_kernel,
        out_shape=jax.ShapeDtypeStruct((2 * chan_rows, near_len), filterbank.dtype),
        in_specs=[in_vmem] * 2,
        out_specs=in_vmem,
        compiler_params=params,
    )(own, other_core)
    near_tiles = near_len // LANES
    early = time_tiles - near_tiles
    rows, delays = within_chip(
        [own, other_core, delay_shifts], [(0, time_len, 0)], time_tiles, early, False
    )
    operands, spans = [own, other_core], [(early * LANES, near_len, 0)]
    if lax.axis_size("tm") > 1:
        operands.append(from_ahead(ahead, 1))
        spans.append((0, near_len, 1))
    main = list(within_chip([*operands, rows, delays], spans, 2 * near_tiles, near_tiles, True))
    late_shifts, late_filters, main[0] = lax.optimization_barrier((delay_shifts, pulse_filters, main[0]))
    columns, taps = pl.pallas_call(
        functools.partial(table_kernel, group_count, block_rows),
        out_shape=[
            jax.ShapeDtypeStruct((LANES, LANES), jnp.float32),
            jax.ShapeDtypeStruct((width_count * LANES, tap_count + LANES), jnp.bfloat16),
        ],
        in_specs=[in_vmem] * 2,
        out_specs=[in_vmem] * 2,
        scratch_shapes=[table],
        compiler_params=params,
    )(late_shifts, late_filters)
    *main, last = exchanged(main)
    columns, taps, last = lax.optimization_barrier((columns, taps, last))
    main.append(last)

    halos, takes = [], []
    rest = far_tiles
    if lax.axis_size("tm") > 1:
        first_tiles = min(time_tiles, far_tiles)
        joined = pl.pallas_call(
            join_kernel,
            out_shape=jax.ShapeDtypeStruct(
                (first_tiles, chan_rows - 2 * block_rows, LANES), jnp.bfloat16
            ),
            in_specs=[in_vmem] * (group_count - 2),
            out_specs=in_vmem,
            scratch_shapes=[pltpu.VMEM((first_tiles, chan_rows - 2 * block_rows, LANES), jnp.float32)],
            compiler_params=params,
        )(*main[:-2])
        for hop in range(1, lax.axis_size("tm")):
            if rest > 0:
                takes.append(min(time_tiles, rest))
                halos.append(from_ahead(joined[: takes[-1]], hop))
                halos += [from_ahead(block[: takes[-1]], hop) for block in main[-2:]]
                rest -= takes[-1]
    lost = -(-sum(2**level for level in far_levels) // LANES) + tap_tiles
    early_tiles = time_tiles - lost
    if early_tiles <= 0:
        plan = Plan(time_tiles, takes, rest, 0, time_tiles, False, False, far_levels, tap_tiles)
        return between_chips(plan, main, halos)[0]
    plan = Plan(time_tiles, [], 0, 0, early_tiles, False, True, far_levels, tap_tiles)
    out, *carried = between_chips(plan, main, [])
    late_tiles = time_tiles - early_tiles
    plan = Plan(time_tiles, takes, rest, early_tiles, late_tiles, True, False, far_levels, tap_tiles)
    return between_chips(plan, main, halos, [*carried, out])[0]


def solution(mesh):
    in_specs = (P(("beams", "freq", "sub"), "tm"), P(), P())
    out_specs = P(("beams", "freq", "sub"), "tm")
    return jax.shard_map(local, mesh=mesh, in_specs=in_specs, out_specs=out_specs, check_vma=False)
```

```python
import functools
import math

import jax
import jax.numpy as jnp
from jax import lax
from jax.experimental import pallas as pl
from jax.experimental.pallas import tpu as pltpu
from jax.sharding import PartitionSpec as P

LANES = 128
SUBLANES = 8
PACKED = 16
SHORT = 4
LOG2_E = 1.4426950408889634
VMEM_LIMIT = 48 * 2**20


def rounded_up(value, unit):
    return -(-value // unit) * unit


def reversed_bits(value, bit_count):
    result = 0
    for bit_num in range(bit_count):
        result = result | (value >> bit_num & 1) << bit_count - 1 - bit_num
    return result


def bits_of(count):
    return count.bit_length() - 1


def from_ahead(value, steps):
    count = lax.axis_size("tm")
    return lax.ppermute(value, "tm", [((block + steps) % count, block) for block in range(count)])


def from_partner(value, axis, mask):
    count = lax.axis_size(axis)
    return lax.ppermute(value, axis, [(source, source ^ mask) for source in range(count)])


def mask_orders(group_count):
    far = list(range(group_count - 1, 1, -1))
    return [*far[:-1], 1, *far[-1:]], [*far[-1:], *far[:-1], 1]


def step_masks(group_count, core):
    orders = mask_orders(group_count)
    return [0] + [jnp.where(core == 0, first, second) for first, second in zip(*orders)]


def exchanged(blocks):
    count = lax.axis_size("freq")
    received = [blocks[0]]
    for block, masks in zip(blocks[1:], zip(*mask_orders(count))):
        route = [
            (chip * 2 + core, (chip ^ masks[core]) * 2 + core) for chip in range(count) for core in range(2)
        ]
        received.append(lax.ppermute(block, ("freq", "sub"), route))
    return received


def lanes():
    return lax.broadcasted_iota(jnp.int32, (SUBLANES, LANES), 1)


def gathered(value, index):
    return jnp.take_along_axis(value, index, axis=1, mode="promise_in_bounds")


def transposed_table(rows, table, columns):
    for index, row in enumerate(rows):
        table[index : index + 1, :] = row.astype(jnp.float32)
    columns[...] = table[...].T


def merge_short(source, target, low, high, outs, tiles, most):
    inside = [lanes() < LANES - delay for delay in range(1, most + 1)]
    chosen = [([amount == delay for delay in range(1, most + 1)], place) for amount, place in outs]

    def rolled(tile):
        value = source[tile, high, :]
        return value, [pltpu.roll(value, LANES - delay, 1) for delay in range(1, most + 1)]

    now = rolled(0)
    for tile in range(tiles):
        later = rolled(tile + 1)
        copies = [jnp.where(*parts) for parts in zip(inside, now[1], later[1])]
        lower = source[tile, low, :]
        for masks, place in chosen:
            moved = now[0]
            for mask, copy in zip(masks, copies):
                moved = jnp.where(mask, copy, moved)
            target[tile, place, :] = lower + moved
        now = later


def merge(source, target, low, high, outs, tiles, most):
    if most <= SHORT:
        return merge_short(source, target, low, high, outs, tiles, most)
    lane = lanes()
    apart = max(most // LANES, 1)
    chosen = []
    for amount, place in outs:
        part = amount if most < LANES else amount & LANES - 1
        moved = (lane < part).astype(jnp.int32)
        if most >= LANES:
            moved = moved + (amount >> bits_of(LANES))
        masks = [moved == offset for offset in range(1, apart + 1)]
        chosen.append((masks, lane + part & LANES - 1, place))
    for masks, index, place in chosen:
        upper = [source[offset, high, :] for offset in range(apart)]
        for tile in range(tiles):
            upper.append(source[tile + apart, high, :])
            mixed = upper[0]
            for mask, other in zip(masks, upper[1:]):
                mixed = jnp.where(mask, other, mixed)
            target[tile, place, :] = source[tile, low, :] + gathered(mixed, index)
            upper = upper[1:]


def tree_levels(state, other, columns, first, levels, held, lengths, packed=False):
    rows = columns.shape[0] // 2
    source, target = state, other
    done = 0
    while done < len(levels):
        narrow = held < SUBLANES
        bits = min(bits_of(SUBLANES // held), len(levels) - done) if narrow else len(levels) - done
        for turn in range(bits):
            level = levels[done + turn]
            inner = turn + 1 < bits
            natural = turn == 0 and not (packed and done == 0)

            def rows_in(vector, start, stride):
                return pl.ds(start, SUBLANES, stride=stride) if natural else pl.ds(vector * SUBLANES, SUBLANES)

            def rows_out(vector, start, stride):
                return pl.ds(vector * SUBLANES, SUBLANES) if inner else pl.ds(start, SUBLANES, stride=stride)

            def amounts(start, stride):
                column = columns[pl.ds(start, SUBLANES, stride=stride), :]
                one = column[:, first + done + turn : first + done + turn + 1]
                return jnp.broadcast_to(one, (SUBLANES, LANES)).astype(jnp.int32)

            if narrow:
                now = held << turn
                for band in range(SUBLANES // (2 * now)):
                    for trial in range(now):
                        low, high = 2 * band * now + trial, (2 * band + 1) * now + trial
                        outs = [band * 2 * now + 2 * trial + odd for odd in range(2)]
                        merge(
                            source,
                            target,
                            rows_in(low, low, SUBLANES),
                            rows_in(high, high, SUBLANES),
                            [(amounts(out, SUBLANES), rows_out(out, out, SUBLANES)) for out in outs],
                            lengths[done + turn],
                            2**level,
                        )
            else:
                groups, split = held // SUBLANES, 2**turn
                for band in range(rows // (2 * held * split)):
                    for group in range(groups):
                        for place in range(split):
                            low, high = [
                                ((2 * band + upper) * groups + group) * split + place for upper in range(2)
                            ]
                            outs = []
                            for odd in range(2):
                                vector = (band * groups + group) * 2 * split + 2 * place + odd
                                start = (band * groups + group) * SUBLANES * 2 * split + 2 * place + odd
                                outs.append((amounts(start, 2 * split), rows_out(vector, start, 2 * split)))
                            merge(
                                source,
                                target,
                                rows_in(low, low * SUBLANES, 1),
                                rows_in(high, high * SUBLANES, 1),
                                outs,
                                lengths[done + turn],
                                2**level,
                            )
            source, target = target, source
        held <<= bits
        done += bits
    return source


def lengths_of(made, levels):
    return [made + -(-sum(2**later for later in levels if later > level) // LANES) for level in levels]


def load_kernel(whole, copied):
    copied[...] = whole[...]


def start_kernel(whole, other, ahead):
    rows, length = whole.shape[0], ahead.shape[1]
    ahead[:rows, :] = whole[:, :length]
    ahead[rows:, :] = other[:, :length]


def placed(target, blocks, tiles, skip):
    chip, core = lax.axis_index("freq"), lax.axis_index("sub")
    rows = blocks[0].shape[1]
    for mask, block in zip(step_masks(len(blocks), core), blocks):
        start = pl.multiple_of((chip ^ mask) * rows, rows)
        for tile in range(skip, tiles):
            target[tile - skip, pl.ds(start, rows), :] = block[tile, :, :].astype(jnp.float32)


def join_kernel(*refs):
    *blocks, out, state = refs
    rows = blocks[0].shape[1]
    for tile in range(out.shape[0]):
        for index, block in enumerate(blocks):
            state[tile, index * rows : (index + 1) * rows, :] = block[tile, :, :].astype(jnp.float32)
        out[tile, :, :] = state[tile, :, :].astype(jnp.bfloat16)


def chip_kernel(spans, out_tiles, group_count, *refs):
    chan_rows = refs[0].shape[0]
    pieces = [[(refs[side], 0)] + [(ref, side * chan_rows) for ref in refs[2 : len(spans) + 1]] for side in range(2)]
    refs = refs[len(spans) + 1 :]
    local_count = bits_of(chan_rows)
    chip, core = lax.axis_index("freq"), lax.axis_index("sub")
    if group_count:
        (earlier, columns), blocks, (raw, ping, pong) = refs[:2], refs[2:-3], refs[-3:]
    else:
        shifts, rows, columns, raw, ping, pong, table = refs
        chunk = shifts[0:SUBLANES, pl.ds(pl.multiple_of(chip * LANES, LANES), LANES)]
        lane, level = lanes(), lax.broadcasted_iota(jnp.int32, (SUBLANES, LANES), 0)
        kept = lane & (1 << level) - 1
        picked = gathered(chunk, (2 * (lane - kept) + (core << level) + kept) & LANES - 1)
        transposed_table([picked[at : at + 1, :] for at in range(local_count + 1)], table, columns)
    for side in range(2):
        place = pl.multiple_of((core ^ side) * chan_rows, chan_rows)
        tile = 0
        for (piece, row), (column, length, ahead) in zip(pieces[side], spans):
            there = lax.axis_index("tm") + ahead < lax.axis_size("tm")
            for start in range(column, column + length, LANES):
                part = piece[row : row + chan_rows, start : start + LANES].astype(jnp.float32)
                if ahead:
                    part = jnp.where(there, part, 0.0)
                raw[tile, pl.ds(place, chan_rows), :] = part
                tile += 1
        for later in range(tile, raw.shape[0] - 1):
            raw[later, pl.ds(place, chan_rows), :] = jnp.zeros((chan_rows, LANES), jnp.float32)
    levels = list(range(local_count + 1))
    lengths = lengths_of(out_tiles, levels)
    mask = lanes() >= core
    for vector in range(SUBLANES):
        low, high = [pl.ds(2 * vector + odd, SUBLANES, stride=2 * SUBLANES) for odd in range(2)]
        upper = raw[0, high, :]
        for tile in range(lengths[0]):
            later = raw[tile + 1, high, :]
            moved = pltpu.roll(jnp.where(mask, upper, later), LANES - core & LANES - 1, 1)
            ping[tile, pl.ds(vector * SUBLANES, SUBLANES), :] = raw[tile, low, :] + moved
            upper = later
    last = tree_levels(ping, pong, columns, 1, levels[1:], 1, lengths[1:], packed=True)
    if not group_count:
        for tile in range(out_tiles):
            rows[tile, :, :] = last[tile, :, :]
        return
    size = chan_rows // group_count
    own = reversed_bits(chip, bits_of(group_count))
    first = earlier.shape[0]
    for mask, block in zip(step_masks(group_count, core), blocks):
        start = pl.multiple_of((own ^ reversed_bits(mask, bits_of(group_count))) * size, size)
        for tile in range(first):
            block[tile, :, :] = earlier[tile, pl.ds(start, size), :].astype(jnp.bfloat16)
        for tile in range(out_tiles):
            block[first + tile, :, :] = last[tile, pl.ds(start, size), :].astype(jnp.bfloat16)


def toeplitz(filters, target):
    width_count, tap_count = filters.shape
    lane = lax.broadcasted_iota(jnp.int32, (LANES, LANES), 1)
    row = lax.broadcasted_iota(jnp.int32, (LANES, LANES), 0)
    taps = filters[...].astype(jnp.float32)
    zeros = jnp.zeros((LANES, LANES), jnp.float32)
    for width in range(width_count):
        before = zeros
        for start in range(0, tap_count + LANES, LANES):
            if start < tap_count:
                spread = jnp.broadcast_to(taps[width : width + 1, start : start + LANES], (LANES, LANES))
                rolled = pltpu.roll(spread, 0, 1, stride=1, stride_axis=0)
            else:
                rolled = zeros
            part = jnp.where(lane >= row, rolled, before)
            target[width * LANES : (width + 1) * LANES, start : start + LANES] = part.astype(jnp.bfloat16)
            before = rolled


def table_kernel(group_count, block_rows, shifts, filters, columns, taps, table):
    level_count = shifts.shape[0]
    chip, core = lax.axis_index("freq"), lax.axis_index("sub")
    own = reversed_bits(chip * 2 + core, bits_of(group_count) + 1)
    lane = lax.broadcasted_iota(jnp.int32, (1, LANES), 1)
    rows = []
    for section in range(bits_of(group_count)):
        level = level_count - bits_of(group_count) + section
        wide = block_rows * 2 ** (section + 1)
        row = jnp.zeros((1, LANES), jnp.int32)
        for subband in range(block_rows * group_count // wide):
            start = subband * 2 ** (level + 1) + own * wide
            tile = pl.multiple_of(start >> bits_of(LANES) << bits_of(LANES), LANES)
            chunk = shifts[level : level + 1, pl.ds(tile, LANES)]
            moved = pltpu.roll(chunk, subband * wide - (start & LANES - 1) & LANES - 1, 1)
            row = jnp.where(lane >= subband * wide, moved, row)
        rows.append(row)
    transposed_table(rows, table, columns)
    toeplitz(filters, taps)


def trial_kernel(plan, group_count, level_count, scale, columns, taps, *refs):
    blocks, refs = refs[:group_count], refs[group_count:]
    halos, refs = refs[: 2 * len(plan.halos)], refs[2 * len(plan.halos) :]
    if plan.taken:
        carried, so_far, refs = refs[0], refs[1], refs[2:]
    out, refs = refs[0], refs[1:]
    if plan.given:
        handed, refs = refs[0], refs[1:]
    state, other, normal, responses, *refs = refs
    if plan.given:
        result = out
    else:
        result, arrived = refs
    chan_rows = result.shape[0]
    block_rows = chan_rows // group_count
    width_count, kept = taps.shape[0] // LANES, taps.shape[1] // LANES - 1
    levels = list(range(level_count - bits_of(group_count), level_count))
    copies = []
    if plan.taken:
        place = out.at[:, pl.ds(0, plan.out_first * LANES)]
        copies.append(pltpu.make_async_copy(so_far, place, arrived.at[len(plan.chunks)]))
        copies[0].start()
    placed(state, blocks, plan.main_tiles, plan.first)
    at = plan.main_tiles - plan.first
    chip, core = lax.axis_index("freq"), lax.axis_index("sub")
    for hop, tiles in enumerate(plan.halos, 1):
        there = lax.axis_index("tm") + hop < lax.axis_size("tm")
        for tile in range(tiles):
            joined, single = [
                jnp.where(there, halo[tile, :, :].astype(jnp.float32), 0.0)
                for halo in halos[2 * hop - 2 : 2 * hop]
            ]
            for index, mask in enumerate(step_masks(group_count, core)):
                start = pl.multiple_of((chip ^ mask) * block_rows, block_rows)
                if index + 1 < group_count:
                    part = joined[index * block_rows : (index + 1) * block_rows]
                else:
                    part = single
                state[at, pl.ds(start, block_rows), :] = part
            at += 1
    for tile in range(at, at + plan.empty_tiles):
        state[tile, :, :] = jnp.zeros((chan_rows, LANES), jnp.float32)
    last = tree_levels(state, other, columns, 0, levels, block_rows, plan.lengths)
    head = kept if plan.taken else 0
    for tile in range(head):
        normal[tile, :, :] = carried[tile, :, :]
    for tile in range(plan.made):
        normal[head + tile, :, :] = (last[tile, :, :] * scale).astype(jnp.bfloat16)
    count = plan.out_tiles
    if plan.given:
        for tile in range(kept):
            handed[tile, :, :] = normal[count + tile, :, :]
    for turn, (first_tile, some) in enumerate(plan.chunks):
        size = some * chan_rows
        windows = [
            normal[first_tile + offset : first_tile + offset + some, :, :].reshape(size, LANES)
            for offset in range(kept + 1)
        ]
        responses[0:size, :] = lax.dot_general(
            jnp.concatenate(windows, axis=1),
            taps[...],
            (((1,), (1,)), ((), ())),
            preferred_element_type=jnp.float32,
        )
        for first_row in range(0, size, PACKED):
            energies = []
            for width in range(width_count):
                one = responses[first_row : first_row + PACKED, width * LANES : (width + 1) * LANES]
                energies.append((0.5 * LOG2_E) * one * one)
            highest = functools.reduce(jnp.maximum, energies)
            total = functools.reduce(jnp.add, [jnp.exp2(energy - highest) for energy in energies])
            tile, row = first_tile + first_row // chan_rows, first_row % chan_rows
            result[row : row + PACKED, tile * LANES : (tile + 1) * LANES] = (
                jnp.log2(total) + highest
            ) * (1.0 / LOG2_E)
        if plan.given:
            continue
        columns_now = pl.ds(first_tile * LANES, some * LANES)
        place = out.at[:, pl.ds((plan.out_first + first_tile) * LANES, some * LANES)]
        copies.append(pltpu.make_async_copy(result.at[:, columns_now], place, arrived.at[turn]))
        copies[-1].start()
    for copy in copies:
        copy.wait()


class Plan:
    def __init__(self, main_tiles, halos, empty_tiles, out_first, out_tiles, taken, given, levels, tap_tiles):
        self.main_tiles, self.halos, self.empty_tiles = main_tiles, halos, empty_tiles
        self.out_first, self.out_tiles = out_first, out_tiles
        self.taken, self.given = taken, given
        self.made = out_tiles if taken else out_tiles + tap_tiles
        self.first = out_first + tap_tiles if taken else 0
        self.lengths = lengths_of(self.made, levels)
        turns = -(-out_tiles // 6)
        ends = [out_tiles * turn // turns for turn in range(turns + 1)]
        self.chunks = [(start, end - start) for start, end in zip(ends, ends[1:])]
        self.state_tiles = main_tiles + sum(halos) + empty_tiles - self.first + max(2 ** levels[-1] // LANES, 1) + 1


def local(filterbank, delay_shifts, pulse_filters):
    chan_rows, time_len = filterbank.shape
    group_count = lax.axis_size("freq")
    assert lax.axis_size("sub") == 2 and 2 * chan_rows == LANES
    level_count = delay_shifts.shape[0]
    width_count, tap_count = pulse_filters.shape
    tap_tiles = tap_count // LANES
    time_tiles = time_len // LANES
    far_levels = range(level_count - bits_of(group_count), level_count)
    near_reach = 2 ** far_levels[0] - 1
    near_len = rounded_up(near_reach, LANES)
    far_tiles = -(-(2**level_count - 1 - near_reach + tap_count) // LANES)

    in_vmem = pl.BlockSpec(memory_space=pltpu.VMEM)
    in_any = pl.BlockSpec(memory_space=pl.ANY)
    params = pltpu.CompilerParams(vmem_limit_bytes=VMEM_LIMIT)
    block_rows = chan_rows // group_count
    table = pltpu.VMEM((LANES, LANES), jnp.float32)

    def within_chip(operands, spans, raw_tiles, out_tiles, sending):
        state = pltpu.VMEM((raw_tiles + 1, chan_rows, LANES), jnp.float32)
        if sending:
            block = jax.ShapeDtypeStruct((time_tiles, block_rows, LANES), jnp.bfloat16)
            out_shape = [block] * group_count
        else:
            out_shape = [
                jax.ShapeDtypeStruct((out_tiles, chan_rows, LANES), jnp.float32),
                jax.ShapeDtypeStruct((LANES, LANES), jnp.float32),
            ]
        return pl.pallas_call(
            functools.partial(chip_kernel, spans, out_tiles, group_count if sending else 0),
            out_shape=out_shape,
            in_specs=[in_vmem] * len(operands),
            out_specs=[in_vmem] * len(out_shape),
            scratch_shapes=[pltpu.VMEM((raw_tiles + 1, 2 * chan_rows, LANES), jnp.float32), state, state]
            + ([] if sending else [table]),
            compiler_params=params,
        )(*operands)

    def between_chips(plan, blocks, halos, carried=()):
        state = pltpu.VMEM((plan.state_tiles, chan_rows, LANES), jnp.float32)
        operands = [columns, taps, *blocks, *halos, *carried]
        result = (chan_rows, plan.out_tiles * LANES)
        if plan.given:
            out_shape = [
                jax.ShapeDtypeStruct(result, jnp.float32),
                jax.ShapeDtypeStruct((tap_tiles, chan_rows, LANES), jnp.bfloat16),
            ]
            out_specs, scratch = [in_vmem] * 2, []
        else:
            out_shape, out_specs = [jax.ShapeDtypeStruct((chan_rows, time_len), jnp.float32)], [in_any]
            scratch = [pltpu.VMEM(result, jnp.float32), pltpu.SemaphoreType.DMA((len(plan.chunks) + 1,))]
        most = max(some for _, some in plan.chunks)
        scale = 1.0 / math.sqrt(delay_shifts.shape[1])
        return pl.pallas_call(
            functools.partial(trial_kernel, plan, group_count, level_count, scale),
            out_shape=out_shape,
            in_specs=[in_vmem] * len(operands),
            out_specs=out_specs,
            scratch_shapes=[
                state,
                state,
                pltpu.VMEM((plan.out_tiles + tap_tiles, chan_rows, LANES), jnp.bfloat16),
                pltpu.VMEM((most * chan_rows, width_count * LANES), jnp.float32),
            ]
            + scratch,
            compiler_params=params,
        )(*operands)

    other_core = from_partner(filterbank, "sub", 1)
    own = pl.pallas_call(
        load_kernel,
        out_shape=jax.ShapeDtypeStruct(filterbank.shape, filterbank.dtype),
        in_specs=[in_vmem],
        out_specs=in_vmem,
        compiler_params=params,
    )(filterbank)
    ahead = pl.pallas_call(
        start_kernel,
        out_shape=jax.ShapeDtypeStruct((2 * chan_rows, near_len), filterbank.dtype),
        in_specs=[in_vmem] * 2,
        out_specs=in_vmem,
        compiler_params=params,
    )(own, other_core)
    near_tiles = near_len // LANES
    early = time_tiles - near_tiles
    rows, delays = within_chip(
        [own, other_core, delay_shifts], [(0, time_len, 0)], time_tiles, early, False
    )
    operands, spans = [own, other_core], [(early * LANES, near_len, 0)]
    if lax.axis_size("tm") > 1:
        operands.append(from_ahead(ahead, 1))
        spans.append((0, near_len, 1))
    main = list(within_chip([*operands, rows, delays], spans, 2 * near_tiles, near_tiles, True))
    late_shifts, late_filters, main[0] = lax.optimization_barrier((delay_shifts, pulse_filters, main[0]))
    columns, taps = pl.pallas_call(
        functools.partial(table_kernel, group_count, block_rows),
        out_shape=[
            jax.ShapeDtypeStruct((LANES, LANES), jnp.float32),
            jax.ShapeDtypeStruct((width_count * LANES, tap_count + LANES), jnp.bfloat16),
        ],
        in_specs=[in_vmem] * 2,
        out_specs=[in_vmem] * 2,
        scratch_shapes=[table],
        compiler_params=params,
    )(late_shifts, late_filters)
    *main, last = exchanged(main)
    columns, taps, last = lax.optimization_barrier((columns, taps, last))
    main.append(last)

    halos, takes = [], []
    rest = far_tiles
    if lax.axis_size("tm") > 1:
        first_tiles = min(time_tiles, far_tiles)
        joined = pl.pallas_call(
            join_kernel,
            out_shape=jax.ShapeDtypeStruct(
                (first_tiles, chan_rows - block_rows, LANES), jnp.bfloat16
            ),
            in_specs=[in_vmem] * (group_count - 1),
            out_specs=in_vmem,
            scratch_shapes=[pltpu.VMEM((first_tiles, chan_rows - block_rows, LANES), jnp.float32)],
            compiler_params=params,
        )(*main[:-1])
        for hop in range(1, lax.axis_size("tm")):
            if rest > 0:
                takes.append(min(time_tiles, rest))
                halos.append(from_ahead(joined[: takes[-1]], hop))
                halos.append(from_ahead(main[-1][: takes[-1]], hop))
                rest -= takes[-1]
    lost = -(-sum(2**level for level in far_levels) // LANES) + tap_tiles
    early_tiles = time_tiles - lost
    if early_tiles <= 0:
        plan = Plan(time_tiles, takes, rest, 0, time_tiles, False, False, far_levels, tap_tiles)
        return between_chips(plan, main, halos)[0]
    plan = Plan(time_tiles, [], 0, 0, early_tiles, False, True, far_levels, tap_tiles)
    out, *carried = between_chips(plan, main, [])
    late_tiles = time_tiles - early_tiles
    plan = Plan(time_tiles, takes, rest, early_tiles, late_tiles, True, False, far_levels, tap_tiles)
    return between_chips(plan, main, halos, [*carried, out])[0]


def solution(mesh):
    in_specs = (P(("beams", "freq", "sub"), "tm"), P(), P())
    out_specs = P(("beams", "freq", "sub"), "tm")
    return jax.shard_map(local, mesh=mesh, in_specs=in_specs, out_specs=out_specs, check_vma=False)
```

```python
import functools
import math

import jax
import jax.numpy as jnp
from jax import lax
from jax.experimental import pallas as pl
from jax.experimental.pallas import tpu as pltpu
from jax.sharding import PartitionSpec as P

LANES = 128
SUBLANES = 8
PACKED = 16
SHORT = 4
LOG2_E = 1.4426950408889634
VMEM_LIMIT = 48 * 2**20


def rounded_up(value, unit):
    return -(-value // unit) * unit


def reversed_bits(value, bit_count):
    result = 0
    for bit_num in range(bit_count):
        result = result | (value >> bit_num & 1) << bit_count - 1 - bit_num
    return result


def bits_of(count):
    return count.bit_length() - 1


def from_ahead(value, steps):
    count = lax.axis_size("tm")
    return lax.ppermute(value, "tm", [((block + steps) % count, block) for block in range(count)])


def from_partner(value, axis, mask):
    count = lax.axis_size(axis)
    return lax.ppermute(value, axis, [(source, source ^ mask) for source in range(count)])


def mask_orders(group_count):
    far = list(range(group_count - 1, 1, -1))
    return [*far[:-1], 1, *far[-1:]], [*far[-1:], *far[:-1], 1]


def step_masks(group_count, core):
    orders = mask_orders(group_count)
    return [0] + [jnp.where(core == 0, first, second) for first, second in zip(*orders)]


def exchanged(blocks, cut):
    count = lax.axis_size("freq")
    received = [(0, 0, blocks[0])]
    for step, masks in enumerate(zip(*mask_orders(count)), 1):
        route = [
            (chip * 2 + core, (chip ^ masks[core]) * 2 + core) for chip in range(count) for core in range(2)
        ]
        tiles = blocks[step].shape[0]
        ends = [0, cut, tiles] if step + 1 == count and 0 < cut < tiles else [0, tiles]
        for first, end in zip(ends, ends[1:]):
            received.append((step, first, lax.ppermute(blocks[step][first:end], ("freq", "sub"), route)))
    return received


def lanes():
    return lax.broadcasted_iota(jnp.int32, (SUBLANES, LANES), 1)


def gathered(value, index):
    return jnp.take_along_axis(value, index, axis=1, mode="promise_in_bounds")


def transposed_table(rows, table, columns):
    for index, row in enumerate(rows):
        table[index : index + 1, :] = row.astype(jnp.float32)
    columns[...] = table[...].T


def merge_short(source, target, low, high, outs, tiles, most):
    inside = [lanes() < LANES - delay for delay in range(1, most + 1)]
    chosen = [([amount == delay for delay in range(1, most + 1)], place) for amount, place in outs]

    def rolled(tile):
        value = source[tile, high, :]
        return value, [pltpu.roll(value, LANES - delay, 1) for delay in range(1, most + 1)]

    now = rolled(0)
    for tile in range(tiles):
        later = rolled(tile + 1)
        copies = [jnp.where(*parts) for parts in zip(inside, now[1], later[1])]
        lower = source[tile, low, :]
        for masks, place in chosen:
            moved = now[0]
            for mask, copy in zip(masks, copies):
                moved = jnp.where(mask, copy, moved)
            target[tile, place, :] = lower + moved
        now = later


def merge(source, target, low, high, outs, tiles, most):
    if most <= SHORT:
        return merge_short(source, target, low, high, outs, tiles, most)
    lane = lanes()
    apart = max(most // LANES, 1)
    chosen = []
    for amount, place in outs:
        part = amount if most < LANES else amount & LANES - 1
        moved = (lane < part).astype(jnp.int32)
        if most >= LANES:
            moved = moved + (amount >> bits_of(LANES))
        masks = [moved == offset for offset in range(1, apart + 1)]
        chosen.append((masks, lane + part & LANES - 1, place))
    for masks, index, place in chosen:
        upper = [source[offset, high, :] for offset in range(apart)]
        for tile in range(tiles):
            upper.append(source[tile + apart, high, :])
            mixed = upper[0]
            for mask, other in zip(masks, upper[1:]):
                mixed = jnp.where(mask, other, mixed)
            target[tile, place, :] = source[tile, low, :] + gathered(mixed, index)
            upper = upper[1:]


def tree_levels(state, other, columns, first, levels, held, lengths, packed=False):
    rows = columns.shape[0] // 2
    source, target = state, other
    done = 0
    while done < len(levels):
        narrow = held < SUBLANES
        bits = min(bits_of(SUBLANES // held), len(levels) - done) if narrow else len(levels) - done
        for turn in range(bits):
            level = levels[done + turn]
            inner = turn + 1 < bits
            natural = turn == 0 and not (packed and done == 0)

            def rows_in(vector, start, stride):
                return pl.ds(start, SUBLANES, stride=stride) if natural else pl.ds(vector * SUBLANES, SUBLANES)

            def rows_out(vector, start, stride):
                return pl.ds(vector * SUBLANES, SUBLANES) if inner else pl.ds(start, SUBLANES, stride=stride)

            def amounts(start, stride):
                column = columns[pl.ds(start, SUBLANES, stride=stride), :]
                one = column[:, first + done + turn : first + done + turn + 1]
                return jnp.broadcast_to(one, (SUBLANES, LANES)).astype(jnp.int32)

            if narrow:
                now = held << turn
                for band in range(SUBLANES // (2 * now)):
                    for trial in range(now):
                        low, high = 2 * band * now + trial, (2 * band + 1) * now + trial
                        outs = [band * 2 * now + 2 * trial + odd for odd in range(2)]
                        merge(
                            source,
                            target,
                            rows_in(low, low, SUBLANES),
                            rows_in(high, high, SUBLANES),
                            [(amounts(out, SUBLANES), rows_out(out, out, SUBLANES)) for out in outs],
                            lengths[done + turn],
                            2**level,
                        )
            else:
                groups, split = held // SUBLANES, 2**turn
                for band in range(rows // (2 * held * split)):
                    for group in range(groups):
                        for place in range(split):
                            low, high = [
                                ((2 * band + upper) * groups + group) * split + place for upper in range(2)
                            ]
                            outs = []
                            for odd in range(2):
                                vector = (band * groups + group) * 2 * split + 2 * place + odd
                                start = (band * groups + group) * SUBLANES * 2 * split + 2 * place + odd
                                outs.append((amounts(start, 2 * split), rows_out(vector, start, 2 * split)))
                            merge(
                                source,
                                target,
                                rows_in(low, low * SUBLANES, 1),
                                rows_in(high, high * SUBLANES, 1),
                                outs,
                                lengths[done + turn],
                                2**level,
                            )
            source, target = target, source
        held <<= bits
        done += bits
    return source


def lengths_of(made, levels):
    return [made + -(-sum(2**later for later in levels if later > level) // LANES) for level in levels]


def load_kernel(whole, copied):
    copied[...] = whole[...]


def start_kernel(whole, other, ahead):
    rows, length = whole.shape[0], ahead.shape[1]
    ahead[:rows, :] = whole[:, :length]
    ahead[rows:, :] = other[:, :length]


def placed(target, blocks, group_count, skip):
    chip, core = lax.axis_index("freq"), lax.axis_index("sub")
    masks = step_masks(group_count, core)
    for step, first, block in blocks:
        tiles, rows = block.shape[:2]
        start = pl.multiple_of((chip ^ masks[step]) * rows, rows)
        for tile in range(max(skip - first, 0), tiles):
            target[first + tile - skip, pl.ds(start, rows), :] = block[tile, :, :].astype(jnp.float32)


def join_kernel(*refs):
    *blocks, out, state = refs
    rows = blocks[0].shape[1]
    for tile in range(out.shape[0]):
        for index, block in enumerate(blocks):
            state[tile, index * rows : (index + 1) * rows, :] = block[tile, :, :].astype(jnp.float32)
        out[tile, :, :] = state[tile, :, :].astype(jnp.bfloat16)


def chip_kernel(spans, out_tiles, group_count, *refs):
    chan_rows = refs[0].shape[0]
    pieces = [[(refs[side], 0)] + [(ref, side * chan_rows) for ref in refs[2 : len(spans) + 1]] for side in range(2)]
    refs = refs[len(spans) + 1 :]
    local_count = bits_of(chan_rows)
    chip, core = lax.axis_index("freq"), lax.axis_index("sub")
    if group_count:
        (earlier, columns), blocks, (raw, ping, pong) = refs[:2], refs[2:-3], refs[-3:]
    else:
        shifts, rows, columns, raw, ping, pong, table = refs
        chunk = shifts[0:SUBLANES, pl.ds(pl.multiple_of(chip * LANES, LANES), LANES)]
        lane, level = lanes(), lax.broadcasted_iota(jnp.int32, (SUBLANES, LANES), 0)
        kept = lane & (1 << level) - 1
        picked = gathered(chunk, (2 * (lane - kept) + (core << level) + kept) & LANES - 1)
        transposed_table([picked[at : at + 1, :] for at in range(local_count + 1)], table, columns)
    for side in range(2):
        place = pl.multiple_of((core ^ side) * chan_rows, chan_rows)
        tile = 0
        for (piece, row), (column, length, ahead) in zip(pieces[side], spans):
            there = lax.axis_index("tm") + ahead < lax.axis_size("tm")
            for start in range(column, column + length, LANES):
                part = piece[row : row + chan_rows, start : start + LANES].astype(jnp.float32)
                if ahead:
                    part = jnp.where(there, part, 0.0)
                raw[tile, pl.ds(place, chan_rows), :] = part
                tile += 1
        for later in range(tile, raw.shape[0] - 1):
            raw[later, pl.ds(place, chan_rows), :] = jnp.zeros((chan_rows, LANES), jnp.float32)
    levels = list(range(local_count + 1))
    lengths = lengths_of(out_tiles, levels)
    mask = lanes() >= core
    for vector in range(SUBLANES):
        low, high = [pl.ds(2 * vector + odd, SUBLANES, stride=2 * SUBLANES) for odd in range(2)]
        upper = raw[0, high, :]
        for tile in range(lengths[0]):
            later = raw[tile + 1, high, :]
            moved = pltpu.roll(jnp.where(mask, upper, later), LANES - core & LANES - 1, 1)
            ping[tile, pl.ds(vector * SUBLANES, SUBLANES), :] = raw[tile, low, :] + moved
            upper = later
    last = tree_levels(ping, pong, columns, 1, levels[1:], 1, lengths[1:], packed=True)
    if not group_count:
        for tile in range(out_tiles):
            rows[tile, :, :] = last[tile, :, :]
        return
    size = chan_rows // group_count
    own = reversed_bits(chip, bits_of(group_count))
    first = earlier.shape[0]
    for mask, block in zip(step_masks(group_count, core), blocks):
        start = pl.multiple_of((own ^ reversed_bits(mask, bits_of(group_count))) * size, size)
        for tile in range(first):
            block[tile, :, :] = earlier[tile, pl.ds(start, size), :].astype(jnp.bfloat16)
        for tile in range(out_tiles):
            block[first + tile, :, :] = last[tile, pl.ds(start, size), :].astype(jnp.bfloat16)


def toeplitz(filters, target):
    width_count, tap_count = filters.shape
    lane = lax.broadcasted_iota(jnp.int32, (LANES, LANES), 1)
    row = lax.broadcasted_iota(jnp.int32, (LANES, LANES), 0)
    taps = filters[...].astype(jnp.float32)
    zeros = jnp.zeros((LANES, LANES), jnp.float32)
    for width in range(width_count):
        before = zeros
        for start in range(0, tap_count + LANES, LANES):
            if start < tap_count:
                spread = jnp.broadcast_to(taps[width : width + 1, start : start + LANES], (LANES, LANES))
                rolled = pltpu.roll(spread, 0, 1, stride=1, stride_axis=0)
            else:
                rolled = zeros
            part = jnp.where(lane >= row, rolled, before)
            target[width * LANES : (width + 1) * LANES, start : start + LANES] = part.astype(jnp.bfloat16)
            before = rolled


def table_kernel(group_count, block_rows, shifts, filters, columns, taps, table):
    level_count = shifts.shape[0]
    chip, core = lax.axis_index("freq"), lax.axis_index("sub")
    own = reversed_bits(chip * 2 + core, bits_of(group_count) + 1)
    lane = lax.broadcasted_iota(jnp.int32, (1, LANES), 1)
    rows = []
    for section in range(bits_of(group_count)):
        level = level_count - bits_of(group_count) + section
        wide = block_rows * 2 ** (section + 1)
        row = jnp.zeros((1, LANES), jnp.int32)
        for subband in range(block_rows * group_count // wide):
            start = subband * 2 ** (level + 1) + own * wide
            tile = pl.multiple_of(start >> bits_of(LANES) << bits_of(LANES), LANES)
            chunk = shifts[level : level + 1, pl.ds(tile, LANES)]
            moved = pltpu.roll(chunk, subband * wide - (start & LANES - 1) & LANES - 1, 1)
            row = jnp.where(lane >= subband * wide, moved, row)
        rows.append(row)
    transposed_table(rows, table, columns)
    toeplitz(filters, taps)


def trial_kernel(plan, group_count, level_count, scale, columns, taps, *refs):
    blocks, refs = refs[: len(plan.pieces)], refs[len(plan.pieces) :]
    halos, refs = refs[: 2 * len(plan.halos)], refs[2 * len(plan.halos) :]
    if plan.taken:
        carried, so_far, refs = refs[0], refs[1], refs[2:]
    out, refs = refs[0], refs[1:]
    if plan.given:
        handed, refs = refs[0], refs[1:]
    state, other, normal, responses, *refs = refs
    if plan.given:
        result = out
    else:
        result, arrived = refs
    chan_rows = result.shape[0]
    block_rows = chan_rows // group_count
    width_count, kept = taps.shape[0] // LANES, taps.shape[1] // LANES - 1
    levels = list(range(level_count - bits_of(group_count), level_count))
    copies = []
    if plan.taken:
        place = out.at[:, pl.ds(0, plan.out_first * LANES)]
        copies.append(pltpu.make_async_copy(so_far, place, arrived.at[len(plan.chunks)]))
        copies[0].start()
    pieces = [(step, first, block) for (step, first), block in zip(plan.pieces, blocks)]
    placed(state, pieces, group_count, plan.first)
    at = plan.main_tiles - plan.first
    chip, core = lax.axis_index("freq"), lax.axis_index("sub")
    for hop, tiles in enumerate(plan.halos, 1):
        there = lax.axis_index("tm") + hop < lax.axis_size("tm")
        for tile in range(tiles):
            joined = [
                jnp.where(there, halo[tile, :, :].astype(jnp.float32), 0.0)
                for halo in halos[2 * hop - 2 : 2 * hop]
            ]
            parts = [
                value[row : row + block_rows] for value in joined for row in range(0, value.shape[0], block_rows)
            ]
            for part, mask in zip(parts, step_masks(group_count, core)):
                start = pl.multiple_of((chip ^ mask) * block_rows, block_rows)
                state[at, pl.ds(start, block_rows), :] = part
            at += 1
    for tile in range(at, at + plan.empty_tiles):
        state[tile, :, :] = jnp.zeros((chan_rows, LANES), jnp.float32)
    last = tree_levels(state, other, columns, 0, levels, block_rows, plan.lengths)
    head = kept if plan.taken else 0
    for tile in range(head):
        normal[tile, :, :] = carried[tile, :, :]
    for tile in range(plan.made):
        normal[head + tile, :, :] = (last[tile, :, :] * scale).astype(jnp.bfloat16)
    count = plan.out_tiles
    if plan.given:
        for tile in range(kept):
            handed[tile, :, :] = normal[count + tile, :, :]
    for turn, (first_tile, some) in enumerate(plan.chunks):
        size = some * chan_rows
        windows = [
            normal[first_tile + offset : first_tile + offset + some, :, :].reshape(size, LANES)
            for offset in range(kept + 1)
        ]
        responses[0:size, :] = lax.dot_general(
            jnp.concatenate(windows, axis=1),
            taps[...],
            (((1,), (1,)), ((), ())),
            preferred_element_type=jnp.float32,
        )
        for first_row in range(0, size, PACKED):
            energies = []
            for width in range(width_count):
                one = responses[first_row : first_row + PACKED, width * LANES : (width + 1) * LANES]
                energies.append((0.5 * LOG2_E) * one * one)
            highest = functools.reduce(jnp.maximum, energies)
            total = functools.reduce(jnp.add, [jnp.exp2(energy - highest) for energy in energies])
            tile, row = first_tile + first_row // chan_rows, first_row % chan_rows
            result[row : row + PACKED, tile * LANES : (tile + 1) * LANES] = (
                jnp.log2(total) + highest
            ) * (1.0 / LOG2_E)
        if plan.given:
            continue
        columns_now = pl.ds(first_tile * LANES, some * LANES)
        place = out.at[:, pl.ds((plan.out_first + first_tile) * LANES, some * LANES)]
        copies.append(pltpu.make_async_copy(result.at[:, columns_now], place, arrived.at[turn]))
        copies[-1].start()
    for copy in copies:
        copy.wait()


class Plan:
    def __init__(self, pieces, main_tiles, halos, empty_tiles, out_first, out_tiles, taken, given, levels, tap_tiles):
        self.pieces = pieces
        self.main_tiles, self.halos, self.empty_tiles = main_tiles, halos, empty_tiles
        self.out_first, self.out_tiles = out_first, out_tiles
        self.taken, self.given = taken, given
        self.made = out_tiles if taken else out_tiles + tap_tiles
        self.first = out_first + tap_tiles if taken else 0
        self.lengths = lengths_of(self.made, levels)
        turns = -(-out_tiles // 6)
        ends = [out_tiles * turn // turns for turn in range(turns + 1)]
        self.chunks = [(start, end - start) for start, end in zip(ends, ends[1:])]
        self.state_tiles = main_tiles + sum(halos) + empty_tiles - self.first + max(2 ** levels[-1] // LANES, 1) + 1


def local(filterbank, delay_shifts, pulse_filters):
    chan_rows, time_len = filterbank.shape
    group_count = lax.axis_size("freq")
    assert lax.axis_size("sub") == 2 and 2 * chan_rows == LANES
    level_count = delay_shifts.shape[0]
    width_count, tap_count = pulse_filters.shape
    tap_tiles = tap_count // LANES
    time_tiles = time_len // LANES
    far_levels = range(level_count - bits_of(group_count), level_count)
    near_reach = 2 ** far_levels[0] - 1
    near_len = rounded_up(near_reach, LANES)
    far_tiles = -(-(2**level_count - 1 - near_reach + tap_count) // LANES)

    in_vmem = pl.BlockSpec(memory_space=pltpu.VMEM)
    in_any = pl.BlockSpec(memory_space=pl.ANY)
    params = pltpu.CompilerParams(vmem_limit_bytes=VMEM_LIMIT)
    block_rows = chan_rows // group_count
    table = pltpu.VMEM((LANES, LANES), jnp.float32)

    def within_chip(operands, spans, raw_tiles, out_tiles, sending):
        state = pltpu.VMEM((raw_tiles + 1, chan_rows, LANES), jnp.float32)
        if sending:
            block = jax.ShapeDtypeStruct((time_tiles, block_rows, LANES), jnp.bfloat16)
            out_shape = [block] * group_count
        else:
            out_shape = [
                jax.ShapeDtypeStruct((out_tiles, chan_rows, LANES), jnp.float32),
                jax.ShapeDtypeStruct((LANES, LANES), jnp.float32),
            ]
        return pl.pallas_call(
            functools.partial(chip_kernel, spans, out_tiles, group_count if sending else 0),
            out_shape=out_shape,
            in_specs=[in_vmem] * len(operands),
            out_specs=[in_vmem] * len(out_shape),
            scratch_shapes=[pltpu.VMEM((raw_tiles + 1, 2 * chan_rows, LANES), jnp.float32), state, state]
            + ([] if sending else [table]),
            compiler_params=params,
        )(*operands)

    def between_chips(plan, blocks, halos, carried=()):
        state = pltpu.VMEM((plan.state_tiles, chan_rows, LANES), jnp.float32)
        operands = [columns, taps, *blocks, *halos, *carried]
        result = (chan_rows, plan.out_tiles * LANES)
        if plan.given:
            out_shape = [
                jax.ShapeDtypeStruct(result, jnp.float32),
                jax.ShapeDtypeStruct((tap_tiles, chan_rows, LANES), jnp.bfloat16),
            ]
            out_specs, scratch = [in_vmem] * 2, []
        else:
            out_shape, out_specs = [jax.ShapeDtypeStruct((chan_rows, time_len), jnp.float32)], [in_any]
            scratch = [pltpu.VMEM(result, jnp.float32), pltpu.SemaphoreType.DMA((len(plan.chunks) + 1,))]
        most = max(some for _, some in plan.chunks)
        scale = 1.0 / math.sqrt(delay_shifts.shape[1])
        return pl.pallas_call(
            functools.partial(trial_kernel, plan, group_count, level_count, scale),
            out_shape=out_shape,
            in_specs=[in_vmem] * len(operands),
            out_specs=out_specs,
            scratch_shapes=[
                state,
                state,
                pltpu.VMEM((plan.out_tiles + tap_tiles, chan_rows, LANES), jnp.bfloat16),
                pltpu.VMEM((most * chan_rows, width_count * LANES), jnp.float32),
            ]
            + scratch,
            compiler_params=params,
            cost_estimate=pl.CostEstimate(
                flops=2 * plan.out_tiles * LANES * chan_rows * width_count * (tap_count + LANES),
                bytes_accessed=40 * plan.out_tiles * LANES * chan_rows * width_count,
                transcendentals=plan.out_tiles * LANES * chan_rows * (width_count + 1),
            ),
        )(*operands)

    other_core = from_partner(filterbank, "sub", 1)
    own = pl.pallas_call(
        load_kernel,
        out_shape=jax.ShapeDtypeStruct(filterbank.shape, filterbank.dtype),
        in_specs=[in_vmem],
        out_specs=in_vmem,
        compiler_params=params,
    )(filterbank)
    ahead = pl.pallas_call(
        start_kernel,
        out_shape=jax.ShapeDtypeStruct((2 * chan_rows, near_len), filterbank.dtype),
        in_specs=[in_vmem] * 2,
        out_specs=in_vmem,
        compiler_params=params,
    )(own, other_core)
    near_tiles = near_len // LANES
    early = time_tiles - near_tiles
    rows, delays = within_chip(
        [own, other_core, delay_shifts], [(0, time_len, 0)], time_tiles, early, False
    )
    operands, spans = [own, other_core], [(early * LANES, near_len, 0)]
    if lax.axis_size("tm") > 1:
        operands.append(from_ahead(ahead, 1))
        spans.append((0, near_len, 1))
    main = list(within_chip([*operands, rows, delays], spans, 2 * near_tiles, near_tiles, True))
    late_shifts, late_filters, main[0] = lax.optimization_barrier((delay_shifts, pulse_filters, main[0]))
    columns, taps = pl.pallas_call(
        functools.partial(table_kernel, group_count, block_rows),
        out_shape=[
            jax.ShapeDtypeStruct((LANES, LANES), jnp.float32),
            jax.ShapeDtypeStruct((width_count * LANES, tap_count + LANES), jnp.bfloat16),
        ],
        in_specs=[in_vmem] * 2,
        out_specs=[in_vmem] * 2,
        scratch_shapes=[table],
        compiler_params=params,
    )(late_shifts, late_filters)
    first_tiles = min(time_tiles, far_tiles) if lax.axis_size("tm") > 1 else 0
    *arrived, (step, first, last) = exchanged(main, max(first_tiles, time_tiles // 2 + 1))
    columns, taps, last = lax.optimization_barrier((columns, taps, last))
    arrived.append((step, first, last))
    pieces = [(step, first) for step, first, _ in arrived]
    main = [block for _, _, block in arrived]

    halos, takes = [], []
    rest = far_tiles
    if lax.axis_size("tm") > 1:
        heads = [block for _, first, block in arrived if first == 0]
        joined = []
        for some in (heads[:-2], heads[-2:]):
            shape = (first_tiles, len(some) * block_rows, LANES)
            joined.append(
                pl.pallas_call(
                    join_kernel,
                    out_shape=jax.ShapeDtypeStruct(shape, jnp.bfloat16),
                    in_specs=[in_vmem] * len(some),
                    out_specs=in_vmem,
                    scratch_shapes=[pltpu.VMEM(shape, jnp.float32)],
                    compiler_params=params,
                )(*some)
            )
        for hop in range(1, lax.axis_size("tm")):
            if rest > 0:
                takes.append(min(time_tiles, rest))
                halos += [from_ahead(rows_now[: takes[-1]], hop) for rows_now in joined]
                rest -= takes[-1]
    lost = -(-sum(2**level for level in far_levels) // LANES) + tap_tiles
    early_tiles = time_tiles - lost
    if early_tiles <= 0:
        plan = Plan(pieces, time_tiles, takes, rest, 0, time_tiles, False, False, far_levels, tap_tiles)
        return between_chips(plan, main, halos)[0]
    plan = Plan(pieces, time_tiles, [], 0, 0, early_tiles, False, True, far_levels, tap_tiles)
    out, *carried = between_chips(plan, main, [])
    late_tiles = time_tiles - early_tiles
    plan = Plan(pieces, time_tiles, takes, rest, early_tiles, late_tiles, True, False, far_levels, tap_tiles)
    return between_chips(plan, main, halos, [*carried, out])[0]


def solution(mesh):
    in_specs = (P(("beams", "freq", "sub"), "tm"), P(), P())
    out_specs = P(("beams", "freq", "sub"), "tm")
    return jax.shard_map(local, mesh=mesh, in_specs=in_specs, out_specs=out_specs, check_vma=False)
```

```python
import functools
import math

import jax
import jax.numpy as jnp
from jax import lax
from jax.experimental import pallas as pl
from jax.experimental.pallas import tpu as pltpu
from jax.sharding import PartitionSpec as P

LANES = 128
SUBLANES = 8
PACKED = 16
SHORT = 4
LOG2_E = 1.4426950408889634
VMEM_LIMIT = 48 * 2**20


def rounded_up(value, unit):
    return -(-value // unit) * unit


def reversed_bits(value, bit_count):
    result = 0
    for bit_num in range(bit_count):
        result = result | (value >> bit_num & 1) << bit_count - 1 - bit_num
    return result


def bits_of(count):
    return count.bit_length() - 1


def from_ahead(value, steps):
    count = lax.axis_size("tm")
    return lax.ppermute(value, "tm", [((block + steps) % count, block) for block in range(count)])


def from_partner(value, axis, mask):
    count = lax.axis_size(axis)
    return lax.ppermute(value, axis, [(source, source ^ mask) for source in range(count)])


def mask_orders(group_count):
    far = list(range(group_count - 1, 1, -1))
    return [*far[:-1], 1, *far[-1:]], [*far[-1:], *far[:-1], 1]


def step_masks(group_count, core):
    orders = mask_orders(group_count)
    return [0] + [jnp.where(core == 0, first, second) for first, second in zip(*orders)]


def exchanged(blocks, cut):
    count = lax.axis_size("freq")
    received = [(0, 0, blocks[0])]
    for step, masks in enumerate(zip(*mask_orders(count)), 1):
        route = [
            (chip * 2 + core, (chip ^ masks[core]) * 2 + core) for chip in range(count) for core in range(2)
        ]
        tiles = blocks[step].shape[0]
        ends = [0, cut, tiles] if step + 1 == count and 0 < cut < tiles else [0, tiles]
        for first, end in zip(ends, ends[1:]):
            received.append((step, first, lax.ppermute(blocks[step][first:end], ("freq", "sub"), route)))
    return received


def lanes():
    return lax.broadcasted_iota(jnp.int32, (SUBLANES, LANES), 1)


def gathered(value, index):
    return jnp.take_along_axis(value, index, axis=1, mode="promise_in_bounds")


def transposed_table(rows, table, columns):
    for index, row in enumerate(rows):
        table[index : index + 1, :] = row.astype(jnp.float32)
    columns[...] = table[...].T


def merge_short(source, target, low, high, outs, tiles, most):
    inside = [lanes() < LANES - delay for delay in range(1, most + 1)]
    chosen = [([amount == delay for delay in range(1, most + 1)], place) for amount, place in outs]

    def rolled(tile):
        value = source[tile, high, :]
        return value, [pltpu.roll(value, LANES - delay, 1) for delay in range(1, most + 1)]

    now = rolled(0)
    for tile in range(tiles):
        later = rolled(tile + 1)
        copies = [jnp.where(*parts) for parts in zip(inside, now[1], later[1])]
        lower = source[tile, low, :]
        for masks, place in chosen:
            moved = now[0]
            for mask, copy in zip(masks, copies):
                moved = jnp.where(mask, copy, moved)
            target[tile, place, :] = lower + moved
        now = later


def merge(source, target, low, high, outs, tiles, most):
    if most <= SHORT:
        return merge_short(source, target, low, high, outs, tiles, most)
    lane = lanes()
    apart = max(most // LANES, 1)
    chosen = []
    for amount, place in outs:
        part = amount if most < LANES else amount & LANES - 1
        moved = (lane < part).astype(jnp.int32)
        if most >= LANES:
            moved = moved + (amount >> bits_of(LANES))
        masks = [moved == offset for offset in range(1, apart + 1)]
        chosen.append((masks, lane + part & LANES - 1, place))
    for masks, index, place in chosen:
        upper = [source[offset, high, :] for offset in range(apart)]
        for tile in range(tiles):
            upper.append(source[tile + apart, high, :])
            mixed = upper[0]
            for mask, other in zip(masks, upper[1:]):
                mixed = jnp.where(mask, other, mixed)
            target[tile, place, :] = source[tile, low, :] + gathered(mixed, index)
            upper = upper[1:]


def tree_levels(state, other, columns, first, levels, held, lengths, packed=False):
    rows = columns.shape[0] // 2
    source, target = state, other
    done = 0
    while done < len(levels):
        narrow = held < SUBLANES
        bits = min(bits_of(SUBLANES // held), len(levels) - done) if narrow else len(levels) - done
        for turn in range(bits):
            level = levels[done + turn]
            inner = turn + 1 < bits
            natural = turn == 0 and not (packed and done == 0)

            def rows_in(vector, start, stride):
                return pl.ds(start, SUBLANES, stride=stride) if natural else pl.ds(vector * SUBLANES, SUBLANES)

            def rows_out(vector, start, stride):
                return pl.ds(vector * SUBLANES, SUBLANES) if inner else pl.ds(start, SUBLANES, stride=stride)

            def amounts(start, stride):
                column = columns[pl.ds(start, SUBLANES, stride=stride), :]
                one = column[:, first + done + turn : first + done + turn + 1]
                return jnp.broadcast_to(one, (SUBLANES, LANES)).astype(jnp.int32)

            if narrow:
                now = held << turn
                for band in range(SUBLANES // (2 * now)):
                    for trial in range(now):
                        low, high = 2 * band * now + trial, (2 * band + 1) * now + trial
                        outs = [band * 2 * now + 2 * trial + odd for odd in range(2)]
                        merge(
                            source,
                            target,
                            rows_in(low, low, SUBLANES),
                            rows_in(high, high, SUBLANES),
                            [(amounts(out, SUBLANES), rows_out(out, out, SUBLANES)) for out in outs],
                            lengths[done + turn],
                            2**level,
                        )
            else:
                groups, split = held // SUBLANES, 2**turn
                for band in range(rows // (2 * held * split)):
                    for group in range(groups):
                        for place in range(split):
                            low, high = [
                                ((2 * band + upper) * groups + group) * split + place for upper in range(2)
                            ]
                            outs = []
                            for odd in range(2):
                                vector = (band * groups + group) * 2 * split + 2 * place + odd
                                start = (band * groups + group) * SUBLANES * 2 * split + 2 * place + odd
                                outs.append((amounts(start, 2 * split), rows_out(vector, start, 2 * split)))
                            merge(
                                source,
                                target,
                                rows_in(low, low * SUBLANES, 1),
                                rows_in(high, high * SUBLANES, 1),
                                outs,
                                lengths[done + turn],
                                2**level,
                            )
            source, target = target, source
        held <<= bits
        done += bits
    return source


def lengths_of(made, levels):
    return [made + -(-sum(2**later for later in levels if later > level) // LANES) for level in levels]


def load_kernel(whole, copied):
    copied[...] = whole[...]


def start_kernel(whole, other, ahead):
    rows, length = whole.shape[0], ahead.shape[1]
    ahead[:rows, :] = whole[:, :length]
    ahead[rows:, :] = other[:, :length]


def placed(target, blocks, group_count, skip):
    chip, core = lax.axis_index("freq"), lax.axis_index("sub")
    masks = step_masks(group_count, core)
    for step, first, block in blocks:
        tiles, rows = block.shape[:2]
        start = pl.multiple_of((chip ^ masks[step]) * rows, rows)
        for tile in range(max(skip - first, 0), tiles):
            target[first + tile - skip, pl.ds(start, rows), :] = block[tile, :, :].astype(jnp.float32)


def join_kernel(*refs):
    *blocks, out, state = refs
    rows = blocks[0].shape[1]
    for tile in range(out.shape[0]):
        for index, block in enumerate(blocks):
            state[tile, index * rows : (index + 1) * rows, :] = block[tile, :, :].astype(jnp.float32)
        out[tile, :, :] = state[tile, :, :].astype(jnp.bfloat16)


def chip_kernel(spans, out_tiles, group_count, *refs):
    chan_rows = refs[0].shape[0]
    pieces = [[(refs[side], 0)] + [(ref, side * chan_rows) for ref in refs[2 : len(spans) + 1]] for side in range(2)]
    refs = refs[len(spans) + 1 :]
    local_count = bits_of(chan_rows)
    chip, core = lax.axis_index("freq"), lax.axis_index("sub")
    if group_count:
        (earlier, columns), blocks, (raw, ping, pong) = refs[:2], refs[2:-3], refs[-3:]
    else:
        shifts, rows, columns, raw, ping, pong, table = refs
        chunk = shifts[0:SUBLANES, pl.ds(pl.multiple_of(chip * LANES, LANES), LANES)]
        lane, level = lanes(), lax.broadcasted_iota(jnp.int32, (SUBLANES, LANES), 0)
        kept = lane & (1 << level) - 1
        picked = gathered(chunk, (2 * (lane - kept) + (core << level) + kept) & LANES - 1)
        transposed_table([picked[at : at + 1, :] for at in range(local_count + 1)], table, columns)
    for side in range(2):
        place = pl.multiple_of((core ^ side) * chan_rows, chan_rows)
        tile = 0
        for (piece, row), (column, length, ahead) in zip(pieces[side], spans):
            there = lax.axis_index("tm") + ahead < lax.axis_size("tm")
            for start in range(column, column + length, LANES):
                part = piece[row : row + chan_rows, start : start + LANES].astype(jnp.float32)
                if ahead:
                    part = jnp.where(there, part, 0.0)
                raw[tile, pl.ds(place, chan_rows), :] = part
                tile += 1
        for later in range(tile, raw.shape[0] - 1):
            raw[later, pl.ds(place, chan_rows), :] = jnp.zeros((chan_rows, LANES), jnp.float32)
    levels = list(range(local_count + 1))
    lengths = lengths_of(out_tiles, levels)
    mask = lanes() >= core
    for vector in range(SUBLANES):
        low, high = [pl.ds(2 * vector + odd, SUBLANES, stride=2 * SUBLANES) for odd in range(2)]
        upper = raw[0, high, :]
        for tile in range(lengths[0]):
            later = raw[tile + 1, high, :]
            moved = pltpu.roll(jnp.where(mask, upper, later), LANES - core & LANES - 1, 1)
            ping[tile, pl.ds(vector * SUBLANES, SUBLANES), :] = raw[tile, low, :] + moved
            upper = later
    last = tree_levels(ping, pong, columns, 1, levels[1:], 1, lengths[1:], packed=True)
    if not group_count:
        for tile in range(out_tiles):
            rows[tile, :, :] = last[tile, :, :]
        return
    size = chan_rows // group_count
    own = reversed_bits(chip, bits_of(group_count))
    first = earlier.shape[0]
    for mask, block in zip(step_masks(group_count, core), blocks):
        start = pl.multiple_of((own ^ reversed_bits(mask, bits_of(group_count))) * size, size)
        for tile in range(first):
            block[tile, :, :] = earlier[tile, pl.ds(start, size), :].astype(jnp.bfloat16)
        for tile in range(out_tiles):
            block[first + tile, :, :] = last[tile, pl.ds(start, size), :].astype(jnp.bfloat16)


def toeplitz(filters, target):
    width_count, tap_count = filters.shape
    lane = lax.broadcasted_iota(jnp.int32, (LANES, LANES), 1)
    row = lax.broadcasted_iota(jnp.int32, (LANES, LANES), 0)
    taps = filters[...].astype(jnp.float32)
    zeros = jnp.zeros((LANES, LANES), jnp.float32)
    for width in range(width_count):
        before = zeros
        for start in range(0, tap_count + LANES, LANES):
            if start < tap_count:
                spread = jnp.broadcast_to(taps[width : width + 1, start : start + LANES], (LANES, LANES))
                rolled = pltpu.roll(spread, 0, 1, stride=1, stride_axis=0)
            else:
                rolled = zeros
            part = jnp.where(lane >= row, rolled, before)
            target[width * LANES : (width + 1) * LANES, start : start + LANES] = part.astype(jnp.bfloat16)
            before = rolled


def table_kernel(group_count, block_rows, shifts, filters, columns, taps, table):
    level_count = shifts.shape[0]
    chip, core = lax.axis_index("freq"), lax.axis_index("sub")
    own = reversed_bits(chip * 2 + core, bits_of(group_count) + 1)
    lane = lax.broadcasted_iota(jnp.int32, (1, LANES), 1)
    rows = []
    for section in range(bits_of(group_count)):
        level = level_count - bits_of(group_count) + section
        wide = block_rows * 2 ** (section + 1)
        row = jnp.zeros((1, LANES), jnp.int32)
        for subband in range(block_rows * group_count // wide):
            start = subband * 2 ** (level + 1) + own * wide
            tile = pl.multiple_of(start >> bits_of(LANES) << bits_of(LANES), LANES)
            chunk = shifts[level : level + 1, pl.ds(tile, LANES)]
            moved = pltpu.roll(chunk, subband * wide - (start & LANES - 1) & LANES - 1, 1)
            row = jnp.where(lane >= subband * wide, moved, row)
        rows.append(row)
    transposed_table(rows, table, columns)
    toeplitz(filters, taps)


def trial_kernel(plan, group_count, level_count, scale, columns, taps, *refs):
    blocks, refs = refs[: len(plan.pieces)], refs[len(plan.pieces) :]
    halos, refs = refs[: 2 * len(plan.halos)], refs[2 * len(plan.halos) :]
    if plan.taken:
        carried, so_far, refs = refs[0], refs[1], refs[2:]
    out, refs = refs[0], refs[1:]
    if plan.given:
        handed, refs = refs[0], refs[1:]
    state, other, normal, responses, *refs = refs
    if plan.given:
        result = out
    else:
        result, arrived = refs
    chan_rows = result.shape[0]
    block_rows = chan_rows // group_count
    width_count, kept = taps.shape[0] // LANES, taps.shape[1] // LANES - 1
    levels = list(range(level_count - bits_of(group_count), level_count))
    copies = []
    if plan.taken:
        place = out.at[:, pl.ds(0, plan.out_first * LANES)]
        copies.append(pltpu.make_async_copy(so_far, place, arrived.at[len(plan.chunks)]))
        copies[0].start()
    pieces = [(step, first, block) for (step, first), block in zip(plan.pieces, blocks)]
    placed(state, pieces, group_count, plan.first)
    at = plan.main_tiles - plan.first
    chip, core = lax.axis_index("freq"), lax.axis_index("sub")
    for hop, tiles in enumerate(plan.halos, 1):
        there = lax.axis_index("tm") + hop < lax.axis_size("tm")
        for tile in range(tiles):
            joined = [
                jnp.where(there, halo[tile, :, :].astype(jnp.float32), 0.0)
                for halo in halos[2 * hop - 2 : 2 * hop]
            ]
            parts = [
                value[row : row + block_rows] for value in joined for row in range(0, value.shape[0], block_rows)
            ]
            for part, mask in zip(parts, step_masks(group_count, core)):
                start = pl.multiple_of((chip ^ mask) * block_rows, block_rows)
                state[at, pl.ds(start, block_rows), :] = part
            at += 1
    for tile in range(at, at + plan.empty_tiles):
        state[tile, :, :] = jnp.zeros((chan_rows, LANES), jnp.float32)
    last = tree_levels(state, other, columns, 0, levels, block_rows, plan.lengths)
    head = kept if plan.taken else 0
    for tile in range(head):
        normal[tile, :, :] = carried[tile, :, :]
    for tile in range(plan.made):
        normal[head + tile, :, :] = (last[tile, :, :] * scale).astype(jnp.bfloat16)
    count = plan.out_tiles
    if plan.given:
        for tile in range(kept):
            handed[tile, :, :] = normal[count + tile, :, :]
    for turn, (first_tile, some) in enumerate(plan.chunks):
        size = some * chan_rows
        windows = [
            normal[first_tile + offset : first_tile + offset + some, :, :].reshape(size, LANES)
            for offset in range(kept + 1)
        ]
        responses[0:size, :] = lax.dot_general(
            jnp.concatenate(windows, axis=1),
            taps[...],
            (((1,), (1,)), ((), ())),
            preferred_element_type=jnp.float32,
        )
        for first_row in range(0, size, PACKED):
            energies = []
            for width in range(width_count):
                one = responses[first_row : first_row + PACKED, width * LANES : (width + 1) * LANES]
                energies.append((0.5 * LOG2_E) * one * one)
            highest = functools.reduce(jnp.maximum, energies)
            total = functools.reduce(jnp.add, [jnp.exp2(energy - highest) for energy in energies])
            tile, row = first_tile + first_row // chan_rows, first_row % chan_rows
            result[row : row + PACKED, tile * LANES : (tile + 1) * LANES] = (
                jnp.log2(total) + highest
            ) * (1.0 / LOG2_E)
        if plan.given:
            continue
        columns_now = pl.ds(first_tile * LANES, some * LANES)
        place = out.at[:, pl.ds((plan.out_first + first_tile) * LANES, some * LANES)]
        copies.append(pltpu.make_async_copy(result.at[:, columns_now], place, arrived.at[turn]))
        copies[-1].start()
    for copy in copies:
        copy.wait()


class Plan:
    def __init__(self, pieces, main_tiles, halos, empty_tiles, out_first, out_tiles, taken, given, levels, tap_tiles):
        self.pieces = pieces
        self.main_tiles, self.halos, self.empty_tiles = main_tiles, halos, empty_tiles
        self.out_first, self.out_tiles = out_first, out_tiles
        self.taken, self.given = taken, given
        self.made = out_tiles if taken else out_tiles + tap_tiles
        self.first = out_first + tap_tiles if taken else 0
        self.lengths = lengths_of(self.made, levels)
        turns = -(-out_tiles // 6)
        ends = [out_tiles * turn // turns for turn in range(turns + 1)]
        self.chunks = [(start, end - start) for start, end in zip(ends, ends[1:])]
        self.state_tiles = main_tiles + sum(halos) + empty_tiles - self.first + max(2 ** levels[-1] // LANES, 1) + 1


def local(filterbank, delay_shifts, pulse_filters):
    chan_rows, time_len = filterbank.shape
    group_count = lax.axis_size("freq")
    assert lax.axis_size("sub") == 2 and 2 * chan_rows == LANES
    level_count = delay_shifts.shape[0]
    width_count, tap_count = pulse_filters.shape
    tap_tiles = tap_count // LANES
    time_tiles = time_len // LANES
    far_levels = range(level_count - bits_of(group_count), level_count)
    near_reach = 2 ** far_levels[0] - 1
    near_len = rounded_up(near_reach, LANES)
    far_tiles = -(-(2**level_count - 1 - near_reach + tap_count) // LANES)

    in_vmem = pl.BlockSpec(memory_space=pltpu.VMEM)
    in_any = pl.BlockSpec(memory_space=pl.ANY)
    params = pltpu.CompilerParams(vmem_limit_bytes=VMEM_LIMIT)
    block_rows = chan_rows // group_count
    table = pltpu.VMEM((LANES, LANES), jnp.float32)

    def within_chip(operands, spans, raw_tiles, out_tiles, sending):
        state = pltpu.VMEM((raw_tiles + 1, chan_rows, LANES), jnp.float32)
        if sending:
            block = jax.ShapeDtypeStruct((time_tiles, block_rows, LANES), jnp.bfloat16)
            out_shape = [block] * group_count
        else:
            out_shape = [
                jax.ShapeDtypeStruct((out_tiles, chan_rows, LANES), jnp.float32),
                jax.ShapeDtypeStruct((LANES, LANES), jnp.float32),
            ]
        return pl.pallas_call(
            functools.partial(chip_kernel, spans, out_tiles, group_count if sending else 0),
            out_shape=out_shape,
            in_specs=[in_vmem] * len(operands),
            out_specs=[in_vmem] * len(out_shape),
            scratch_shapes=[pltpu.VMEM((raw_tiles + 1, 2 * chan_rows, LANES), jnp.float32), state, state]
            + ([] if sending else [table]),
            compiler_params=params,
        )(*operands)

    def between_chips(plan, blocks, halos, carried=()):
        state = pltpu.VMEM((plan.state_tiles, chan_rows, LANES), jnp.float32)
        operands = [columns, taps, *blocks, *halos, *carried]
        result = (chan_rows, plan.out_tiles * LANES)
        if plan.given:
            out_shape = [
                jax.ShapeDtypeStruct(result, jnp.float32),
                jax.ShapeDtypeStruct((tap_tiles, chan_rows, LANES), jnp.bfloat16),
            ]
            out_specs, scratch = [in_vmem] * 2, []
        else:
            out_shape, out_specs = [jax.ShapeDtypeStruct((chan_rows, time_len), jnp.float32)], [in_any]
            scratch = [pltpu.VMEM(result, jnp.float32), pltpu.SemaphoreType.DMA((len(plan.chunks) + 1,))]
        most = max(some for _, some in plan.chunks)
        scale = 1.0 / math.sqrt(delay_shifts.shape[1])
        return pl.pallas_call(
            functools.partial(trial_kernel, plan, group_count, level_count, scale),
            out_shape=out_shape,
            in_specs=[in_vmem] * len(operands),
            out_specs=out_specs,
            scratch_shapes=[
                state,
                state,
                pltpu.VMEM((plan.out_tiles + tap_tiles, chan_rows, LANES), jnp.bfloat16),
                pltpu.VMEM((most * chan_rows, width_count * LANES), jnp.float32),
            ]
            + scratch,
            compiler_params=params,
            cost_estimate=pl.CostEstimate(
                flops=2 * plan.out_tiles * LANES * chan_rows * width_count * (tap_count + LANES),
                bytes_accessed=40 * plan.out_tiles * LANES * chan_rows * width_count,
                transcendentals=plan.out_tiles * LANES * chan_rows * (width_count + 1),
            ),
        )(*operands)

    other_core = from_partner(filterbank, "sub", 1)
    own = pl.pallas_call(
        load_kernel,
        out_shape=jax.ShapeDtypeStruct(filterbank.shape, filterbank.dtype),
        in_specs=[in_vmem],
        out_specs=in_vmem,
        compiler_params=params,
    )(filterbank)
    ahead = pl.pallas_call(
        start_kernel,
        out_shape=jax.ShapeDtypeStruct((2 * chan_rows, near_len), filterbank.dtype),
        in_specs=[in_vmem] * 2,
        out_specs=in_vmem,
        compiler_params=params,
    )(own, other_core)
    near_tiles = near_len // LANES
    early = time_tiles - near_tiles
    rows, delays = within_chip(
        [own, other_core, delay_shifts], [(0, time_len, 0)], time_tiles, early, False
    )
    operands, spans = [own, other_core], [(early * LANES, near_len, 0)]
    if lax.axis_size("tm") > 1:
        operands.append(from_ahead(ahead, 1))
        spans.append((0, near_len, 1))
    main = list(within_chip([*operands, rows, delays], spans, 2 * near_tiles, near_tiles, True))
    late_shifts, late_filters, main[0] = lax.optimization_barrier((delay_shifts, pulse_filters, main[0]))
    columns, taps = pl.pallas_call(
        functools.partial(table_kernel, group_count, block_rows),
        out_shape=[
            jax.ShapeDtypeStruct((LANES, LANES), jnp.float32),
            jax.ShapeDtypeStruct((width_count * LANES, tap_count + LANES), jnp.bfloat16),
        ],
        in_specs=[in_vmem] * 2,
        out_specs=[in_vmem] * 2,
        scratch_shapes=[table],
        compiler_params=params,
    )(late_shifts, late_filters)
    first_tiles = min(time_tiles, far_tiles) if lax.axis_size("tm") > 1 else 0
    arrived = exchanged(main, max(first_tiles, time_tiles // 2 + 1))
    step, first, block = arrived[2]
    columns, taps, block = lax.optimization_barrier((columns, taps, block))
    arrived[2] = (step, first, block)
    pieces = [(step, first) for step, first, _ in arrived]
    main = [block for _, _, block in arrived]

    halos, takes = [], []
    rest = far_tiles
    if lax.axis_size("tm") > 1:
        heads = [block for _, first, block in arrived if first == 0]
        joined = []
        for some in (heads[:-2], heads[-2:]):
            shape = (first_tiles, len(some) * block_rows, LANES)
            joined.append(
                pl.pallas_call(
                    join_kernel,
                    out_shape=jax.ShapeDtypeStruct(shape, jnp.bfloat16),
                    in_specs=[in_vmem] * len(some),
                    out_specs=in_vmem,
                    scratch_shapes=[pltpu.VMEM(shape, jnp.float32)],
                    compiler_params=params,
                )(*some)
            )
        for hop in range(1, lax.axis_size("tm")):
            if rest > 0:
                takes.append(min(time_tiles, rest))
                halos += [from_ahead(rows_now[: takes[-1]], hop) for rows_now in joined]
                rest -= takes[-1]
    lost = -(-sum(2**level for level in far_levels) // LANES) + tap_tiles
    early_tiles = time_tiles - lost
    if early_tiles <= 0:
        plan = Plan(pieces, time_tiles, takes, rest, 0, time_tiles, False, False, far_levels, tap_tiles)
        return between_chips(plan, main, halos)[0]
    plan = Plan(pieces, time_tiles, [], 0, 0, early_tiles, False, True, far_levels, tap_tiles)
    out, *carried = between_chips(plan, main, [])
    late_tiles = time_tiles - early_tiles
    plan = Plan(pieces, time_tiles, takes, rest, early_tiles, late_tiles, True, False, far_levels, tap_tiles)
    return between_chips(plan, main, halos, [*carried, out])[0]


def solution(mesh):
    in_specs = (P(("beams", "freq", "sub"), "tm"), P(), P())
    out_specs = P(("beams", "freq", "sub"), "tm")
    return jax.shard_map(local, mesh=mesh, in_specs=in_specs, out_specs=out_specs, check_vma=False)
```

```python
import functools
import math

import jax
import jax.numpy as jnp
from jax import lax
from jax.experimental import pallas as pl
from jax.experimental.pallas import tpu as pltpu
from jax.sharding import PartitionSpec as P

LANES = 128
SUBLANES = 8
PACKED = 16
SHORT = 4
LOG2_E = 1.4426950408889634
VMEM_LIMIT = 48 * 2**20


def rounded_up(value, unit):
    return -(-value // unit) * unit


def reversed_bits(value, bit_count):
    result = 0
    for bit_num in range(bit_count):
        result = result | (value >> bit_num & 1) << bit_count - 1 - bit_num
    return result


def bits_of(count):
    return count.bit_length() - 1


def from_ahead(value, steps):
    count = lax.axis_size("tm")
    return lax.ppermute(value, "tm", [((block + steps) % count, block) for block in range(count)])


def from_partner(value, axis, mask):
    count = lax.axis_size(axis)
    return lax.ppermute(value, axis, [(source, source ^ mask) for source in range(count)])


def mask_orders(group_count):
    far = list(range(group_count - 1, 1, -1))
    return [1, *far], [*far[-1:], *far[:-1], 1]


def step_masks(group_count, core):
    orders = mask_orders(group_count)
    return [0] + [jnp.where(core == 0, first, second) for first, second in zip(*orders)]


def exchanged(blocks, cut):
    count = lax.axis_size("freq")
    received = [(0, 0, blocks[0])]
    for step, masks in enumerate(zip(*mask_orders(count)), 1):
        route = [
            (chip * 2 + core, (chip ^ masks[core]) * 2 + core) for chip in range(count) for core in range(2)
        ]
        tiles = blocks[step].shape[0]
        ends = [0, cut, tiles] if step + 1 == count and 0 < cut < tiles else [0, tiles]
        for first, end in zip(ends, ends[1:]):
            received.append((step, first, lax.ppermute(blocks[step][first:end], ("freq", "sub"), route)))
    return received


def lanes():
    return lax.broadcasted_iota(jnp.int32, (SUBLANES, LANES), 1)


def gathered(value, index):
    return jnp.take_along_axis(value, index, axis=1, mode="promise_in_bounds")


def transposed_table(rows, table, columns):
    for index, row in enumerate(rows):
        table[index : index + 1, :] = row.astype(jnp.float32)
    columns[...] = table[...].T


def merge_short(source, target, low, high, outs, tiles, most):
    inside = [lanes() < LANES - delay for delay in range(1, most + 1)]
    chosen = [([amount == delay for delay in range(1, most + 1)], place) for amount, place in outs]

    def rolled(tile):
        value = source[tile, high, :]
        return value, [pltpu.roll(value, LANES - delay, 1) for delay in range(1, most + 1)]

    now = rolled(0)
    for tile in range(tiles):
        later = rolled(tile + 1)
        copies = [jnp.where(*parts) for parts in zip(inside, now[1], later[1])]
        lower = source[tile, low, :]
        for masks, place in chosen:
            moved = now[0]
            for mask, copy in zip(masks, copies):
                moved = jnp.where(mask, copy, moved)
            target[tile, place, :] = lower + moved
        now = later


def merge(source, target, low, high, outs, tiles, most):
    if most <= SHORT:
        return merge_short(source, target, low, high, outs, tiles, most)
    lane = lanes()
    apart = max(most // LANES, 1)
    chosen = []
    for amount, place in outs:
        part = amount if most < LANES else amount & LANES - 1
        moved = (lane < part).astype(jnp.int32)
        if most >= LANES:
            moved = moved + (amount >> bits_of(LANES))
        masks = [moved == offset for offset in range(1, apart + 1)]
        chosen.append((masks, lane + part & LANES - 1, place))
    for masks, index, place in chosen:
        upper = [source[offset, high, :] for offset in range(apart)]
        for tile in range(tiles):
            upper.append(source[tile + apart, high, :])
            mixed = upper[0]
            for mask, other in zip(masks, upper[1:]):
                mixed = jnp.where(mask, other, mixed)
            target[tile, place, :] = source[tile, low, :] + gathered(mixed, index)
            upper = upper[1:]


def tree_levels(state, other, columns, first, levels, held, lengths, packed=False):
    rows = columns.shape[0] // 2
    source, target = state, other
    done = 0
    while done < len(levels):
        narrow = held < SUBLANES
        bits = min(bits_of(SUBLANES // held), len(levels) - done) if narrow else len(levels) - done
        for turn in range(bits):
            level = levels[done + turn]
            inner = turn + 1 < bits
            natural = turn == 0 and not (packed and done == 0)

            def rows_in(vector, start, stride):
                return pl.ds(start, SUBLANES, stride=stride) if natural else pl.ds(vector * SUBLANES, SUBLANES)

            def rows_out(vector, start, stride):
                return pl.ds(vector * SUBLANES, SUBLANES) if inner else pl.ds(start, SUBLANES, stride=stride)

            def amounts(start, stride):
                column = columns[pl.ds(start, SUBLANES, stride=stride), :]
                one = column[:, first + done + turn : first + done + turn + 1]
                return jnp.broadcast_to(one, (SUBLANES, LANES)).astype(jnp.int32)

            if narrow:
                now = held << turn
                for band in range(SUBLANES // (2 * now)):
                    for trial in range(now):
                        low, high = 2 * band * now + trial, (2 * band + 1) * now + trial
                        outs = [band * 2 * now + 2 * trial + odd for odd in range(2)]
                        merge(
                            source,
                            target,
                            rows_in(low, low, SUBLANES),
                            rows_in(high, high, SUBLANES),
                            [(amounts(out, SUBLANES), rows_out(out, out, SUBLANES)) for out in outs],
                            lengths[done + turn],
                            2**level,
                        )
            else:
                groups, split = held // SUBLANES, 2**turn
                for band in range(rows // (2 * held * split)):
                    for group in range(groups):
                        for place in range(split):
                            low, high = [
                                ((2 * band + upper) * groups + group) * split + place for upper in range(2)
                            ]
                            outs = []
                            for odd in range(2):
                                vector = (band * groups + group) * 2 * split + 2 * place + odd
                                start = (band * groups + group) * SUBLANES * 2 * split + 2 * place + odd
                                outs.append((amounts(start, 2 * split), rows_out(vector, start, 2 * split)))
                            merge(
                                source,
                                target,
                                rows_in(low, low * SUBLANES, 1),
                                rows_in(high, high * SUBLANES, 1),
                                outs,
                                lengths[done + turn],
                                2**level,
                            )
            source, target = target, source
        held <<= bits
        done += bits
    return source


def lengths_of(made, levels):
    return [made + -(-sum(2**later for later in levels if later > level) // LANES) for level in levels]


def load_kernel(whole, copied):
    copied[...] = whole[...]


def start_kernel(whole, other, ahead):
    rows, length = whole.shape[0], ahead.shape[1]
    ahead[:rows, :] = whole[:, :length]
    ahead[rows:, :] = other[:, :length]


def placed(target, blocks, group_count, skip):
    chip, core = lax.axis_index("freq"), lax.axis_index("sub")
    masks = step_masks(group_count, core)
    for step, first, block in blocks:
        tiles, rows = block.shape[:2]
        start = pl.multiple_of((chip ^ masks[step]) * rows, rows)
        for tile in range(max(skip - first, 0), tiles):
            target[first + tile - skip, pl.ds(start, rows), :] = block[tile, :, :].astype(jnp.float32)


def join_kernel(*refs):
    *blocks, out, state = refs
    rows = blocks[0].shape[1]
    for tile in range(out.shape[0]):
        for index, block in enumerate(blocks):
            state[tile, index * rows : (index + 1) * rows, :] = block[tile, :, :].astype(jnp.float32)
        out[tile, :, :] = state[tile, :, :].astype(jnp.bfloat16)


def chip_kernel(spans, out_tiles, group_count, *refs):
    chan_rows = refs[0].shape[0]
    pieces = [[(refs[side], 0)] + [(ref, side * chan_rows) for ref in refs[2 : len(spans) + 1]] for side in range(2)]
    refs = refs[len(spans) + 1 :]
    local_count = bits_of(chan_rows)
    chip, core = lax.axis_index("freq"), lax.axis_index("sub")
    if group_count:
        (earlier, columns), blocks, (raw, ping, pong) = refs[:2], refs[2:-3], refs[-3:]
    else:
        shifts, rows, columns, raw, ping, pong, table = refs
        chunk = shifts[0:SUBLANES, pl.ds(pl.multiple_of(chip * LANES, LANES), LANES)]
        lane, level = lanes(), lax.broadcasted_iota(jnp.int32, (SUBLANES, LANES), 0)
        kept = lane & (1 << level) - 1
        picked = gathered(chunk, (2 * (lane - kept) + (core << level) + kept) & LANES - 1)
        transposed_table([picked[at : at + 1, :] for at in range(local_count + 1)], table, columns)
    for side in range(2):
        place = pl.multiple_of((core ^ side) * chan_rows, chan_rows)
        tile = 0
        for (piece, row), (column, length, ahead) in zip(pieces[side], spans):
            there = lax.axis_index("tm") + ahead < lax.axis_size("tm")
            for start in range(column, column + length, LANES):
                part = piece[row : row + chan_rows, start : start + LANES].astype(jnp.float32)
                if ahead:
                    part = jnp.where(there, part, 0.0)
                raw[tile, pl.ds(place, chan_rows), :] = part
                tile += 1
        for later in range(tile, raw.shape[0] - 1):
            raw[later, pl.ds(place, chan_rows), :] = jnp.zeros((chan_rows, LANES), jnp.float32)
    levels = list(range(local_count + 1))
    lengths = lengths_of(out_tiles, levels)
    mask = lanes() >= core
    for vector in range(SUBLANES):
        low, high = [pl.ds(2 * vector + odd, SUBLANES, stride=2 * SUBLANES) for odd in range(2)]
        upper = raw[0, high, :]
        for tile in range(lengths[0]):
            later = raw[tile + 1, high, :]
            moved = pltpu.roll(jnp.where(mask, upper, later), LANES - core & LANES - 1, 1)
            ping[tile, pl.ds(vector * SUBLANES, SUBLANES), :] = raw[tile, low, :] + moved
            upper = later
    last = tree_levels(ping, pong, columns, 1, levels[1:], 1, lengths[1:], packed=True)
    if not group_count:
        for tile in range(out_tiles):
            rows[tile, :, :] = last[tile, :, :]
        return
    size = chan_rows // group_count
    own = reversed_bits(chip, bits_of(group_count))
    first = earlier.shape[0]
    for mask, block in zip(step_masks(group_count, core), blocks):
        start = pl.multiple_of((own ^ reversed_bits(mask, bits_of(group_count))) * size, size)
        for tile in range(first):
            block[tile, :, :] = earlier[tile, pl.ds(start, size), :].astype(jnp.bfloat16)
        for tile in range(out_tiles):
            block[first + tile, :, :] = last[tile, pl.ds(start, size), :].astype(jnp.bfloat16)


def toeplitz(filters, target):
    width_count, tap_count = filters.shape
    lane = lax.broadcasted_iota(jnp.int32, (LANES, LANES), 1)
    row = lax.broadcasted_iota(jnp.int32, (LANES, LANES), 0)
    taps = filters[...].astype(jnp.float32)
    zeros = jnp.zeros((LANES, LANES), jnp.float32)
    for width in range(width_count):
        before = zeros
        for start in range(0, tap_count + LANES, LANES):
            if start < tap_count:
                spread = jnp.broadcast_to(taps[width : width + 1, start : start + LANES], (LANES, LANES))
                rolled = pltpu.roll(spread, 0, 1, stride=1, stride_axis=0)
            else:
                rolled = zeros
            part = jnp.where(lane >= row, rolled, before)
            target[width * LANES : (width + 1) * LANES, start : start + LANES] = part.astype(jnp.bfloat16)
            before = rolled


def table_kernel(group_count, block_rows, shifts, filters, columns, taps, table):
    level_count = shifts.shape[0]
    chip, core = lax.axis_index("freq"), lax.axis_index("sub")
    own = reversed_bits(chip * 2 + core, bits_of(group_count) + 1)
    lane = lax.broadcasted_iota(jnp.int32, (1, LANES), 1)
    rows = []
    for section in range(bits_of(group_count)):
        level = level_count - bits_of(group_count) + section
        wide = block_rows * 2 ** (section + 1)
        row = jnp.zeros((1, LANES), jnp.int32)
        for subband in range(block_rows * group_count // wide):
            start = subband * 2 ** (level + 1) + own * wide
            tile = pl.multiple_of(start >> bits_of(LANES) << bits_of(LANES), LANES)
            chunk = shifts[level : level + 1, pl.ds(tile, LANES)]
            moved = pltpu.roll(chunk, subband * wide - (start & LANES - 1) & LANES - 1, 1)
            row = jnp.where(lane >= subband * wide, moved, row)
        rows.append(row)
    transposed_table(rows, table, columns)
    toeplitz(filters, taps)


def trial_kernel(plan, group_count, level_count, scale, columns, taps, *refs):
    blocks, refs = refs[: len(plan.pieces)], refs[len(plan.pieces) :]
    halos, refs = refs[: 2 * len(plan.halos)], refs[2 * len(plan.halos) :]
    if plan.taken:
        carried, so_far, refs = refs[0], refs[1], refs[2:]
    out, refs = refs[0], refs[1:]
    if plan.given:
        handed, refs = refs[0], refs[1:]
    state, other, normal, responses, *refs = refs
    if plan.given:
        result = out
    else:
        result, arrived = refs
    chan_rows = result.shape[0]
    block_rows = chan_rows // group_count
    width_count, kept = taps.shape[0] // LANES, taps.shape[1] // LANES - 1
    levels = list(range(level_count - bits_of(group_count), level_count))
    copies = []
    if plan.taken:
        place = out.at[:, pl.ds(0, plan.out_first * LANES)]
        copies.append(pltpu.make_async_copy(so_far, place, arrived.at[len(plan.chunks)]))
        copies[0].start()
    pieces = [(step, first, block) for (step, first), block in zip(plan.pieces, blocks)]
    placed(state, pieces, group_count, plan.first)
    at = plan.main_tiles - plan.first
    chip, core = lax.axis_index("freq"), lax.axis_index("sub")
    for hop, tiles in enumerate(plan.halos, 1):
        there = lax.axis_index("tm") + hop < lax.axis_size("tm")
        for tile in range(tiles):
            joined = [
                jnp.where(there, halo[tile, :, :].astype(jnp.float32), 0.0)
                for halo in halos[2 * hop - 2 : 2 * hop]
            ]
            parts = [
                value[row : row + block_rows] for value in joined for row in range(0, value.shape[0], block_rows)
            ]
            for part, mask in zip(parts, step_masks(group_count, core)):
                start = pl.multiple_of((chip ^ mask) * block_rows, block_rows)
                state[at, pl.ds(start, block_rows), :] = part
            at += 1
    for tile in range(at, at + plan.empty_tiles):
        state[tile, :, :] = jnp.zeros((chan_rows, LANES), jnp.float32)
    last = tree_levels(state, other, columns, 0, levels, block_rows, plan.lengths)
    head = kept if plan.taken else 0
    for tile in range(head):
        normal[tile, :, :] = carried[tile, :, :]
    for tile in range(plan.made):
        normal[head + tile, :, :] = (last[tile, :, :] * scale).astype(jnp.bfloat16)
    count = plan.out_tiles
    if plan.given:
        for tile in range(kept):
            handed[tile, :, :] = normal[count + tile, :, :]
    for turn, (first_tile, some) in enumerate(plan.chunks):
        size = some * chan_rows
        windows = [
            normal[first_tile + offset : first_tile + offset + some, :, :].reshape(size, LANES)
            for offset in range(kept + 1)
        ]
        responses[0:size, :] = lax.dot_general(
            jnp.concatenate(windows, axis=1),
            taps[...],
            (((1,), (1,)), ((), ())),
            preferred_element_type=jnp.float32,
        )
        for first_row in range(0, size, PACKED):
            energies = []
            for width in range(width_count):
                one = responses[first_row : first_row + PACKED, width * LANES : (width + 1) * LANES]
                energies.append((0.5 * LOG2_E) * one * one)
            highest = functools.reduce(jnp.maximum, energies)
            total = functools.reduce(jnp.add, [jnp.exp2(energy - highest) for energy in energies])
            tile, row = first_tile + first_row // chan_rows, first_row % chan_rows
            result[row : row + PACKED, tile * LANES : (tile + 1) * LANES] = (
                jnp.log2(total) + highest
            ) * (1.0 / LOG2_E)
        if plan.given:
            continue
        columns_now = pl.ds(first_tile * LANES, some * LANES)
        place = out.at[:, pl.ds((plan.out_first + first_tile) * LANES, some * LANES)]
        copies.append(pltpu.make_async_copy(result.at[:, columns_now], place, arrived.at[turn]))
        copies[-1].start()
    for copy in copies:
        copy.wait()


class Plan:
    def __init__(self, pieces, main_tiles, halos, empty_tiles, out_first, out_tiles, taken, given, levels, tap_tiles):
        self.pieces = pieces
        self.main_tiles, self.halos, self.empty_tiles = main_tiles, halos, empty_tiles
        self.out_first, self.out_tiles = out_first, out_tiles
        self.taken, self.given = taken, given
        self.made = out_tiles if taken else out_tiles + tap_tiles
        self.first = out_first + tap_tiles if taken else 0
        self.lengths = lengths_of(self.made, levels)
        turns = -(-out_tiles // 6)
        ends = [out_tiles * turn // turns for turn in range(turns + 1)]
        self.chunks = [(start, end - start) for start, end in zip(ends, ends[1:])]
        self.state_tiles = main_tiles + sum(halos) + empty_tiles - self.first + max(2 ** levels[-1] // LANES, 1) + 1


def local(filterbank, delay_shifts, pulse_filters):
    chan_rows, time_len = filterbank.shape
    group_count = lax.axis_size("freq")
    assert lax.axis_size("sub") == 2 and 2 * chan_rows == LANES
    level_count = delay_shifts.shape[0]
    width_count, tap_count = pulse_filters.shape
    tap_tiles = tap_count // LANES
    time_tiles = time_len // LANES
    far_levels = range(level_count - bits_of(group_count), level_count)
    near_reach = 2 ** far_levels[0] - 1
    near_len = rounded_up(near_reach, LANES)
    far_tiles = -(-(2**level_count - 1 - near_reach + tap_count) // LANES)

    in_vmem = pl.BlockSpec(memory_space=pltpu.VMEM)
    in_any = pl.BlockSpec(memory_space=pl.ANY)
    params = pltpu.CompilerParams(vmem_limit_bytes=VMEM_LIMIT)
    block_rows = chan_rows // group_count
    table = pltpu.VMEM((LANES, LANES), jnp.float32)

    def within_chip(operands, spans, raw_tiles, out_tiles, sending):
        state = pltpu.VMEM((raw_tiles + 1, chan_rows, LANES), jnp.float32)
        if sending:
            block = jax.ShapeDtypeStruct((time_tiles, block_rows, LANES), jnp.bfloat16)
            out_shape = [block] * group_count
        else:
            out_shape = [
                jax.ShapeDtypeStruct((out_tiles, chan_rows, LANES), jnp.float32),
                jax.ShapeDtypeStruct((LANES, LANES), jnp.float32),
            ]
        return pl.pallas_call(
            functools.partial(chip_kernel, spans, out_tiles, group_count if sending else 0),
            out_shape=out_shape,
            in_specs=[in_vmem] * len(operands),
            out_specs=[in_vmem] * len(out_shape),
            scratch_shapes=[pltpu.VMEM((raw_tiles + 1, 2 * chan_rows, LANES), jnp.float32), state, state]
            + ([] if sending else [table]),
            compiler_params=params,
        )(*operands)

    def between_chips(plan, blocks, halos, carried=()):
        state = pltpu.VMEM((plan.state_tiles, chan_rows, LANES), jnp.float32)
        operands = [columns, taps, *blocks, *halos, *carried]
        result = (chan_rows, plan.out_tiles * LANES)
        if plan.given:
            out_shape = [
                jax.ShapeDtypeStruct(result, jnp.float32),
                jax.ShapeDtypeStruct((tap_tiles, chan_rows, LANES), jnp.bfloat16),
            ]
            out_specs, scratch = [in_vmem] * 2, []
        else:
            out_shape, out_specs = [jax.ShapeDtypeStruct((chan_rows, time_len), jnp.float32)], [in_any]
            scratch = [pltpu.VMEM(result, jnp.float32), pltpu.SemaphoreType.DMA((len(plan.chunks) + 1,))]
        most = max(some for _, some in plan.chunks)
        scale = 1.0 / math.sqrt(delay_shifts.shape[1])
        return pl.pallas_call(
            functools.partial(trial_kernel, plan, group_count, level_count, scale),
            out_shape=out_shape,
            in_specs=[in_vmem] * len(operands),
            out_specs=out_specs,
            scratch_shapes=[
                state,
                state,
                pltpu.VMEM((plan.out_tiles + tap_tiles, chan_rows, LANES), jnp.bfloat16),
                pltpu.VMEM((most * chan_rows, width_count * LANES), jnp.float32),
            ]
            + scratch,
            compiler_params=params,
            cost_estimate=pl.CostEstimate(
                flops=2 * plan.out_tiles * LANES * chan_rows * width_count * (tap_count + LANES),
                bytes_accessed=40 * plan.out_tiles * LANES * chan_rows * width_count,
                transcendentals=plan.out_tiles * LANES * chan_rows * (width_count + 1),
            ),
        )(*operands)

    other_core = from_partner(filterbank, "sub", 1)
    own = pl.pallas_call(
        load_kernel,
        out_shape=jax.ShapeDtypeStruct(filterbank.shape, filterbank.dtype),
        in_specs=[in_vmem],
        out_specs=in_vmem,
        compiler_params=params,
    )(filterbank)
    ahead = pl.pallas_call(
        start_kernel,
        out_shape=jax.ShapeDtypeStruct((2 * chan_rows, near_len), filterbank.dtype),
        in_specs=[in_vmem] * 2,
        out_specs=in_vmem,
        compiler_params=params,
    )(own, other_core)
    near_tiles = near_len // LANES
    early = time_tiles - near_tiles
    rows, delays = within_chip(
        [own, other_core, delay_shifts], [(0, time_len, 0)], time_tiles, early, False
    )
    operands, spans = [own, other_core], [(early * LANES, near_len, 0)]
    if lax.axis_size("tm") > 1:
        operands.append(from_ahead(ahead, 1))
        spans.append((0, near_len, 1))
    main = list(within_chip([*operands, rows, delays], spans, 2 * near_tiles, near_tiles, True))
    late_shifts, late_filters, main[0] = lax.optimization_barrier((delay_shifts, pulse_filters, main[0]))
    columns, taps = pl.pallas_call(
        functools.partial(table_kernel, group_count, block_rows),
        out_shape=[
            jax.ShapeDtypeStruct((LANES, LANES), jnp.float32),
            jax.ShapeDtypeStruct((width_count * LANES, tap_count + LANES), jnp.bfloat16),
        ],
        in_specs=[in_vmem] * 2,
        out_specs=[in_vmem] * 2,
        scratch_shapes=[table],
        compiler_params=params,
    )(late_shifts, late_filters)
    first_tiles = min(time_tiles, far_tiles) if lax.axis_size("tm") > 1 else 0
    *arrived, (step, first, last) = exchanged(main, max(first_tiles, time_tiles // 2 + 1))
    columns, taps, last = lax.optimization_barrier((columns, taps, last))
    arrived.append((step, first, last))
    pieces = [(step, first) for step, first, _ in arrived]
    main = [block for _, _, block in arrived]

    halos, takes = [], []
    rest = far_tiles
    if lax.axis_size("tm") > 1:
        heads = [block for _, first, block in arrived if first == 0]
        joined = []
        for some in (heads[:-2], heads[-2:]):
            shape = (first_tiles, len(some) * block_rows, LANES)
            joined.append(
                pl.pallas_call(
                    join_kernel,
                    out_shape=jax.ShapeDtypeStruct(shape, jnp.bfloat16),
                    in_specs=[in_vmem] * len(some),
                    out_specs=in_vmem,
                    scratch_shapes=[pltpu.VMEM(shape, jnp.float32)],
                    compiler_params=params,
                )(*some)
            )
        for hop in range(1, lax.axis_size("tm")):
            if rest > 0:
                takes.append(min(time_tiles, rest))
                halos += [from_ahead(rows_now[: takes[-1]], hop) for rows_now in joined]
                rest -= takes[-1]
    lost = -(-sum(2**level for level in far_levels) // LANES) + tap_tiles
    early_tiles = time_tiles - lost
    if early_tiles <= 0:
        plan = Plan(pieces, time_tiles, takes, rest, 0, time_tiles, False, False, far_levels, tap_tiles)
        return between_chips(plan, main, halos)[0]
    plan = Plan(pieces, time_tiles, [], 0, 0, early_tiles, False, True, far_levels, tap_tiles)
    out, *carried = between_chips(plan, main, [])
    late_tiles = time_tiles - early_tiles
    plan = Plan(pieces, time_tiles, takes, rest, early_tiles, late_tiles, True, False, far_levels, tap_tiles)
    return between_chips(plan, main, halos, [*carried, out])[0]


def solution(mesh):
    in_specs = (P(("beams", "freq", "sub"), "tm"), P(), P())
    out_specs = P(("beams", "freq", "sub"), "tm")
    return jax.shard_map(local, mesh=mesh, in_specs=in_specs, out_specs=out_specs, check_vma=False)
```
